512 devices in a mesh: lat: 8 (over z_lo, x), lon: 64 (over z_hi, y, core).
Axes of the slice: x: 4, y: 8, z: 8 (z_hi: 4, z_lo: 2; z = z_hi * 2 + z_lo), core: 2. Of those that a mesh axis runs over, the one named last changes fastest.
Arguments:
- innovations: float32 [8, 64, 16, 512], P('lat', 'lon'), may hold values from -6 to 6
- obs_error: float32 [8, 64, 512], P('lat', 'lon'), may hold values from 0.3 to 1.2
- where_frac: bfloat16 [8, 64, 3, 512], P('lat', 'lon'), may hold values from 0 to 1
- spread: bfloat16 [8, 64, 512], P('lat', 'lon'), may hold values from 2 to 4
- obs_type: int32 [8, 64, 512], P('lat', 'lon'), may hold values from 0 to 2
Outputs:
- solution: float32 [8, 64, 16, 512], P('lat', 'lon')
- residual: float32 [8, 64, 16, 512], P('lat', 'lon')
The draws below stay inside these ranges and needn't reach their ends.
All inputs are finite; a program needn't handle non-finite values.
Results may differ from the reference program's by a relative error of at most 0.0098.
Values may be sent and summed in bfloat16 or wider, within the bound.
No kernel may reach another device: no remote copies, remote signals or barrier semaphores. Data moves between devices by JAX's collectives and lax.ppermute only.
A program may use at most 64 MiB of HBM per device.

```python
import math
import jax
import jax.numpy as jnp
from jax import lax

OBS_DEV = 512
RHS = 16
ITERS = 3
BANDS = 8
SECTORS = 64


def draw_where_frac(key, part):
    key = jax.random.fold_in(key, 11)
    side_key, near_key, level_key = jax.random.split(key, 3)
    upper = jax.random.bernoulli(side_key, 0.5, (BANDS, SECTORS, 2, OBS_DEV))
    nearness = 0.05 * jax.random.uniform(near_key, (BANDS, SECTORS, 2, OBS_DEV), jnp.float32)
    horizontal = jnp.where(upper, 1.0 - nearness, nearness)
    level = jax.random.uniform(level_key, (BANDS, SECTORS, 1, OBS_DEV), jnp.float32)
    return jnp.concatenate([horizontal, level], axis=2).astype(jnp.bfloat16)


def set_ends(values, key, smallest, high):
    shape = values.shape
    spot = [jax.random.randint(jax.random.fold_in(key, axis), (), 0, shape[axis]) for axis in range(len(shape))]
    values = values.at[tuple(spot)].set(smallest)
    longest = shape.index(max(shape))
    spot[longest] = (spot[longest] + 1) % shape[longest]
    return values.at[tuple(spot)].set(high)


def shard_levels(own_key, shape, pieces, least, high):
    def one(dim, shards_of):
        heights = jax.random.uniform(jax.random.fold_in(jax.random.fold_in(own_key, 6), dim), (shards_of,), jnp.float32, least / len(pieces), high / len(pieces))
        return jnp.repeat(jnp.exp(heights), shape[dim] // shards_of).reshape((-1,) + (1,) * (len(shape) - dim - 1))

    loudness = one(*pieces[0])
    for cut in pieces[1:]:
        loudness = loudness * one(*cut)
    return loudness


def gaussian(rng, extent, width, most, cuts=(), held_as=jnp.bfloat16):
    factor_of = shard_levels(rng, extent, cuts, -0.22, 0.18) if cuts else 1.0
    values = jax.random.normal(rng, extent, jnp.float32) * width * factor_of
    return jnp.minimum(jnp.maximum(values, -most), most).astype(held_as)


def setup_inputs(seed: int = 0) -> dict:
    keys = jax.random.split(jax.random.key(seed), 6)
    innovations = gaussian(keys[0], (BANDS, SECTORS, RHS, OBS_DEV), 1.0, 6.0, ((0, 8), (1, 64)), jnp.float32)
    obs_error = jnp.clip(jnp.exp(math.log(1.2) - 1.3862944 * jax.random.uniform(keys[1], (BANDS, SECTORS, OBS_DEV), jnp.float32) ** shard_levels(keys[1], (BANDS, SECTORS, OBS_DEV), ((0, 8), (1, 64)), -0.2, 0.2)), 0.3, 1.2)
    where_frac = draw_where_frac(jax.random.fold_in(keys[5], 71), 0)
    spread = jnp.clip(jnp.exp(math.log(4.0) - 0.6931472 * jax.random.uniform(keys[3], (BANDS, SECTORS, OBS_DEV), jnp.float32) ** shard_levels(keys[3], (BANDS, SECTORS, OBS_DEV), ((0, 8), (1, 64)), -0.2, 0.2)), 2.0, 4.0).astype(jnp.bfloat16)
    obs_type = set_ends(jax.random.randint(keys[4], (BANDS, SECTORS, OBS_DEV), 0, 3), jax.random.fold_in(keys[4], 1), 0, 2).astype(jnp.int32)
    return {"innovations": innovations, "obs_error": obs_error, "where_frac": where_frac, "spread": spread, "obs_type": obs_type}


LAT_LIMIT = 80.0 * math.pi / 180.0
HORIZ_SQ = 0.05 * 0.05
VERT_SQ = 0.3 * 0.3
TAPER_STEP = 0.45


def features(obs_info, band_at, sector_at, bands, sectors):
    values = obs_info.astype(jnp.float32)
    latitude = (band_at.astype(jnp.float32) + values[0]) * (2.0 * LAT_LIMIT / bands) - LAT_LIMIT
    longitude = (sector_at.astype(jnp.float32) + values[1]) * (2.0 * math.pi / sectors)
    cos_lat = jnp.cos(latitude)
    return (cos_lat * jnp.cos(longitude), cos_lat * jnp.sin(longitude), jnp.sin(latitude), values[2], values[3], values[4])


def tile_rows(own_feat, far_feat, weight):
    inner = own_feat[0][:, None] * far_feat[0][None, :] + own_feat[1][:, None] * far_feat[1][None, :] + own_feat[2][:, None] * far_feat[2][None, :]
    vert_gap = own_feat[3][:, None] - far_feat[3][None, :]
    kernel = jnp.exp((inner - 1.0) / HORIZ_SQ - vert_gap * vert_gap / (2.0 * VERT_SQ))
    same_type = own_feat[5][:, None] == far_feat[5][None, :]
    height_pair = (own_feat[5][:, None] == 0.0) | (far_feat[5][None, :] == 0.0)
    coupling = jnp.where(same_type, 1.0, jnp.where(height_pair, 0.45, 0.25)).astype(jnp.float32)
    return ((own_feat[4][:, None] * far_feat[4][None, :]) * coupling * kernel * weight).astype(jnp.bfloat16)


def wrap_pad(field):
    wrapped = jnp.concatenate([field[:, -1:], field, field[:, :1]], axis=1)
    zeros = jnp.zeros((1,) + wrapped.shape[1:], wrapped.dtype)
    return jnp.concatenate([zeros, wrapped, zeros], axis=0)


def reference(innovations, obs_error, where_frac, spread, obs_type):
    obs_info = jnp.concatenate([where_frac.astype(jnp.float32), spread.astype(jnp.float32)[:, :, None], obs_type.astype(jnp.float32)[:, :, None]], axis=2)
    info_pad = wrap_pad(obs_info)

    def apply(direction):
        field_pad = wrap_pad(direction.astype(jnp.bfloat16).astype(jnp.float32))

        def one_block(flat_index):
            band_at = (flat_index // SECTORS).astype(jnp.int32)
            sector_at = (flat_index % SECTORS).astype(jnp.int32)
            near_info = lax.dynamic_slice(info_pad, (band_at, sector_at, jnp.int32(0), jnp.int32(0)), (3, 3, 5, OBS_DEV))
            near_field = lax.dynamic_slice(field_pad, (band_at, sector_at, jnp.int32(0), jnp.int32(0)), (3, 3, RHS, OBS_DEV))
            own_feat = features(near_info[1, 1], band_at, sector_at, BANDS, SECTORS)
            result = jnp.zeros((RHS, OBS_DEV), jnp.float32)
            for step_lat in (-1, 0, 1):
                for step_lon in (-1, 0, 1):
                    far_feat = features(near_info[step_lat + 1, step_lon + 1], band_at + step_lat, sector_at + step_lon, BANDS, SECTORS)
                    tile = tile_rows(own_feat, far_feat, TAPER_STEP ** (abs(step_lat) + abs(step_lon))).astype(jnp.float32)
                    result = result + jnp.dot(near_field[step_lat + 1, step_lon + 1], tile.T, precision=lax.Precision.HIGHEST)
            return result

        blocks = lax.map(one_block, jnp.arange(BANDS * SECTORS, dtype=jnp.int32))
        return blocks.reshape(BANDS, SECTORS, RHS, OBS_DEV) + obs_error[:, :, None, :] * direction

    solution = jnp.zeros_like(innovations)
    residual = innovations
    direction = innovations
    norm_now = jnp.sum(residual * residual, axis=(0, 1, 3))
    for iteration in range(ITERS):
        image = apply(direction)
        step_len = norm_now / jnp.sum(direction * image, axis=(0, 1, 3))
        solution = solution + step_len[None, None, :, None] * direction
        residual = residual - step_len[None, None, :, None] * image
        norm_next = jnp.sum(residual * residual, axis=(0, 1, 3))
        direction = residual + (norm_next / norm_now)[None, None, :, None] * direction
        norm_now = norm_next
    return solution, residual
```

```python
import math

import jax
import jax.numpy as jnp
from jax import lax
from jax.sharding import Mesh, PartitionSpec as P

ITERS = 3


LAT_LIMIT = 80.0 * math.pi / 180.0
HORIZ_SQ = 0.05 * 0.05
VERT_SQ = 0.3 * 0.3
TAPER_STEP = 0.45


def features(obs_info, band_at, sector_at, bands, sectors):
    values = obs_info.astype(jnp.float32)
    latitude = (band_at.astype(jnp.float32) + values[0]) * (2.0 * LAT_LIMIT / bands) - LAT_LIMIT
    longitude = (sector_at.astype(jnp.float32) + values[1]) * (2.0 * math.pi / sectors)
    cos_lat = jnp.cos(latitude)
    return (
        cos_lat * jnp.cos(longitude),
        cos_lat * jnp.sin(longitude),
        jnp.sin(latitude),
        values[2],
        values[3],
        values[4],
    )


def tile_rows(own_feat, far_feat, weight):
    inner = (
        own_feat[0][:, None] * far_feat[0][None, :]
        + own_feat[1][:, None] * far_feat[1][None, :]
        + own_feat[2][:, None] * far_feat[2][None, :]
    )
    vert_gap = own_feat[3][:, None] - far_feat[3][None, :]
    kernel = jnp.exp((inner - 1.0) / HORIZ_SQ - vert_gap * vert_gap / (2.0 * VERT_SQ))
    same_type = own_feat[5][:, None] == far_feat[5][None, :]
    height_pair = (own_feat[5][:, None] == 0.0) | (far_feat[5][None, :] == 0.0)
    coupling = jnp.where(same_type, 1.0, jnp.where(height_pair, 0.45, 0.25)).astype(jnp.float32)
    return (own_feat[4][:, None] * far_feat[4][None, :] * coupling * kernel * weight).astype(
        jnp.bfloat16
    )


def build_tile(own_feat, far_feat, weight):
    count = own_feat[0].shape[0]
    stacked = jnp.stack(own_feat).reshape(6, count // 128, 128).transpose(1, 0, 2)
    pieces = lax.map(
        lambda piece: tile_rows(tuple((piece[i] for i in range(6))), far_feat, weight), stacked
    )
    return pieces.reshape(count, count)


LAT = ("z_lo", "x")
LON = ("z_hi", "y", "core")
GROUPS = (("z_lo", "z_hi", "x"), ("y", "core"))


def extent(axes):
    size = 1
    for axis in axes:
        size *= lax.axis_size(axis)
    return size


def swaps(count, first):
    pairs = []
    for low in range(first, count + first - 1, 2):
        high = (low + 1) % count
        pairs += [(low, high), (high, low)]
    return pairs


def widened(block):
    count = extent(LON)
    outer = lax.ppermute(block, LON, swaps(count, 1))
    inner = lax.ppermute(block, LON, swaps(count, 0))
    odd = lax.axis_index(LON) % 2 == 1
    return jnp.stack([jnp.where(odd, inner, outer), block, jnp.where(odd, outer, inner)])


def all_bands(wide):
    count = extent(LAT)
    below = lax.ppermute(wide, LAT, [(i, i + 1) for i in range(count - 1)])
    above = lax.ppermute(wide, LAT, [(i + 1, i) for i in range(count - 1)])
    return below, above


def contract(field, tile):
    return lax.dot_general(
        field, tile, (((1,), (1,)), ((), ())), preferred_element_type=jnp.float32
    )


def global_sum(value):
    for axes in GROUPS:
        count = extent(axes)
        spread_out = jnp.broadcast_to(value, (count,) + value.shape)
        value = jnp.sum(lax.all_to_all(spread_out, axes, 0, 0), axis=0)
    return value


def coefficients(gram):
    def inner(left, right):
        total = 0.0
        for i in range(4):
            for j in range(4):
                if left[i] is not None and right[j] is not None:
                    total = total + left[i] * right[j] * gram[min(i, j), max(i, j)]
        return total

    def axpy(scale, added, start):
        out = []
        for a, s in zip(added, start):
            if a is None:
                out.append(s)
            else:
                out.append(scale * a if s is None else s + scale * a)
        return out

    one = jnp.ones_like(gram[0, 0])
    answer = [None] * 4
    residual = [one, None, None, None]
    direction = residual
    norm_now = gram[0, 0]
    for iteration in range(ITERS):
        image = [None] + direction[:3]
        step_len = norm_now / inner(direction, image)
        answer = axpy(step_len, direction, answer)
        residual = axpy(-step_len, image, residual)
        if iteration < ITERS - 1:
            norm_next = inner(residual, residual)
            direction = axpy(norm_next / norm_now, direction, residual)
            norm_now = norm_next
    return answer[:3], residual


def local(innovations, obs_error, where_frac, spread, obs_type):
    bands = extent(LAT)
    sectors = extent(LON)
    my_band = lax.axis_index(LAT)
    my_sector = lax.axis_index(LON)
    start = innovations[0, 0]
    error_var = obs_error[0, 0]
    message = jnp.concatenate(
        [
            start.astype(jnp.bfloat16),
            where_frac[0, 0],
            spread[0, 0][None],
            obs_type[0, 0][None].astype(jnp.bfloat16),
            jnp.zeros((3, start.shape[1]), jnp.bfloat16),
        ],
        axis=0,
    )
    wide = widened(message)
    below, above = all_bands(wide)
    blocks = {-1: below, 0: wide, 1: above}
    own_feat = features(message[16:21], my_band, my_sector, bands, sectors)
    offsets = [(a, b) for a in (-1, 0, 1) for b in (-1, 0, 1)]

    def far_tile(step_lat, step_lon):
        near_info = blocks[step_lat][step_lon + 1, 16:21]
        far_feat = features(near_info, my_band + step_lat, my_sector + step_lon, bands, sectors)
        return build_tile(own_feat, far_feat, TAPER_STEP ** (abs(step_lat) + abs(step_lon)))

    tiles = [far_tile(a, b) for a, b in offsets]

    def apply(field, near):
        result = error_var[None, :] * field
        for (a, b), tile in zip(offsets, tiles):
            result = result + contract(near[a][b + 1, :16], tile)
        return result

    basis = [start]
    for power in range(3):
        if power > 0:
            wide = widened(basis[-1].astype(jnp.bfloat16))
            below, above = all_bands(wide)
            blocks = {-1: below, 0: wide, 1: above}
        basis.append(apply(basis[-1], blocks))
    pairs = [(i, j) for i in range(4) for j in range(i, 4) if (i, j) != (3, 3)]
    parts = [jnp.sum(basis[i] * basis[j], axis=1) for i, j in pairs]
    parts += [jnp.zeros_like(parts[0])] * (16 - len(parts))
    sums = global_sum(jnp.concatenate(parts).reshape(2, 128)).reshape(16, 16)
    gram = {pair: sums[i] for i, pair in enumerate(pairs)}
    answer, residual = coefficients(gram)
    answer = sum(c[:, None] * v for c, v in zip(answer, basis))
    residual = sum(c[:, None] * v for c, v in zip(residual, basis))
    return (answer[None, None], residual[None, None])


def solution(mesh):
    fine = Mesh(mesh.devices.reshape(2, 4, 4, 8, 2), LAT + LON)
    in_specs = (
        P(LAT, LON, None, None),
        P(LAT, LON, None),
        P(LAT, LON, None, None),
        P(LAT, LON, None),
        P(LAT, LON, None),
    )
    out_specs = (P(LAT, LON, None, None), P(LAT, LON, None, None))
    return jax.shard_map(local, mesh=fine, in_specs=in_specs, out_specs=out_specs, check_vma=False)
```

```python
import functools
import math

import jax
import jax.numpy as jnp
from jax import lax
from jax.experimental import pallas as pl
from jax.experimental.pallas import tpu as pltpu
from jax.sharding import Mesh, PartitionSpec as P

ITERS = 3
BANDS = 8
SECTORS = 64
OBS = 512
RHS = 16

LAT_LIMIT = 80.0 * math.pi / 180.0
HORIZ_SQ = 0.05 * 0.05
VERT_SQ = 0.3 * 0.3
TAPER_STEP = 0.45
LOG2E = 1.0 / math.log(2.0)
HORIZ = LOG2E / HORIZ_SQ
VERT = LOG2E / (2.0 * VERT_SQ)
COUPLING = ((1.0, 0.45, 0.45), (0.45, 1.0, 0.25), (0.45, 0.25, 1.0))

LAT = ("z_lo", "x")
LON = ("z_hi", "y", "core")
GROUPS = (("z_lo", "z_hi", "x"), ("y", "core"))


def extent(axes):
    size = 1
    for axis in axes:
        size *= lax.axis_size(axis)
    return size


def swaps(count, first):
    pairs = []
    for low in range(first, count + first - 1, 2):
        high = (low + 1) % count
        pairs += [(low, high), (high, low)]
    return pairs


def widened(block):
    count = extent(LON)
    inner = lax.ppermute(block, LON, swaps(count, 0))
    outer = lax.ppermute(block, LON, swaps(count, 1))
    odd = lax.axis_index(LON) % 2 == 1
    return jnp.stack([jnp.where(odd, inner, outer), block, jnp.where(odd, outer, inner)])


def all_bands(wide):
    count = extent(LAT)
    below = lax.ppermute(wide, LAT, [(i, i + 1) for i in range(count - 1)])
    above = lax.ppermute(wide, LAT, [(i + 1, i) for i in range(count - 1)])
    return below, above


def rounded(value):
    return value.astype(jnp.bfloat16).astype(jnp.float32)


def pieces(value):
    high = rounded(value)
    mid = rounded(value - high)
    return high, mid, rounded(value - high - mid)


def describe_kernel(place_ref, start_ref, frac_ref, spread_ref, type_ref, message_ref, own_ref, far_rows, own_rows):
    frac = frac_ref[...].astype(jnp.float32)
    latitude = (place_ref[0].astype(jnp.float32) + frac[0:1]) * (2.0 * LAT_LIMIT / BANDS) - LAT_LIMIT
    longitude = (place_ref[1].astype(jnp.float32) + frac[1:2]) * (2.0 * math.pi / SECTORS)
    angles = jnp.concatenate([latitude, longitude], axis=0)
    cosines, sines = jnp.cos(angles), jnp.sin(angles)
    place = (cosines[0:1] * cosines[1:2], cosines[0:1] * sines[1:2], sines[0:1])
    level = frac[2:3]
    sigma = jnp.log(spread_ref[...].astype(jnp.float32)) * LOG2E - VERT * level * level
    kind = type_ref[...]
    one = jnp.ones_like(level)
    table = [[math.log2(k) for k in row] for row in COUPLING]

    def looked_up(column):
        return jnp.where(kind == 0, table[0][column], jnp.where(kind == 1, table[1][column], table[2][column]))

    at_height = looked_up(0)
    far = []
    own = []
    for axis in place:
        far += pieces(axis)
        own += [HORIZ * axis] * 3
    far += [level, jnp.where(kind == 1, one, 0.0), jnp.where(kind == 2, one, 0.0)]
    own += [2.0 * VERT * level, looked_up(1) - at_height, looked_up(2) - at_height]
    far += [*pieces(sigma), one]
    own += [one, one, one, sigma + at_height - HORIZ]
    for row in range(16):
        far_rows[row : row + 1, :] = far[row]
        own_rows[row : row + 1, :] = own[row]
    message_ref[0:16, :] = start_ref[...].astype(jnp.bfloat16)
    message_ref[16:32, :] = far_rows[...].astype(jnp.bfloat16)
    left = own_rows[...]
    for piece in range(3):
        part = left.astype(jnp.bfloat16)
        own_ref[16 * piece : 16 * piece + 16, :] = part
        left = left - part.astype(jnp.float32)


def whole(space=pltpu.VMEM):
    return pl.BlockSpec(memory_space=space)


def describe(place, start, where_frac, spread, obs_type):
    return pl.pallas_call(
        describe_kernel,
        out_shape=(
            jax.ShapeDtypeStruct((32, OBS), jnp.bfloat16),
            jax.ShapeDtypeStruct((48, OBS), jnp.bfloat16),
        ),
        in_specs=[whole(pltpu.SMEM)] + [whole()] * 4,
        out_specs=(whole(), whole()),
        scratch_shapes=[pltpu.VMEM((16, OBS), jnp.float32)] * 2,
        name="describe",
    )(place, start, where_frac, spread, obs_type)


CHUNK = 256


def build_kernel(steps, carried, *refs):
    messages, (own_ref, added_ref), (tile_ref, sum_ref, *sent) = refs[: len(carried)], refs[len(carried) : len(carried) + 2], refs[len(carried) + 2 :]
    own = own_ref[...]
    total = added_ref[...]
    for k, (which, slot, step) in enumerate(steps):
        taper = step * math.log2(TAPER_STEP)
        for low in range(0, OBS, CHUNK):
            far = messages[which][slot, 16:32, low : low + CHUNK]
            far = jnp.concatenate([far, far, far], axis=0)
            power = lax.dot_general(far, own, (((0,), (0,)), ((), ())), preferred_element_type=jnp.float32)
            tile = jnp.exp2(power + taper if step else power).astype(jnp.bfloat16)
            tile_ref[k, low : low + CHUNK, :] = tile
            field = messages[which][slot, 0:16, low : low + CHUNK]
            total = total + jnp.dot(field, tile, preferred_element_type=jnp.float32)
    sum_ref[...] = total
    for ref in sent:
        ref[...] = total.astype(jnp.bfloat16)


def apply_kernel(steps, carried, *refs):
    messages, (tile_ref, added_ref), (sum_ref, *sent) = refs[: len(carried)], refs[len(carried) : len(carried) + 2], refs[len(carried) + 2 :]
    total = added_ref[...]
    for k, (which, slot, _) in enumerate(steps):
        total = total + jnp.dot(messages[which][slot], tile_ref[k], preferred_element_type=jnp.float32)
    sum_ref[...] = total
    for ref in sent:
        ref[...] = total.astype(jnp.bfloat16)


SAME_BAND = ((0, 0, 1), (0, 1, 0), (0, 2, 1))
OTHER_BANDS = ((0, 0, 2), (0, 1, 1), (0, 2, 2), (1, 0, 2), (1, 1, 1), (1, 2, 2))


def cost(steps, built):
    entries = len(steps) * OBS * OBS
    return pl.CostEstimate(
        flops=2 * entries * (RHS + 256 * built),
        bytes_accessed=2 * entries,
        transcendentals=entries * built,
    )


def sums(last):
    shapes = [jax.ShapeDtypeStruct((RHS, OBS), jnp.float32)]
    if last:
        shapes.append(jax.ShapeDtypeStruct((RHS, OBS), jnp.bfloat16))
    return shapes


def build(steps, carried, own, added, last):
    tiles = pltpu.VMEM((len(steps), OBS, OBS), jnp.bfloat16)
    shapes = [tiles] + sums(last)
    return pl.pallas_call(
        functools.partial(build_kernel, steps, carried),
        out_shape=shapes,
        in_specs=[whole()] * (len(carried) + 2),
        out_specs=[whole()] * len(shapes),
        compiler_params=pltpu.CompilerParams(vmem_limit_bytes=24 << 20),
        cost_estimate=cost(steps, 1),
        name="build",
    )(*carried, own, added)


def apply(steps, carried, tiles, added, last):
    shapes = sums(last)
    return pl.pallas_call(
        functools.partial(apply_kernel, steps, carried),
        out_shape=shapes,
        in_specs=[whole()] * (len(carried) + 2),
        out_specs=[whole()] * len(shapes),
        compiler_params=pltpu.CompilerParams(vmem_limit_bytes=24 << 20),
        cost_estimate=cost(steps, 0),
        name="apply",
    )(*carried, tiles, added)


def local(innovations, obs_error, where_frac, spread, obs_type):
    start = innovations[0, 0]
    error_var = obs_error[0, 0][None]
    place = jnp.stack([lax.axis_index(LAT), lax.axis_index(LON)]).astype(jnp.int32)
    message, own = describe(place, start, where_frac[0, 0], spread[0], obs_type[0])
    wide = widened(message)
    below, above = all_bands(wide)
    near_tiles, part = build(SAME_BAND, [wide], own, error_var * start, False)
    far_tiles, field, sent = build(OTHER_BANDS, [below, above], own, part, True)
    basis = [start, field]
    for last in (False, True):
        wide = widened(sent)
        below, above = all_bands(wide)
        part, = apply(SAME_BAND, [wide], near_tiles, error_var * field, False)
        if last:
            field, = apply(OTHER_BANDS, [below, above], far_tiles, part, False)
        else:
            field, sent = apply(OTHER_BANDS, [below, above], far_tiles, part, True)
        basis.append(field)
    pairs = [(i, j) for i in range(4) for j in range(i, 4) if (i, j) != (3, 3)]
    parts = [jnp.sum(basis[i] * basis[j], axis=1) for i, j in pairs]
    parts += [jnp.zeros_like(parts[0])] * (16 - len(parts))
    totals = global_sum(jnp.concatenate(parts).reshape(2, 128)).reshape(16, 16)
    gram = {pair: totals[i] for i, pair in enumerate(pairs)}
    answer, residual = coefficients(gram)
    answer = sum(c[:, None] * v for c, v in zip(answer, basis))
    residual = sum(c[:, None] * v for c, v in zip(residual, basis))
    return (answer[None, None], residual[None, None])


def global_sum(value):
    for axes in GROUPS:
        count = extent(axes)
        spread_out = jnp.broadcast_to(value, (count,) + value.shape)
        value = jnp.sum(lax.all_to_all(spread_out, axes, 0, 0), axis=0)
    return value


def coefficients(gram):
    def inner(left, right):
        total = 0.0
        for i in range(4):
            for j in range(4):
                if left[i] is not None and right[j] is not None:
                    total = total + left[i] * right[j] * gram[min(i, j), max(i, j)]
        return total

    def axpy(scale, added, start):
        out = []
        for a, s in zip(added, start):
            if a is None:
                out.append(s)
            else:
                out.append(scale * a if s is None else s + scale * a)
        return out

    one = jnp.ones_like(gram[0, 0])
    answer = [None] * 4
    residual = [one, None, None, None]
    direction = residual
    norm_now = gram[0, 0]
    for iteration in range(ITERS):
        image = [None] + direction[:3]
        step_len = norm_now / inner(direction, image)
        answer = axpy(step_len, direction, answer)
        residual = axpy(-step_len, image, residual)
        if iteration < ITERS - 1:
            norm_next = inner(residual, residual)
            direction = axpy(norm_next / norm_now, direction, residual)
            norm_now = norm_next
    return answer[:3], residual


def solution(mesh):
    fine = Mesh(mesh.devices.reshape(2, 4, 4, 8, 2), LAT + LON)
    in_specs = (
        P(LAT, LON, None, None),
        P(LAT, LON, None),
        P(LAT, LON, None, None),
        P(LAT, LON, None),
        P(LAT, LON, None),
    )
    out_specs = (P(LAT, LON, None, None), P(LAT, LON, None, None))
    return jax.shard_map(local, mesh=fine, in_specs=in_specs, out_specs=out_specs, check_vma=False)
```

```python
import functools
import math

import jax
import jax.numpy as jnp
from jax import lax
from jax.experimental import pallas as pl
from jax.experimental.pallas import tpu as pltpu
from jax.sharding import Mesh, PartitionSpec as P

ITERS = 3
BANDS = 8
SECTORS = 64
OBS = 512
RHS = 16

LAT_LIMIT = 80.0 * math.pi / 180.0
HORIZ_SQ = 0.05 * 0.05
VERT_SQ = 0.3 * 0.3
TAPER_STEP = 0.45
LOG2E = 1.0 / math.log(2.0)
HORIZ = LOG2E / HORIZ_SQ
VERT = LOG2E / (2.0 * VERT_SQ)
COUPLING = ((1.0, 0.45, 0.45), (0.45, 1.0, 0.25), (0.45, 0.25, 1.0))

LAT = ("z_lo", "x")
LON = ("z_hi", "y", "core")
GROUPS = (("z_lo", "z_hi", "x"), ("y", "core"))


def extent(axes):
    size = 1
    for axis in axes:
        size *= lax.axis_size(axis)
    return size


def swaps(count, first):
    pairs = []
    for low in range(first, count + first - 1, 2):
        high = (low + 1) % count
        pairs += [(low, high), (high, low)]
    return pairs


def widened(block):
    count = extent(LON)
    inner = lax.ppermute(block, LON, swaps(count, 0))
    outer = lax.ppermute(block, LON, swaps(count, 1))
    return jnp.stack([outer, block, inner])


def all_bands(wide):
    count = extent(LAT)
    below = lax.ppermute(wide, LAT, [(i, i + 1) for i in range(count - 1)])
    above = lax.ppermute(wide, LAT, [(i + 1, i) for i in range(count - 1)])
    return below, above


def rounded(value):
    return value.astype(jnp.bfloat16).astype(jnp.float32)


def pieces(value):
    high = rounded(value)
    mid = rounded(value - high)
    return high, mid, rounded(value - high - mid)


def describe_kernel(
    place_ref, start_ref, error_ref, frac_ref, spread_ref, type_ref,
    message_ref, own_ref, error_out_ref, added_ref, far_rows, own_rows,
):
    frac = frac_ref[...].astype(jnp.float32)
    latitude = (place_ref[0].astype(jnp.float32) + frac[0:1]) * (2.0 * LAT_LIMIT / BANDS) - LAT_LIMIT
    longitude = (place_ref[1].astype(jnp.float32) + frac[1:2]) * (2.0 * math.pi / SECTORS)
    angles = jnp.concatenate([latitude, longitude], axis=0)
    cosines, sines = jnp.cos(angles), jnp.sin(angles)
    place = (cosines[0:1] * cosines[1:2], cosines[0:1] * sines[1:2], sines[0:1])
    level = frac[2:3]
    sigma = jnp.log(spread_ref[...].astype(jnp.float32)) * LOG2E - VERT * level * level
    kind = type_ref[...]
    one = jnp.ones_like(level)
    table = [[math.log2(k) for k in row] for row in COUPLING]

    def looked_up(column):
        return jnp.where(kind == 0, table[0][column], jnp.where(kind == 1, table[1][column], table[2][column]))

    at_height = looked_up(0)
    far = []
    own = []
    for axis in place:
        far += pieces(axis)
        own += [HORIZ * axis] * 3
    far += [level, jnp.where(kind == 1, one, 0.0), jnp.where(kind == 2, one, 0.0)]
    own += [2.0 * VERT * level, looked_up(1) - at_height, looked_up(2) - at_height]
    far += [*pieces(sigma), one]
    own += [one, one, one, sigma + at_height - HORIZ]
    for row in range(16):
        far_rows[row : row + 1, :] = far[row]
        own_rows[row : row + 1, :] = own[row]
    message_ref[0:16, :] = start_ref[...].astype(jnp.bfloat16)
    message_ref[16:32, :] = far_rows[...].astype(jnp.bfloat16)
    error_out_ref[...] = error_ref[...]
    added_ref[...] = error_ref[...] * start_ref[...]
    left = own_rows[...]
    for piece in range(3):
        part = left.astype(jnp.bfloat16)
        own_ref[16 * piece : 16 * piece + 16, :] = part
        left = left - part.astype(jnp.float32)


def whole(space=pltpu.VMEM):
    return pl.BlockSpec(memory_space=space)


def describe(place, start, error_var, where_frac, spread, obs_type):
    return pl.pallas_call(
        describe_kernel,
        out_shape=(
            pltpu.VMEM((32, OBS), jnp.bfloat16),
            pltpu.VMEM((48, OBS), jnp.bfloat16),
            pltpu.VMEM((1, OBS), jnp.float32),
            pltpu.VMEM((RHS, OBS), jnp.float32),
        ),
        in_specs=[whole(pltpu.SMEM)] + [whole()] * 5,
        out_specs=[whole()] * 4,
        scratch_shapes=[pltpu.VMEM((16, OBS), jnp.float32)] * 2,
        name="describe",
    )(place, start, error_var, where_frac, spread, obs_type)


CHUNK = 256


def build_kernel(steps, carried, *refs):
    messages, (own_ref, added_ref), (tile_ref, sum_ref, *sent) = refs[: len(carried)], refs[len(carried) : len(carried) + 2], refs[len(carried) + 2 :]
    own = own_ref[...]
    total = added_ref[...]
    for k, (which, slot, step) in enumerate(steps):
        taper = step * math.log2(TAPER_STEP)
        for low in range(0, OBS, CHUNK):
            far = messages[which][slot, 16:32, low : low + CHUNK]
            far = jnp.concatenate([far, far, far], axis=0)
            power = lax.dot_general(far, own, (((0,), (0,)), ((), ())), preferred_element_type=jnp.float32)
            tile = jnp.exp2(power + taper if step else power).astype(jnp.bfloat16)
            tile_ref[k, low : low + CHUNK, :] = tile
            field = messages[which][slot, 0:16, low : low + CHUNK]
            total = total + jnp.dot(field, tile, preferred_element_type=jnp.float32)
    sum_ref[...] = total
    for ref in sent:
        ref[...] = total.astype(jnp.bfloat16)


def apply_kernel(steps, carried, scaled, *refs):
    messages, (tile_ref, *added) = refs[: len(carried)], refs[len(carried) : len(carried) + 2 + scaled]
    sum_ref, *sent = refs[len(carried) + 2 + scaled :]
    total = added[0][...]
    if scaled:
        total = total * added[1][...]
    for k, (which, slot, _) in enumerate(steps):
        total = total + jnp.dot(messages[which][slot], tile_ref[k], preferred_element_type=jnp.float32)
    sum_ref[...] = total
    for ref in sent:
        ref[...] = total.astype(jnp.bfloat16)


SAME_BAND = ((0, 0, 1), (0, 1, 0), (0, 2, 1))
OTHER_BANDS = ((0, 0, 2), (0, 1, 1), (0, 2, 2), (1, 0, 2), (1, 1, 1), (1, 2, 2))


def cost(steps, built):
    entries = len(steps) * OBS * OBS
    return pl.CostEstimate(
        flops=2 * entries * (RHS + 256 * built),
        bytes_accessed=2 * entries,
        transcendentals=entries * built,
    )


def sums(last):
    shapes = [pltpu.VMEM((RHS, OBS), jnp.float32)]
    if last:
        shapes.append(pltpu.VMEM((RHS, OBS), jnp.bfloat16))
    return shapes


def build(steps, carried, own, added, last):
    tiles = pltpu.VMEM((len(steps), OBS, OBS), jnp.bfloat16)
    shapes = [tiles] + sums(last)
    return pl.pallas_call(
        functools.partial(build_kernel, steps, carried),
        out_shape=shapes,
        in_specs=[whole()] * (len(carried) + 2),
        out_specs=[whole()] * len(shapes),
        compiler_params=pltpu.CompilerParams(vmem_limit_bytes=24 << 20),
        cost_estimate=cost(steps, 1),
        name="build",
    )(*carried, own, added)


def apply(steps, carried, tiles, added, last):
    shapes = sums(last)
    scaled = len(added) - 1
    return pl.pallas_call(
        functools.partial(apply_kernel, steps, carried, scaled),
        out_shape=shapes,
        in_specs=[whole()] * (len(carried) + 2 + scaled),
        out_specs=[whole()] * len(shapes),
        compiler_params=pltpu.CompilerParams(vmem_limit_bytes=24 << 20),
        cost_estimate=cost(steps, 0),
        name="apply",
    )(*carried, tiles, *added)


def local(innovations, obs_error, where_frac, spread, obs_type):
    start = innovations[0, 0]
    place = jnp.stack([lax.axis_index(LAT), lax.axis_index(LON)]).astype(jnp.int32)
    message, own, error_var, added = describe(place, start, obs_error[0], where_frac[0, 0], spread[0], obs_type[0])
    wide = widened(message)
    below, above = all_bands(wide)
    near_tiles, part = build(SAME_BAND, [wide], own, added, False)
    far_tiles, field, sent = build(OTHER_BANDS, [below, above], own, part, True)
    basis = [start, field]
    for last in (False, True):
        wide = widened(sent)
        below, above = all_bands(wide)
        part, = apply(SAME_BAND, [wide], near_tiles, [field, error_var], False)
        if last:
            field, = apply(OTHER_BANDS, [below, above], far_tiles, [part], False)
        else:
            field, sent = apply(OTHER_BANDS, [below, above], far_tiles, [part], True)
        basis.append(field)
    pairs = [(i, j) for i in range(4) for j in range(i, 4) if (i, j) != (3, 3)]
    parts = [jnp.sum(basis[i] * basis[j], axis=1) for i, j in pairs]
    parts += [jnp.zeros_like(parts[0])] * (16 - len(parts))
    totals = global_sum(jnp.concatenate(parts).reshape(2, 128)).reshape(16, 16)
    gram = {pair: totals[i] for i, pair in enumerate(pairs)}
    answer, residual = coefficients(gram)
    answer = sum(c[:, None] * v for c, v in zip(answer, basis))
    residual = sum(c[:, None] * v for c, v in zip(residual, basis))
    return (answer[None, None], residual[None, None])


def global_sum(value):
    for axes in GROUPS:
        count = extent(axes)
        spread_out = jnp.broadcast_to(value, (count,) + value.shape)
        value = jnp.sum(lax.all_to_all(spread_out, axes, 0, 0), axis=0)
    return value


def coefficients(gram):
    def inner(left, right):
        total = 0.0
        for i in range(4):
            for j in range(4):
                if left[i] is not None and right[j] is not None:
                    total = total + left[i] * right[j] * gram[min(i, j), max(i, j)]
        return total

    def axpy(scale, added, start):
        out = []
        for a, s in zip(added, start):
            if a is None:
                out.append(s)
            else:
                out.append(scale * a if s is None else s + scale * a)
        return out

    one = jnp.ones_like(gram[0, 0])
    answer = [None] * 4
    residual = [one, None, None, None]
    direction = residual
    norm_now = gram[0, 0]
    for iteration in range(ITERS):
        image = [None] + direction[:3]
        step_len = norm_now / inner(direction, image)
        answer = axpy(step_len, direction, answer)
        residual = axpy(-step_len, image, residual)
        if iteration < ITERS - 1:
            norm_next = inner(residual, residual)
            direction = axpy(norm_next / norm_now, direction, residual)
            norm_now = norm_next
    return answer[:3], residual


def solution(mesh):
    fine = Mesh(mesh.devices.reshape(2, 4, 4, 8, 2), LAT + LON)
    in_specs = (
        P(LAT, LON, None, None),
        P(LAT, LON, None),
        P(LAT, LON, None, None),
        P(LAT, LON, None),
        P(LAT, LON, None),
    )
    out_specs = (P(LAT, LON, None, None), P(LAT, LON, None, None))
    return jax.shard_map(local, mesh=fine, in_specs=in_specs, out_specs=out_specs, check_vma=False)
```

```python
import functools
import math

import jax
import jax.numpy as jnp
from jax import lax
from jax.experimental import pallas as pl
from jax.experimental.pallas import tpu as pltpu
from jax.sharding import Mesh, PartitionSpec as P

ITERS = 3
BANDS = 8
SECTORS = 64
OBS = 512
RHS = 16

LAT_LIMIT = 80.0 * math.pi / 180.0
HORIZ_SQ = 0.05 * 0.05
VERT_SQ = 0.3 * 0.3
TAPER_STEP = 0.45
LOG2E = 1.0 / math.log(2.0)
HORIZ = LOG2E / HORIZ_SQ
VERT = LOG2E / (2.0 * VERT_SQ)
COUPLING = ((1.0, 0.45, 0.45), (0.45, 1.0, 0.25), (0.45, 0.25, 1.0))

LAT = ("z_lo", "x")
LON = ("z_hi", "y", "core")
GROUPS = (("z_lo", "z_hi", "x"), ("y", "core"))


def extent(axes):
    size = 1
    for axis in axes:
        size *= lax.axis_size(axis)
    return size


def swaps(count, first):
    pairs = []
    for low in range(first, count + first - 1, 2):
        high = (low + 1) % count
        pairs += [(low, high), (high, low)]
    return pairs


def widened(block):
    count = extent(LON)
    inner = lax.ppermute(block, LON, swaps(count, 0))
    outer = lax.ppermute(block, LON, swaps(count, 1))
    return jnp.stack([outer, block, inner])


def all_bands(wide):
    count = extent(LAT)
    below = lax.ppermute(wide, LAT, [(i, i + 1) for i in range(count - 1)])
    above = lax.ppermute(wide, LAT, [(i + 1, i) for i in range(count - 1)])
    return below, above


def rounded(value):
    return value.astype(jnp.bfloat16).astype(jnp.float32)


def pieces(value):
    high = rounded(value)
    mid = rounded(value - high)
    return high, mid, rounded(value - high - mid)


def describe_kernel(
    start_ref, error_ref, frac_ref, spread_ref, type_ref,
    message_ref, own_ref, error_out_ref, added_ref, far_rows, own_rows,
):
    frac = frac_ref[...].astype(jnp.float32)
    latitude = (lax.axis_index(LAT).astype(jnp.float32) + frac[0:1]) * (2.0 * LAT_LIMIT / BANDS) - LAT_LIMIT
    longitude = (lax.axis_index(LON).astype(jnp.float32) + frac[1:2]) * (2.0 * math.pi / SECTORS)
    angles = jnp.concatenate([latitude, longitude], axis=0)
    cosines, sines = jnp.cos(angles), jnp.sin(angles)
    place = (cosines[0:1] * cosines[1:2], cosines[0:1] * sines[1:2], sines[0:1])
    level = frac[2:3]
    sigma = jnp.log(spread_ref[...].astype(jnp.float32)) * LOG2E - VERT * level * level
    kind = type_ref[...]
    one = jnp.ones_like(level)
    table = [[math.log2(k) for k in row] for row in COUPLING]

    def looked_up(column):
        return jnp.where(kind == 0, table[0][column], jnp.where(kind == 1, table[1][column], table[2][column]))

    at_height = looked_up(0)
    far = []
    own = []
    for axis in place:
        far += pieces(axis)
        own += [HORIZ * axis] * 3
    far += [level, jnp.where(kind == 1, one, 0.0), jnp.where(kind == 2, one, 0.0)]
    own += [2.0 * VERT * level, looked_up(1) - at_height, looked_up(2) - at_height]
    far += [*pieces(sigma), one]
    own += [one, one, one, sigma + at_height - HORIZ]
    for row in range(16):
        far_rows[row : row + 1, :] = far[row]
        own_rows[row : row + 1, :] = own[row]
    message_ref[0:16, :] = start_ref[...].astype(jnp.bfloat16)
    message_ref[16:32, :] = far_rows[...].astype(jnp.bfloat16)
    error_out_ref[...] = error_ref[...]
    added_ref[...] = error_ref[...] * start_ref[...]
    for step in range(3):
        if step:
            own_rows[15:16, :] = own[15] + step * math.log2(TAPER_STEP)
        left = own_rows[...]
        for piece in range(3):
            part = left.astype(jnp.bfloat16)
            own_ref[step, 16 * piece : 16 * piece + 16, :] = part
            left = left - part.astype(jnp.float32)


def whole(space=pltpu.VMEM):
    return pl.BlockSpec(memory_space=space)


def describe(start, error_var, where_frac, spread, obs_type):
    return pl.pallas_call(
        describe_kernel,
        out_shape=(
            pltpu.VMEM((32, OBS), jnp.bfloat16),
            pltpu.VMEM((3, 48, OBS), jnp.bfloat16),
            pltpu.VMEM((1, OBS), jnp.float32),
            pltpu.VMEM((RHS, OBS), jnp.float32),
        ),
        in_specs=[whole()] * 5,
        out_specs=[whole()] * 4,
        scratch_shapes=[pltpu.VMEM((16, OBS), jnp.float32)] * 2,
        name="describe",
    )(start, error_var, where_frac, spread, obs_type)


CHUNK = 256


def build_kernel(steps, near_ref, own_ref, added_ref, tile_ref, sum_ref, *sent):
    total = added_ref[...]
    for slot, step in enumerate(steps):
        own = own_ref[step]
        for low in range(0, OBS, CHUNK):
            far = near_ref[slot, 16:32, low : low + CHUNK]
            far = jnp.concatenate([far, far, far], axis=0)
            power = lax.dot_general(far, own, (((0,), (0,)), ((), ())), preferred_element_type=jnp.float32)
            tile = jnp.exp2(power).astype(jnp.bfloat16)
            tile_ref[slot, low : low + CHUNK, :] = tile
            field = near_ref[slot, 0:16, low : low + CHUNK]
            total = total + jnp.dot(field, tile, preferred_element_type=jnp.float32)
    sum_ref[...] = total
    for ref in sent:
        ref[...] = total.astype(jnp.bfloat16)


def apply_kernel(scaled, near_ref, tile_ref, *refs):
    total = refs[0][...]
    if scaled:
        total = total * refs[1][...]
    for slot in range(3):
        total = total + jnp.dot(near_ref[slot], tile_ref[slot], preferred_element_type=jnp.float32)
    sum_ref, *sent = refs[1 + scaled :]
    sum_ref[...] = total
    for ref in sent:
        ref[...] = total.astype(jnp.bfloat16)


SAME_BAND = (1, 0, 1)
OTHER_BAND = (2, 1, 2)


def cost(built):
    entries = 3 * OBS * OBS
    return pl.CostEstimate(
        flops=2 * entries * (RHS + 256 * built),
        bytes_accessed=2 * entries,
        transcendentals=entries * built,
    )


def sums(last):
    shapes = [pltpu.VMEM((RHS, OBS), jnp.float32)]
    if last:
        shapes.append(pltpu.VMEM((RHS, OBS), jnp.bfloat16))
    return shapes


def build(steps, near, own, added, last=False):
    shapes = [pltpu.VMEM((3, OBS, OBS), jnp.bfloat16)] + sums(last)
    return pl.pallas_call(
        functools.partial(build_kernel, steps),
        out_shape=shapes,
        in_specs=[whole()] * 3,
        out_specs=[whole()] * len(shapes),
        compiler_params=pltpu.CompilerParams(vmem_limit_bytes=16 << 20),
        cost_estimate=cost(1),
        name="build",
    )(near, own, added)


def apply(near, tiles, added, scale=None, last=False):
    shapes = sums(last)
    scales = [] if scale is None else [scale]
    return pl.pallas_call(
        functools.partial(apply_kernel, len(scales)),
        out_shape=shapes,
        in_specs=[whole()] * (3 + len(scales)),
        out_specs=[whole()] * len(shapes),
        compiler_params=pltpu.CompilerParams(vmem_limit_bytes=16 << 20),
        cost_estimate=cost(0),
        name="apply",
    )(near, tiles, added, *scales)


def local(innovations, obs_error, where_frac, spread, obs_type):
    start = innovations[0, 0]
    message, own, error_var, added = describe(start, obs_error[0], where_frac[0, 0], spread[0], obs_type[0])
    wide = widened(message)
    below, above = all_bands(wide)
    tiles, part = build(SAME_BAND, wide, own, added)
    tiles_below, part = build(OTHER_BAND, below, own, part)
    tiles_above, first, sent = build(OTHER_BAND, above, own, part, True)
    wide = widened(sent)
    below, above = all_bands(wide)
    part, = apply(wide, tiles, first, error_var)
    part, = apply(below, tiles_below, part)
    second, sent = apply(above, tiles_above, part, last=True)
    wide = widened(sent)
    below, above = all_bands(wide)
    part, = apply(wide, tiles, second, error_var)
    lower, = apply(below, tiles_below, part)
    basis = [start, first, second]
    products = [start * start, start * first, first * first, start * second, first * second, second * second]
    products.append(second * (2.0 * lower - part))
    parts = [jnp.sum(product, axis=1) for product in products]
    parts.append(jnp.zeros_like(parts[0]))
    totals = global_sum(jnp.concatenate(parts).reshape(1, 128)).reshape(8, 16)
    third, = apply(above, tiles_above, lower)
    basis.append(third)
    names = {(0, 0): 0, (0, 1): 1, (1, 1): 2, (0, 2): 3, (1, 2): 4, (2, 2): 5, (2, 3): 6, (0, 3): 4, (1, 3): 5}
    gram = {pair: totals[at] for pair, at in names.items()}
    answer, residual = coefficients(gram)
    answer = sum(c[:, None] * v for c, v in zip(answer, basis))
    residual = sum(c[:, None] * v for c, v in zip(residual, basis))
    return (answer[None, None], residual[None, None])


def global_sum(value):
    for axes in GROUPS:
        count = extent(axes)
        spread_out = jnp.broadcast_to(value, (count,) + value.shape)
        value = jnp.sum(lax.all_to_all(spread_out, axes, 0, 0), axis=0)
    return value


def coefficients(gram):
    def inner(left, right):
        total = 0.0
        for i in range(4):
            for j in range(4):
                if left[i] is not None and right[j] is not None:
                    total = total + left[i] * right[j] * gram[min(i, j), max(i, j)]
        return total

    def axpy(scale, added, start):
        out = []
        for a, s in zip(added, start):
            if a is None:
                out.append(s)
            else:
                out.append(scale * a if s is None else s + scale * a)
        return out

    one = jnp.ones_like(gram[0, 0])
    answer = [None] * 4
    residual = [one, None, None, None]
    direction = residual
    norm_now = gram[0, 0]
    for iteration in range(ITERS):
        image = [None] + direction[:3]
        step_len = norm_now / inner(direction, image)
        answer = axpy(step_len, direction, answer)
        residual = axpy(-step_len, image, residual)
        if iteration < ITERS - 1:
            norm_next = inner(residual, residual)
            direction = axpy(norm_next / norm_now, direction, residual)
            norm_now = norm_next
    return answer[:3], residual


def solution(mesh):
    fine = Mesh(mesh.devices.reshape(2, 4, 4, 8, 2), LAT + LON)
    in_specs = (
        P(LAT, LON, None, None),
        P(LAT, LON, None),
        P(LAT, LON, None, None),
        P(LAT, LON, None),
        P(LAT, LON, None),
    )
    out_specs = (P(LAT, LON, None, None), P(LAT, LON, None, None))
    return jax.shard_map(local, mesh=fine, in_specs=in_specs, out_specs=out_specs, check_vma=False)
```

```python
import functools
import math

import jax
import jax.numpy as jnp
from jax import lax
from jax.experimental import pallas as pl
from jax.experimental.pallas import tpu as pltpu
from jax.sharding import Mesh, PartitionSpec as P

ITERS = 3
BANDS = 8
SECTORS = 64
OBS = 512
RHS = 16

LAT_LIMIT = 80.0 * math.pi / 180.0
HORIZ_SQ = 0.05 * 0.05
VERT_SQ = 0.3 * 0.3
TAPER_STEP = 0.45
LOG2E = 1.0 / math.log(2.0)
HORIZ = LOG2E / HORIZ_SQ
VERT = LOG2E / (2.0 * VERT_SQ)
COUPLING = ((1.0, 0.45, 0.45), (0.45, 1.0, 0.25), (0.45, 0.25, 1.0))

LAT = ("z_lo", "x")
LON = ("z_hi", "y", "core")
GROUPS = (("z_lo", "z_hi", "x"), ("y", "core"))


def extent(axes):
    size = 1
    for axis in axes:
        size *= lax.axis_size(axis)
    return size


def pairs(count, first):
    return [[low, (low + 1) % count] for low in range(first, count, 2)]


def partner(block, axes, first):
    both = lax.all_gather(block, axes, axis_index_groups=pairs(extent(axes), first))
    leads = lax.axis_index(axes) % 2 == first
    return jnp.where(leads, both[1], both[0])


def widened(block):
    inner = partner(block, LON, 0)
    inner, block = lax.optimization_barrier((inner, block))
    outer = partner(block, LON, 1)
    return jnp.stack([outer, block, inner])


def all_bands(wide):
    count = extent(LAT)
    below = lax.ppermute(wide, LAT, [(i, i + 1) for i in range(count - 1)])
    above = lax.ppermute(wide, LAT, [(i + 1, i) for i in range(count - 1)])
    return below, above


def all_bands_paired(wide):
    count = extent(LAT)
    band = lax.axis_index(LAT)
    inner = lax.ppermute(wide, LAT, [p for a, b in pairs(count, 0) for p in ((a, b), (b, a))])
    outer = partner(wide, LAT, 1)
    outer = jnp.where((band == 0) | (band == count - 1), jnp.zeros_like(outer), outer)
    odd = band % 2 == 1
    return jnp.where(odd, inner, outer), jnp.where(odd, outer, inner)


def rounded(value):
    return value.astype(jnp.bfloat16).astype(jnp.float32)


def pieces(value):
    high = rounded(value)
    mid = rounded(value - high)
    return high, mid, rounded(value - high - mid)


def describe_kernel(
    start_ref, error_ref, frac_ref, spread_ref, type_ref,
    message_ref, own_ref, error_out_ref, added_ref, kept_ref, far_rows, own_rows,
):
    frac = frac_ref[...].astype(jnp.float32)
    latitude = (lax.axis_index(LAT).astype(jnp.float32) + frac[0:1]) * (2.0 * LAT_LIMIT / BANDS) - LAT_LIMIT
    longitude = (lax.axis_index(LON).astype(jnp.float32) + frac[1:2]) * (2.0 * math.pi / SECTORS)
    angles = jnp.concatenate([latitude, longitude], axis=0)
    cosines, sines = jnp.cos(angles), jnp.sin(angles)
    place = (cosines[0:1] * cosines[1:2], cosines[0:1] * sines[1:2], sines[0:1])
    level = frac[2:3]
    sigma = jnp.log(spread_ref[...].astype(jnp.float32)) * LOG2E - VERT * level * level
    kind = type_ref[...]
    one = jnp.ones_like(level)
    table = [[math.log2(k) for k in row] for row in COUPLING]

    def looked_up(column):
        return jnp.where(kind == 0, table[0][column], jnp.where(kind == 1, table[1][column], table[2][column]))

    at_height = looked_up(0)
    far = []
    own = []
    for axis in place:
        far += pieces(axis)
        own += [HORIZ * axis] * 3
    far += [level, jnp.where(kind == 1, one, 0.0), jnp.where(kind == 2, one, 0.0)]
    own += [2.0 * VERT * level, looked_up(1) - at_height, looked_up(2) - at_height]
    far += [*pieces(sigma), one]
    own += [one, one, one, sigma + at_height - HORIZ]
    for row in range(16):
        far_rows[row : row + 1, :] = far[row]
        own_rows[row : row + 1, :] = own[row]
    message_ref[0:16, :] = start_ref[...].astype(jnp.bfloat16)
    message_ref[16:32, :] = far_rows[...].astype(jnp.bfloat16)
    error_out_ref[...] = error_ref[...]
    kept_ref[...] = start_ref[...]
    added_ref[...] = error_ref[...] * start_ref[...]
    for step in range(3):
        if step:
            own_rows[15:16, :] = own[15] + step * math.log2(TAPER_STEP)
        left = own_rows[...]
        for piece in range(3):
            part = left.astype(jnp.bfloat16)
            own_ref[step, 16 * piece : 16 * piece + 16, :] = part
            left = left - part.astype(jnp.float32)


def whole(space=pltpu.VMEM):
    return pl.BlockSpec(memory_space=space)


def describe(start, error_var, where_frac, spread, obs_type):
    return pl.pallas_call(
        describe_kernel,
        out_shape=(
            pltpu.VMEM((32, OBS), jnp.bfloat16),
            pltpu.VMEM((3, 48, OBS), jnp.bfloat16),
            pltpu.VMEM((1, OBS), jnp.float32),
            pltpu.VMEM((RHS, OBS), jnp.float32),
            pltpu.VMEM((RHS, OBS), jnp.float32),
        ),
        in_specs=[whole()] * 5,
        out_specs=[whole()] * 5,
        scratch_shapes=[pltpu.VMEM((16, OBS), jnp.float32)] * 2,
        name="describe",
    )(start, error_var, where_frac, spread, obs_type)


CHUNK = 256


def build_kernel(steps, near_ref, own_ref, added_ref, tile_ref, sum_ref, *sent):
    total = added_ref[...]
    for slot, step in enumerate(steps):
        own = own_ref[step]
        for low in range(0, OBS, CHUNK):
            far = near_ref[slot, 16:32, low : low + CHUNK]
            far = jnp.concatenate([far, far, far], axis=0)
            power = lax.dot_general(far, own, (((0,), (0,)), ((), ())), preferred_element_type=jnp.float32)
            tile = jnp.exp2(power).astype(jnp.bfloat16)
            tile_ref[slot, low : low + CHUNK, :] = tile
            field = near_ref[slot, 0:16, low : low + CHUNK]
            total = total + jnp.dot(field, tile, preferred_element_type=jnp.float32)
    sum_ref[...] = total
    for ref in sent:
        ref[...] = total.astype(jnp.bfloat16)


def apply_kernel(scaled, near_ref, tile_ref, *refs):
    total = refs[0][...]
    if scaled:
        total = total * refs[1][...]
    for slot in range(3):
        total = total + jnp.dot(near_ref[slot], tile_ref[slot], preferred_element_type=jnp.float32)
    sum_ref, *sent = refs[1 + scaled :]
    sum_ref[...] = total
    for ref in sent:
        ref[...] = total.astype(jnp.bfloat16)


SAME_BAND = (1, 0, 1)
OTHER_BAND = (2, 1, 2)


def cost(built):
    entries = 3 * OBS * OBS
    return pl.CostEstimate(
        flops=2 * entries * (RHS + 256 * built),
        bytes_accessed=2 * entries,
        transcendentals=entries * built,
    )


def sums(last):
    shapes = [pltpu.VMEM((RHS, OBS), jnp.float32)]
    if last:
        shapes.append(pltpu.VMEM((RHS, OBS), jnp.bfloat16))
    return shapes


def build(steps, near, own, added, last=False):
    shapes = [pltpu.VMEM((3, OBS, OBS), jnp.bfloat16)] + sums(last)
    return pl.pallas_call(
        functools.partial(build_kernel, steps),
        out_shape=shapes,
        in_specs=[whole()] * 3,
        out_specs=[whole()] * len(shapes),
        compiler_params=pltpu.CompilerParams(vmem_limit_bytes=16 << 20),
        cost_estimate=cost(1),
        name="build",
    )(near, own, added)


def apply(near, tiles, added, scale=None, last=False):
    shapes = sums(last)
    scales = [] if scale is None else [scale]
    return pl.pallas_call(
        functools.partial(apply_kernel, len(scales)),
        out_shape=shapes,
        in_specs=[whole()] * (3 + len(scales)),
        out_specs=[whole()] * len(shapes),
        compiler_params=pltpu.CompilerParams(vmem_limit_bytes=16 << 20),
        cost_estimate=cost(0),
        name="apply",
    )(near, tiles, added, *scales)


def coefficients(gram):
    def inner(left, right):
        total = 0.0
        for i in range(4):
            for j in range(4):
                if left[i] is not None and right[j] is not None:
                    total = total + left[i] * right[j] * gram[min(i, j), max(i, j)]
        return total

    def axpy(scale, added, start):
        out = []
        for a, s in zip(added, start):
            if a is None:
                out.append(s)
            else:
                out.append(scale * a if s is None else s + scale * a)
        return out

    one = jnp.ones_like(gram[0, 0])
    answer = [None] * 4
    residual = [one, None, None, None]
    direction = residual
    norm_now = gram[0, 0]
    for iteration in range(ITERS):
        image = [None] + direction[:3]
        step_len = norm_now / inner(direction, image)
        answer = axpy(step_len, direction, answer)
        residual = axpy(-step_len, image, residual)
        if iteration < ITERS - 1:
            norm_next = inner(residual, residual)
            direction = axpy(norm_next / norm_now, direction, residual)
            norm_now = norm_next
    return answer[:3], residual


def lane_sums(products):
    empty = jnp.zeros((128 - RHS * len(products), OBS), jnp.float32)
    stacked = jnp.concatenate([*products, empty], axis=0) if len(products) < 8 else jnp.concatenate(products, axis=0)
    ones = jnp.ones((8, OBS), jnp.bfloat16)
    total = 0.0
    for part in pieces(stacked):
        total = total + lax.dot_general(
            ones, part.astype(jnp.bfloat16), (((1,), (1,)), ((), ())), preferred_element_type=jnp.float32
        )
    return total[0:1]


MOMENTS = 6


def same_band_kernel(near_ref, tile_ref, second_ref, scale_ref, start_ref, first_ref, sum_ref, row_ref):
    start, first, second = start_ref[...], first_ref[...], second_ref[...]
    total = second * scale_ref[...]
    for slot in range(3):
        total = total + jnp.dot(near_ref[slot], tile_ref[slot], preferred_element_type=jnp.float32)
    sum_ref[...] = total
    row_ref[...] = lane_sums(
        [start * start, start * first, first * first, start * second, first * second, second * second]
    )


def below_kernel(near_ref, tile_ref, part_ref, second_ref, row_ref, sum_ref, copies_ref):
    part = part_ref[...]
    total = part
    for slot in range(3):
        total = total + jnp.dot(near_ref[slot], tile_ref[slot], preferred_element_type=jnp.float32)
    sum_ref[...] = total
    product = second_ref[...] * (2.0 * total - part)
    before = [jnp.zeros_like(product)] * MOMENTS
    row = row_ref[...] + lane_sums([*before, product])
    copies_ref[...] = jnp.broadcast_to(row[None], copies_ref.shape)


def finish_kernel(
    total_ref, near_ref, tile_ref, lower_ref, start_ref, first_ref, second_ref, answer_ref, residual_ref
):
    totals = jnp.broadcast_to(jnp.sum(total_ref[...], axis=0), (RHS, 128))
    lane = lax.broadcasted_iota(jnp.int32, (RHS, 128), 1)
    row = lax.broadcasted_iota(jnp.int32, (RHS, 128), 0)
    moments = [
        jnp.sum(jnp.where(lane == row + RHS * at, totals, 0.0), axis=1, keepdims=True) for at in range(MOMENTS + 1)
    ]
    names = {(0, 0): 0, (0, 1): 1, (1, 1): 2, (0, 2): 3, (1, 2): 4, (2, 2): 5, (2, 3): 6, (0, 3): 4, (1, 3): 5}
    answer, residual = coefficients({pair: moments[at] for pair, at in names.items()})
    third = lower_ref[...]
    for slot in range(3):
        third = third + jnp.dot(near_ref[slot], tile_ref[slot], preferred_element_type=jnp.float32)
    basis = (start_ref[...], first_ref[...], second_ref[...], third)
    answer_ref[0, 0] = sum(c * v for c, v in zip(answer, basis))
    residual_ref[0, 0] = sum(c * v for c, v in zip(residual, basis))


def call(kernel, shapes, operands, name):
    return pl.pallas_call(
        kernel,
        out_shape=shapes,
        in_specs=[whole()] * len(operands),
        out_specs=[whole()] * len(shapes),
        compiler_params=pltpu.CompilerParams(vmem_limit_bytes=16 << 20),
        cost_estimate=cost(0),
        name=name,
    )(*operands)


def global_sum(copies):
    for at, axes in enumerate(GROUPS):
        if at:
            copies = jnp.broadcast_to(jnp.sum(copies, axis=0), (extent(axes),) + copies.shape[1:])
        copies = lax.all_to_all(copies, axes, 0, 0)
    return copies


def local(innovations, obs_error, where_frac, spread, obs_type):
    message, own, error_var, added, start = describe(
        innovations[0, 0], obs_error[0], where_frac[0, 0], spread[0], obs_type[0]
    )
    wide = widened(message)
    below, above = all_bands(wide)
    tiles, part = build(SAME_BAND, wide, own, added)
    tiles_below, part = build(OTHER_BAND, below, own, part)
    tiles_above, first, sent = build(OTHER_BAND, above, own, part, True)
    wide = widened(sent)
    below, above = all_bands_paired(wide)
    part, = apply(wide, tiles, first, error_var)
    part, = apply(below, tiles_below, part)
    second, sent = apply(above, tiles_above, part, last=True)
    wide = widened(sent)
    below, above = all_bands(wide)
    field = pltpu.VMEM((RHS, OBS), jnp.float32)
    part, row = call(
        same_band_kernel,
        [field, pltpu.VMEM((1, 128), jnp.float32)],
        [wide, tiles, second, error_var, start, first],
        "same_band",
    )
    copies = pltpu.VMEM((extent(GROUPS[0]), 1, 128), jnp.float32)
    lower, copies = call(below_kernel, [field, copies], [below, tiles_below, part, second, row], "below")
    totals = global_sum(copies)
    whole_field = jax.ShapeDtypeStruct((1, 1, RHS, OBS), jnp.float32)
    return call(
        finish_kernel,
        [whole_field] * 2,
        [totals, above, tiles_above, lower, start, first, second],
        "finish",
    )


def solution(mesh):
    fine = Mesh(mesh.devices.reshape(2, 4, 4, 8, 2), LAT + LON)
    in_specs = (
        P(LAT, LON, None, None),
        P(LAT, LON, None),
        P(LAT, LON, None, None),
        P(LAT, LON, None),
        P(LAT, LON, None),
    )
    out_specs = (P(LAT, LON, None, None), P(LAT, LON, None, None))
    return jax.shard_map(local, mesh=fine, in_specs=in_specs, out_specs=out_specs, check_vma=False)
```

```python
import functools
import math

import jax
import jax.numpy as jnp
from jax import lax
from jax.experimental import pallas as pl
from jax.experimental.pallas import tpu as pltpu
from jax.sharding import Mesh, PartitionSpec as P

ITERS = 3
BANDS = 8
SECTORS = 64
OBS = 512
RHS = 16

LAT_LIMIT = 80.0 * math.pi / 180.0
HORIZ_SQ = 0.05 * 0.05
VERT_SQ = 0.3 * 0.3
TAPER_STEP = 0.45
LOG2E = 1.0 / math.log(2.0)
HORIZ = LOG2E / HORIZ_SQ
VERT = LOG2E / (2.0 * VERT_SQ)
COUPLING = ((1.0, 0.45, 0.45), (0.45, 1.0, 0.25), (0.45, 0.25, 1.0))

LAT = ("z_lo", "x")
LON = ("z_hi", "y", "core")
GROUPS = (("z_lo", "z_hi", "x"), ("y", "core"))


def extent(axes):
    size = 1
    for axis in axes:
        size *= lax.axis_size(axis)
    return size


def pairs(count, first):
    return [[low, (low + 1) % count] for low in range(first, count, 2)]


def partner(block, axes, first):
    both = lax.all_gather(block, axes, axis_index_groups=pairs(extent(axes), first))
    leads = lax.axis_index(axes) % 2 == first
    return jnp.where(leads, both[1], both[0])


def widened(block):
    inner = partner(block, LON, 0)
    inner, block = lax.optimization_barrier((inner, block))
    outer = partner(block, LON, 1)
    return jnp.stack([outer, block, inner])


def all_bands(wide):
    count = extent(LAT)
    below = lax.ppermute(wide, LAT, [(i, i + 1) for i in range(count - 1)])
    above = lax.ppermute(wide, LAT, [(i + 1, i) for i in range(count - 1)])
    return below, above


def all_bands_paired(wide):
    count = extent(LAT)
    swap = lax.ppermute(wide, LAT, [p for a, b in pairs(count, 0) for p in ((a, b), (b, a))])
    return swap, lax.all_gather(wide, LAT, axis_index_groups=pairs(count, 1))


def rounded(value):
    return value.astype(jnp.bfloat16).astype(jnp.float32)


def pieces(value):
    high = rounded(value)
    mid = rounded(value - high)
    return high, mid, rounded(value - high - mid)


def describe_kernel(
    start_ref, error_ref, frac_ref, spread_ref, type_ref,
    message_ref, own_ref, error_out_ref, added_ref, kept_ref, far_rows, own_rows,
):
    frac = frac_ref[...].astype(jnp.float32)
    latitude = (lax.axis_index(LAT).astype(jnp.float32) + frac[0:1]) * (2.0 * LAT_LIMIT / BANDS) - LAT_LIMIT
    longitude = (lax.axis_index(LON).astype(jnp.float32) + frac[1:2]) * (2.0 * math.pi / SECTORS)
    angles = jnp.concatenate([latitude, longitude], axis=0)
    cosines, sines = jnp.cos(angles), jnp.sin(angles)
    place = (cosines[0:1] * cosines[1:2], cosines[0:1] * sines[1:2], sines[0:1])
    level = frac[2:3]
    sigma = jnp.log(spread_ref[...].astype(jnp.float32)) * LOG2E - VERT * level * level
    kind = type_ref[...]
    one = jnp.ones_like(level)
    table = [[math.log2(k) for k in row] for row in COUPLING]

    def looked_up(column):
        return jnp.where(kind == 0, table[0][column], jnp.where(kind == 1, table[1][column], table[2][column]))

    at_height = looked_up(0)
    far = []
    own = []
    for axis in place:
        far += pieces(axis)
        own += [HORIZ * axis] * 3
    far += [level, jnp.where(kind == 1, one, 0.0), jnp.where(kind == 2, one, 0.0)]
    own += [2.0 * VERT * level, looked_up(1) - at_height, looked_up(2) - at_height]
    far += [*pieces(sigma), one]
    own += [one, one, one, sigma + at_height - HORIZ]
    for row in range(16):
        far_rows[row : row + 1, :] = far[row]
        own_rows[row : row + 1, :] = own[row]
    message_ref[0:16, :] = start_ref[...].astype(jnp.bfloat16)
    message_ref[16:32, :] = far_rows[...].astype(jnp.bfloat16)
    error_out_ref[...] = error_ref[...]
    kept_ref[...] = start_ref[...]
    added_ref[...] = error_ref[...] * start_ref[...]
    for step in range(3):
        if step:
            own_rows[15:16, :] = own[15] + step * math.log2(TAPER_STEP)
        left = own_rows[...]
        for piece in range(3):
            part = left.astype(jnp.bfloat16)
            own_ref[step, 16 * piece : 16 * piece + 16, :] = part
            left = left - part.astype(jnp.float32)


def whole(space=pltpu.VMEM):
    return pl.BlockSpec(memory_space=space)


def describe(start, error_var, where_frac, spread, obs_type):
    return pl.pallas_call(
        describe_kernel,
        out_shape=(
            pltpu.VMEM((32, OBS), jnp.bfloat16),
            pltpu.VMEM((3, 48, OBS), jnp.bfloat16),
            pltpu.VMEM((1, OBS), jnp.float32),
            pltpu.VMEM((RHS, OBS), jnp.float32),
            pltpu.VMEM((RHS, OBS), jnp.float32),
        ),
        in_specs=[whole()] * 5,
        out_specs=[whole()] * 5,
        scratch_shapes=[pltpu.VMEM((16, OBS), jnp.float32)] * 2,
        name="describe",
    )(start, error_var, where_frac, spread, obs_type)


def build_kernel(steps, near_ref, own_ref, added_ref, tile_ref, sum_ref, *sent):
    for slot, step in enumerate(steps):
        far = near_ref[slot, 16:32, :]
        far = jnp.concatenate([far, far, far], axis=0)
        power = lax.dot_general(far, own_ref[step], (((0,), (0,)), ((), ())), preferred_element_type=jnp.float32)
        tile_ref[slot] = jnp.exp2(power).astype(jnp.bfloat16)
    total = added_ref[...] + products(lambda slot: near_ref[slot, 0:16, :], tile_ref)
    sum_ref[...] = total
    for ref in sent:
        ref[...] = total.astype(jnp.bfloat16)


def products(field_of, tile_ref):
    return sum(jnp.dot(field_of(slot), tile_ref[slot], preferred_element_type=jnp.float32) for slot in range(3))


def apply_kernel(scaled, near_ref, tile_ref, *refs):
    total = refs[0][...]
    if scaled:
        total = total * refs[1][...]
    total = total + products(lambda slot: near_ref[slot], tile_ref)
    sum_ref, *sent = refs[1 + scaled :]
    sum_ref[...] = total
    for ref in sent:
        ref[...] = total.astype(jnp.bfloat16)


SAME_BAND = (1, 0, 1)
OTHER_BAND = (2, 1, 2)


def cost(built):
    entries = 3 * OBS * OBS
    return pl.CostEstimate(
        flops=2 * entries * (RHS + 256 * built),
        bytes_accessed=2 * entries,
        transcendentals=entries * built,
    )


def sums(last):
    shapes = [pltpu.VMEM((RHS, OBS), jnp.float32)]
    if last:
        shapes.append(pltpu.VMEM((RHS, OBS), jnp.bfloat16))
    return shapes


def build(steps, near, own, added, last=False):
    shapes = [pltpu.VMEM((3, OBS, OBS), jnp.bfloat16)] + sums(last)
    return pl.pallas_call(
        functools.partial(build_kernel, steps),
        out_shape=shapes,
        in_specs=[whole()] * 3,
        out_specs=[whole()] * len(shapes),
        compiler_params=pltpu.CompilerParams(vmem_limit_bytes=16 << 20),
        cost_estimate=cost(1),
        name="build",
    )(near, own, added)


def apply(near, tiles, added, scale=None, last=False):
    shapes = sums(last)
    scales = [] if scale is None else [scale]
    return pl.pallas_call(
        functools.partial(apply_kernel, len(scales)),
        out_shape=shapes,
        in_specs=[whole()] * (3 + len(scales)),
        out_specs=[whole()] * len(shapes),
        compiler_params=pltpu.CompilerParams(vmem_limit_bytes=16 << 20),
        cost_estimate=cost(0),
        name="apply",
    )(near, tiles, added, *scales)


def coefficients(gram):
    def inner(left, right):
        total = 0.0
        for i in range(4):
            for j in range(4):
                if left[i] is not None and right[j] is not None:
                    total = total + left[i] * right[j] * gram[min(i, j), max(i, j)]
        return total

    def axpy(scale, added, start):
        out = []
        for a, s in zip(added, start):
            if a is None:
                out.append(s)
            else:
                out.append(scale * a if s is None else s + scale * a)
        return out

    one = jnp.ones_like(gram[0, 0])
    answer = [None] * 4
    residual = [one, None, None, None]
    direction = residual
    norm_now = gram[0, 0]
    for iteration in range(ITERS):
        image = [None] + direction[:3]
        step_len = norm_now / inner(direction, image)
        answer = axpy(step_len, direction, answer)
        residual = axpy(-step_len, image, residual)
        if iteration < ITERS - 1:
            norm_next = inner(residual, residual)
            direction = axpy(norm_next / norm_now, direction, residual)
            norm_now = norm_next
    return answer[:3], residual


def lane_sums(products):
    empty = jnp.zeros((128 - RHS * len(products), OBS), jnp.float32)
    stacked = jnp.concatenate([*products, empty], axis=0) if len(products) < 8 else jnp.concatenate(products, axis=0)
    ones = jnp.ones((8, OBS), jnp.bfloat16)
    total = 0.0
    for part in pieces(stacked):
        total = total + lax.dot_general(
            ones, part.astype(jnp.bfloat16), (((1,), (1,)), ((), ())), preferred_element_type=jnp.float32
        )
    return total[0:1]


MOMENTS = 6


def same_band_kernel(near_ref, tile_ref, second_ref, scale_ref, start_ref, first_ref, sum_ref, row_ref):
    start, first, second = start_ref[...], first_ref[...], second_ref[...]
    sum_ref[...] = second * scale_ref[...] + products(lambda slot: near_ref[slot], tile_ref)
    row_ref[...] = lane_sums(
        [start * start, start * first, first * first, start * second, first * second, second * second]
    )


def below_kernel(near_ref, tile_ref, part_ref, second_ref, row_ref, sum_ref, copies_ref):
    part = part_ref[...]
    total = part + products(lambda slot: near_ref[slot], tile_ref)
    sum_ref[...] = total
    product = second_ref[...] * (2.0 * total - part)
    before = [jnp.zeros_like(product)] * MOMENTS
    row = row_ref[...] + lane_sums([*before, product])
    copies_ref[...] = jnp.broadcast_to(row[None], copies_ref.shape)


def paired_kernel(swap_ref, both_ref, below_ref, above_ref, part_ref, sum_ref, sent_ref):
    band = lax.axis_index(LAT)
    inside = jnp.where((band == 0) | (band == BANDS - 1), 0.0, 1.0)

    def add(swap_tiles, both_tiles, position):
        total = part_ref[...] + products(lambda slot: swap_ref[slot], swap_tiles)
        total = total + inside * products(lambda slot: both_ref[position, slot], both_tiles)
        sum_ref[...] = total
        sent_ref[...] = total.astype(jnp.bfloat16)

    @pl.when(band % 2 == 1)
    def _():
        add(below_ref, above_ref, 1)

    @pl.when(band % 2 == 0)
    def _():
        add(above_ref, below_ref, 0)


def above_kernel(near_ref, total_ref, tile_ref, lower_ref, third_ref, copies_ref):
    third_ref[...] = lower_ref[...] + products(lambda slot: near_ref[slot], tile_ref)
    copies_ref[...] = jnp.broadcast_to(jnp.sum(total_ref[...], axis=0)[None], copies_ref.shape)


def finish_kernel(total_ref, start_ref, first_ref, second_ref, third_ref, answer_ref, residual_ref):
    totals = jnp.broadcast_to(jnp.sum(total_ref[...], axis=0), (RHS, 128))
    lane = lax.broadcasted_iota(jnp.int32, (RHS, 128), 1)
    row = lax.broadcasted_iota(jnp.int32, (RHS, 128), 0)
    moments = [
        jnp.sum(jnp.where(lane == row + RHS * at, totals, 0.0), axis=1, keepdims=True) for at in range(MOMENTS + 1)
    ]
    names = {(0, 0): 0, (0, 1): 1, (1, 1): 2, (0, 2): 3, (1, 2): 4, (2, 2): 5, (2, 3): 6, (0, 3): 4, (1, 3): 5}
    answer, residual = coefficients({pair: moments[at] for pair, at in names.items()})
    basis = (start_ref[...], first_ref[...], second_ref[...], third_ref[...])
    answer_ref[0, 0] = sum(c * v for c, v in zip(answer, basis))
    residual_ref[0, 0] = sum(c * v for c, v in zip(residual, basis))


def call(kernel, shapes, operands, name):
    return pl.pallas_call(
        kernel,
        out_shape=shapes,
        in_specs=[whole()] * len(operands),
        out_specs=[whole()] * len(shapes),
        compiler_params=pltpu.CompilerParams(vmem_limit_bytes=16 << 20),
        cost_estimate=cost(0),
        name=name,
    )(*operands)


def local(innovations, obs_error, where_frac, spread, obs_type):
    message, own, error_var, added, start = describe(
        innovations[0, 0], obs_error[0], where_frac[0, 0], spread[0], obs_type[0]
    )
    wide = widened(message)
    below, above = all_bands(wide)
    tiles, part = build(SAME_BAND, wide, own, added)
    tiles_below, part = build(OTHER_BAND, below, own, part)
    tiles_above, first, sent = build(OTHER_BAND, above, own, part, True)
    wide = widened(sent)
    swap, both = all_bands_paired(wide)
    part, = apply(wide, tiles, first, error_var)
    field = pltpu.VMEM((RHS, OBS), jnp.float32)
    second, sent = call(
        paired_kernel,
        [field, pltpu.VMEM((RHS, OBS), jnp.bfloat16)],
        [swap, both, tiles_below, tiles_above, part],
        "paired",
    )
    wide = widened(sent)
    below, above = all_bands(wide)
    part, row = call(
        same_band_kernel,
        [field, pltpu.VMEM((1, 128), jnp.float32)],
        [wide, tiles, second, error_var, start, first],
        "same_band",
    )
    copies = [pltpu.VMEM((extent(axes), 1, 128), jnp.float32) for axes in GROUPS]
    lower, partial = call(below_kernel, [field, copies[0]], [below, tiles_below, part, second, row], "below")
    partial = lax.all_to_all(partial, GROUPS[0], 0, 0)
    third, partial = call(above_kernel, [field, copies[1]], [above, partial, tiles_above, lower], "above")
    totals = lax.all_to_all(partial, GROUPS[1], 0, 0)
    whole_field = jax.ShapeDtypeStruct((1, 1, RHS, OBS), jnp.float32)
    return call(finish_kernel, [whole_field] * 2, [totals, start, first, second, third], "finish")


def solution(mesh):
    fine = Mesh(mesh.devices.reshape(2, 4, 4, 8, 2), LAT + LON)
    in_specs = (
        P(LAT, LON, None, None),
        P(LAT, LON, None),
        P(LAT, LON, None, None),
        P(LAT, LON, None),
        P(LAT, LON, None),
    )
    out_specs = (P(LAT, LON, None, None), P(LAT, LON, None, None))
    return jax.shard_map(local, mesh=fine, in_specs=in_specs, out_specs=out_specs, check_vma=False)
```

```python
import functools
import math

import jax
import jax.numpy as jnp
from jax import lax
from jax.experimental import pallas as pl
from jax.experimental.pallas import tpu as pltpu
from jax.sharding import Mesh, PartitionSpec as P

ITERS = 3
BANDS = 8
SECTORS = 64
OBS = 512
RHS = 16

LAT_LIMIT = 80.0 * math.pi / 180.0
HORIZ_SQ = 0.05 * 0.05
VERT_SQ = 0.3 * 0.3
TAPER_STEP = 0.45
LOG2E = 1.0 / math.log(2.0)
HORIZ = LOG2E / HORIZ_SQ
VERT = LOG2E / (2.0 * VERT_SQ)
COUPLING = ((1.0, 0.45, 0.45), (0.45, 1.0, 0.25), (0.45, 0.25, 1.0))

LAT = ("z_lo", "x")
LON = ("z_hi", "y", "core")
GROUPS = (("z_lo", "z_hi", "x"), ("y", "core"))


def extent(axes):
    size = 1
    for axis in axes:
        size *= lax.axis_size(axis)
    return size


def pairs(count, first):
    return [[low, (low + 1) % count] for low in range(first, count, 2)]


def partner(block, axes, first):
    both = lax.all_gather(block, axes, axis_index_groups=pairs(extent(axes), first))
    leads = lax.axis_index(axes) % 2 == first
    return jnp.where(leads, both[1], both[0])


def widened(block):
    inner = partner(block, LON, 0)
    inner, block = lax.optimization_barrier((inner, block))
    outer = partner(block, LON, 1)
    return jnp.stack([outer, block, inner])


def all_bands(wide):
    count = extent(LAT)
    below = lax.ppermute(wide, LAT, [(i, i + 1) for i in range(count - 1)])
    above = lax.ppermute(wide, LAT, [(i + 1, i) for i in range(count - 1)])
    return below, above


def all_bands_paired(wide):
    count = extent(LAT)
    swap = lax.ppermute(wide, LAT, [p for a, b in pairs(count, 0) for p in ((a, b), (b, a))])
    return swap, lax.all_gather(wide, LAT, axis_index_groups=pairs(count, 1))


def rounded(value):
    return value.astype(jnp.bfloat16).astype(jnp.float32)


def pieces(value):
    high = rounded(value)
    mid = rounded(value - high)
    return high, mid, rounded(value - high - mid)


def describe_kernel(
    start_ref, error_ref, frac_ref, spread_ref, type_ref,
    message_ref, own_ref, error_out_ref, added_ref, kept_ref, far_rows, own_rows,
):
    frac = frac_ref[...].astype(jnp.float32)
    latitude = (lax.axis_index(LAT).astype(jnp.float32) + frac[0:1]) * (2.0 * LAT_LIMIT / BANDS) - LAT_LIMIT
    longitude = (lax.axis_index(LON).astype(jnp.float32) + frac[1:2]) * (2.0 * math.pi / SECTORS)
    angles = jnp.concatenate([latitude, longitude], axis=0)
    cosines, sines = jnp.cos(angles), jnp.sin(angles)
    place = (cosines[0:1] * cosines[1:2], cosines[0:1] * sines[1:2], sines[0:1])
    level = frac[2:3]
    sigma = jnp.log(spread_ref[...].astype(jnp.float32)) * LOG2E - VERT * level * level
    kind = type_ref[...]
    one = jnp.ones_like(level)
    table = [[math.log2(k) for k in row] for row in COUPLING]

    def looked_up(column):
        return jnp.where(kind == 0, table[0][column], jnp.where(kind == 1, table[1][column], table[2][column]))

    at_height = looked_up(0)
    far = []
    own = []
    for axis in place:
        far += pieces(axis)
        own += [HORIZ * axis] * 3
    far += [level, jnp.where(kind == 1, one, 0.0), jnp.where(kind == 2, one, 0.0)]
    own += [2.0 * VERT * level, looked_up(1) - at_height, looked_up(2) - at_height]
    far += [*pieces(sigma), one]
    own += [one, one, one, sigma + at_height - HORIZ]
    for row in range(16):
        far_rows[row : row + 1, :] = far[row]
        own_rows[row : row + 1, :] = own[row]
    message_ref[0:16, :] = start_ref[...].astype(jnp.bfloat16)
    message_ref[16:32, :] = far_rows[...].astype(jnp.bfloat16)
    error_out_ref[...] = error_ref[...]
    kept_ref[...] = start_ref[...]
    added_ref[...] = error_ref[...] * start_ref[...]
    for step in range(3):
        if step:
            own_rows[15:16, :] = own[15] + step * math.log2(TAPER_STEP)
        left = own_rows[...]
        for piece in range(3):
            part = left.astype(jnp.bfloat16)
            own_ref[step, 16 * piece : 16 * piece + 16, :] = part
            left = left - part.astype(jnp.float32)


def whole(space=pltpu.VMEM):
    return pl.BlockSpec(memory_space=space)


def describe(start, error_var, where_frac, spread, obs_type):
    return pl.pallas_call(
        describe_kernel,
        out_shape=(
            pltpu.VMEM((32, OBS), jnp.bfloat16),
            pltpu.VMEM((3, 48, OBS), jnp.bfloat16),
            pltpu.VMEM((1, OBS), jnp.float32),
            pltpu.VMEM((RHS, OBS), jnp.float32),
            pltpu.VMEM((RHS, OBS), jnp.float32),
        ),
        in_specs=[whole()] * 5,
        out_specs=[whole()] * 5,
        scratch_shapes=[pltpu.VMEM((16, OBS), jnp.float32)] * 2,
        name="describe",
    )(start, error_var, where_frac, spread, obs_type)


def build_kernel(steps, near_ref, own_ref, added_ref, tile_ref, sum_ref, *sent):
    for slot, step in enumerate(steps):
        far = near_ref[slot, 16:32, :]
        far = jnp.concatenate([far, far, far], axis=0)
        power = lax.dot_general(far, own_ref[step], (((0,), (0,)), ((), ())), preferred_element_type=jnp.float32)
        tile_ref[slot] = jnp.exp2(power).astype(jnp.bfloat16)
    total = added_ref[...] + products(lambda slot: near_ref[slot, 0:16, :], tile_ref)
    sum_ref[...] = total
    for ref in sent:
        ref[...] = total.astype(jnp.bfloat16)


def products(field_of, tile_ref):
    return sum(jnp.dot(field_of(slot), tile_ref[slot], preferred_element_type=jnp.float32) for slot in range(3))


def apply_kernel(scaled, near_ref, tile_ref, *refs):
    total = refs[0][...]
    if scaled:
        total = total * refs[1][...]
    total = total + products(lambda slot: near_ref[slot], tile_ref)
    sum_ref, *sent = refs[1 + scaled :]
    sum_ref[...] = total
    for ref in sent:
        ref[...] = total.astype(jnp.bfloat16)


SAME_BAND = (1, 0, 1)
OTHER_BAND = (2, 1, 2)


def cost(built):
    entries = 3 * OBS * OBS
    return pl.CostEstimate(
        flops=2 * entries * (RHS + 256 * built),
        bytes_accessed=2 * entries,
        transcendentals=entries * built,
    )


def sums(last):
    shapes = [pltpu.VMEM((RHS, OBS), jnp.float32)]
    if last:
        shapes.append(pltpu.VMEM((RHS, OBS), jnp.bfloat16))
    return shapes


def build(steps, near, own, added, last=False):
    shapes = [pltpu.VMEM((3, OBS, OBS), jnp.bfloat16)] + sums(last)
    return pl.pallas_call(
        functools.partial(build_kernel, steps),
        out_shape=shapes,
        in_specs=[whole()] * 3,
        out_specs=[whole()] * len(shapes),
        compiler_params=pltpu.CompilerParams(vmem_limit_bytes=16 << 20),
        cost_estimate=cost(1),
        name="build",
    )(near, own, added)


def apply(near, tiles, added, scale=None, last=False):
    shapes = sums(last)
    scales = [] if scale is None else [scale]
    return pl.pallas_call(
        functools.partial(apply_kernel, len(scales)),
        out_shape=shapes,
        in_specs=[whole()] * (3 + len(scales)),
        out_specs=[whole()] * len(shapes),
        compiler_params=pltpu.CompilerParams(vmem_limit_bytes=16 << 20),
        cost_estimate=cost(0),
        name="apply",
    )(near, tiles, added, *scales)


def coefficients(gram):
    def inner(left, right):
        total = 0.0
        for i in range(4):
            for j in range(4):
                if left[i] is not None and right[j] is not None:
                    total = total + left[i] * right[j] * gram[min(i, j), max(i, j)]
        return total

    def axpy(scale, added, start):
        out = []
        for a, s in zip(added, start):
            if a is None:
                out.append(s)
            else:
                out.append(scale * a if s is None else s + scale * a)
        return out

    one = jnp.ones_like(gram[0, 0])
    answer = [None] * 4
    residual = [one, None, None, None]
    direction = residual
    norm_now = gram[0, 0]
    for iteration in range(ITERS):
        image = [None] + direction[:3]
        step_len = norm_now / inner(direction, image)
        answer = axpy(step_len, direction, answer)
        residual = axpy(-step_len, image, residual)
        if iteration < ITERS - 1:
            norm_next = inner(residual, residual)
            direction = axpy(norm_next / norm_now, direction, residual)
            norm_now = norm_next
    return answer[:3], residual


def lane_sums(products):
    empty = jnp.zeros((128 - RHS * len(products), OBS), jnp.float32)
    stacked = jnp.concatenate([*products, empty], axis=0) if len(products) < 8 else jnp.concatenate(products, axis=0)
    ones = jnp.ones((8, OBS), jnp.bfloat16)
    total = 0.0
    for part in pieces(stacked):
        total = total + lax.dot_general(
            ones, part.astype(jnp.bfloat16), (((1,), (1,)), ((), ())), preferred_element_type=jnp.float32
        )
    return total[0:1]


MOMENTS = 6


def same_band_kernel(near_ref, tile_ref, second_ref, scale_ref, start_ref, first_ref, sum_ref, row_ref):
    start, first, second = start_ref[...], first_ref[...], second_ref[...]
    sum_ref[...] = second * scale_ref[...] + products(lambda slot: near_ref[slot], tile_ref)
    row_ref[...] = lane_sums(
        [start * start, start * first, first * first, start * second, first * second, second * second]
    )


def other_bands(swap_ref, both_ref, below_ref, above_ref, done):
    band = lax.axis_index(LAT)
    inside = jnp.where((band == 0) | (band == BANDS - 1), 0.0, 1.0)

    def add(swap_tiles, both_tiles, position):
        total = products(lambda slot: swap_ref[slot], swap_tiles)
        done(total + inside * products(lambda slot: both_ref[position, slot], both_tiles))

    @pl.when(band % 2 == 1)
    def _():
        add(below_ref, above_ref, 1)

    @pl.when(band % 2 == 0)
    def _():
        add(above_ref, below_ref, 0)


def second_kernel(swap_ref, both_ref, below_ref, above_ref, part_ref, sum_ref, sent_ref):
    def done(others):
        total = part_ref[...] + others
        sum_ref[...] = total
        sent_ref[...] = total.astype(jnp.bfloat16)

    other_bands(swap_ref, both_ref, below_ref, above_ref, done)


def third_kernel(swap_ref, both_ref, below_ref, above_ref, part_ref, second_ref, row_ref, sum_ref, copies_ref):
    def done(others):
        total = part_ref[...] + others
        sum_ref[...] = total
        before = [jnp.zeros_like(total)] * MOMENTS
        row = row_ref[...] + lane_sums([*before, second_ref[...] * total])
        copies_ref[...] = jnp.broadcast_to(row[None], copies_ref.shape)

    other_bands(swap_ref, both_ref, below_ref, above_ref, done)


def between_kernel(total_ref, copies_ref):
    copies_ref[...] = jnp.broadcast_to(jnp.sum(total_ref[...], axis=0)[None], copies_ref.shape)


def finish_kernel(total_ref, start_ref, first_ref, second_ref, third_ref, answer_ref, residual_ref):
    totals = jnp.broadcast_to(jnp.sum(total_ref[...], axis=0), (RHS, 128))
    lane = lax.broadcasted_iota(jnp.int32, (RHS, 128), 1)
    row = lax.broadcasted_iota(jnp.int32, (RHS, 128), 0)
    moments = [
        jnp.sum(jnp.where(lane == row + RHS * at, totals, 0.0), axis=1, keepdims=True) for at in range(MOMENTS + 1)
    ]
    names = {(0, 0): 0, (0, 1): 1, (1, 1): 2, (0, 2): 3, (1, 2): 4, (2, 2): 5, (2, 3): 6, (0, 3): 4, (1, 3): 5}
    answer, residual = coefficients({pair: moments[at] for pair, at in names.items()})
    basis = (start_ref[...], first_ref[...], second_ref[...], third_ref[...])
    answer_ref[0, 0] = sum(c * v for c, v in zip(answer, basis))
    residual_ref[0, 0] = sum(c * v for c, v in zip(residual, basis))


def call(kernel, shapes, operands, name):
    return pl.pallas_call(
        kernel,
        out_shape=shapes,
        in_specs=[whole()] * len(operands),
        out_specs=[whole()] * len(shapes),
        compiler_params=pltpu.CompilerParams(vmem_limit_bytes=16 << 20),
        cost_estimate=cost(0),
        name=name,
    )(*operands)


def local(innovations, obs_error, where_frac, spread, obs_type):
    message, own, error_var, added, start = describe(
        innovations[0, 0], obs_error[0], where_frac[0, 0], spread[0], obs_type[0]
    )
    wide = widened(message)
    below, above = all_bands(wide)
    tiles, part = build(SAME_BAND, wide, own, added)
    tiles_below, part = build(OTHER_BAND, below, own, part)
    tiles_above, first, sent = build(OTHER_BAND, above, own, part, True)
    wide = widened(sent)
    swap, both = all_bands_paired(wide)
    part, = apply(wide, tiles, first, error_var)
    field = pltpu.VMEM((RHS, OBS), jnp.float32)
    second, sent = call(
        second_kernel,
        [field, pltpu.VMEM((RHS, OBS), jnp.bfloat16)],
        [swap, both, tiles_below, tiles_above, part],
        "second",
    )
    wide = widened(sent)
    swap, both = all_bands_paired(wide)
    part, row = call(
        same_band_kernel,
        [field, pltpu.VMEM((1, 128), jnp.float32)],
        [wide, tiles, second, error_var, start, first],
        "same_band",
    )
    copies = [pltpu.VMEM((extent(axes), 1, 128), jnp.float32) for axes in GROUPS]
    third, partial = call(
        third_kernel,
        [field, copies[0]],
        [swap, both, tiles_below, tiles_above, part, second, row],
        "third",
    )
    partial = lax.all_to_all(partial, GROUPS[0], 0, 0)
    partial, = call(between_kernel, [copies[1]], [partial], "between")
    totals = lax.all_to_all(partial, GROUPS[1], 0, 0)
    whole_field = jax.ShapeDtypeStruct((1, 1, RHS, OBS), jnp.float32)
    return call(finish_kernel, [whole_field] * 2, [totals, start, first, second, third], "finish")


def solution(mesh):
    fine = Mesh(mesh.devices.reshape(2, 4, 4, 8, 2), LAT + LON)
    in_specs = (
        P(LAT, LON, None, None),
        P(LAT, LON, None),
        P(LAT, LON, None, None),
        P(LAT, LON, None),
        P(LAT, LON, None),
    )
    out_specs = (P(LAT, LON, None, None), P(LAT, LON, None, None))
    return jax.shard_map(local, mesh=fine, in_specs=in_specs, out_specs=out_specs, check_vma=False)
```

```python
import functools
import math

import jax
import jax.numpy as jnp
from jax import lax
from jax.experimental import pallas as pl
from jax.experimental.pallas import tpu as pltpu
from jax.sharding import Mesh, PartitionSpec as P

ITERS = 3
BANDS = 8
SECTORS = 64
OBS = 512
RHS = 16

LAT_LIMIT = 80.0 * math.pi / 180.0
HORIZ_SQ = 0.05 * 0.05
VERT_SQ = 0.3 * 0.3
TAPER_STEP = 0.45
LOG2E = 1.0 / math.log(2.0)
HORIZ = LOG2E / HORIZ_SQ
VERT = LOG2E / (2.0 * VERT_SQ)
COUPLING = ((1.0, 0.45, 0.45), (0.45, 1.0, 0.25), (0.45, 0.25, 1.0))

LAT = ("z_lo", "x")
LON = ("z_hi", "y", "core")
GROUPS = (("z_lo", "z_hi", "x"), ("y", "core"))


def extent(axes):
    size = 1
    for axis in axes:
        size *= lax.axis_size(axis)
    return size


def pairs(count, first):
    return [[low, (low + 1) % count] for low in range(first, count, 2)]


def partner(block, axes, first):
    both = lax.all_gather(block, axes, axis_index_groups=pairs(extent(axes), first))
    leads = lax.axis_index(axes) % 2 == first
    return jnp.where(leads, both[1], both[0])


def widened(block):
    inner = partner(block, LON, 0)
    inner, block = lax.optimization_barrier((inner, block))
    outer = partner(block, LON, 1)
    return jnp.stack([outer, block, inner])


def all_bands(wide):
    count = extent(LAT)
    below = lax.ppermute(wide, LAT, [(i, i + 1) for i in range(count - 1)])
    above = lax.ppermute(wide, LAT, [(i + 1, i) for i in range(count - 1)])
    return below, above


def all_bands_paired(wide):
    count = extent(LAT)
    swap = lax.ppermute(wide, LAT, [p for a, b in pairs(count, 0) for p in ((a, b), (b, a))])
    return swap, lax.all_gather(wide, LAT, axis_index_groups=pairs(count, 1))


def rounded(value):
    return value.astype(jnp.bfloat16).astype(jnp.float32)


def pieces(value):
    high = rounded(value)
    mid = rounded(value - high)
    return high, mid, rounded(value - high - mid)


def own_side(place, level, kinds, offset):
    one = jnp.ones_like(level)

    def looked_up(column):
        logs = [math.log2(row[column]) for row in COUPLING]
        return logs[0] + kinds[0] * (logs[1] - logs[0]) + kinds[1] * (logs[2] - logs[0])

    at_height = looked_up(0)
    rows = [HORIZ * axis for axis in place for _ in range(3)]
    rows += [2.0 * VERT * level, looked_up(1) - at_height, looked_up(2) - at_height]
    return rows + [one, one, offset + at_height - HORIZ, jnp.zeros_like(level)]


def far_side(place, level, kinds, offset, error):
    rows = [piece for axis in place for piece in pieces(axis)]
    return rows + [level, *kinds, *pieces(offset)[:2], jnp.ones_like(level), error]


def write_own(own_ref, rows_ref, rows):
    for row in range(16):
        rows_ref[row : row + 1, :] = rows[row]
    for step in range(3):
        if step:
            rows_ref[14:15, :] = rows[14] + step * math.log2(TAPER_STEP)
        left = rows_ref[...]
        for piece in range(3):
            part = left.astype(jnp.bfloat16)
            own_ref[step, 16 * piece : 16 * piece + 16, :] = part
            left = left - part.astype(jnp.float32)


def describe_kernel(
    start_ref, error_ref, frac_ref, spread_ref, type_ref,
    message_ref, own_ref, error_out_ref, added_ref, kept_ref, rows_ref,
):
    frac = frac_ref[...].astype(jnp.float32)
    latitude = (lax.axis_index(LAT).astype(jnp.float32) + frac[0:1]) * (2.0 * LAT_LIMIT / BANDS) - LAT_LIMIT
    longitude = (lax.axis_index(LON).astype(jnp.float32) + frac[1:2]) * (2.0 * math.pi / SECTORS)
    angles = jnp.concatenate([latitude, longitude], axis=0)
    cosines, sines = jnp.cos(angles), jnp.sin(angles)
    place = (cosines[0:1] * cosines[1:2], cosines[0:1] * sines[1:2], sines[0:1])
    level = frac[2:3]
    offset = jnp.log(spread_ref[...].astype(jnp.float32)) * LOG2E - VERT * level * level
    kinds = [jnp.where(type_ref[...] == kind, jnp.ones_like(level), 0.0) for kind in (1, 2)]
    far = far_side(place, level, kinds, offset, error_ref[...])
    for row in range(16):
        rows_ref[row : row + 1, :] = far[row]
    message_ref[0:16, :] = start_ref[...].astype(jnp.bfloat16)
    message_ref[16:32, :] = rows_ref[...].astype(jnp.bfloat16)
    error_out_ref[...] = error_ref[...]
    kept_ref[...] = start_ref[...]
    added_ref[...] = error_ref[...] * start_ref[...]
    write_own(own_ref, rows_ref, own_side(place, level, kinds, offset))


def whole(space=pltpu.VMEM):
    return pl.BlockSpec(memory_space=space)


def describe(start, error_var, where_frac, spread, obs_type):
    return pl.pallas_call(
        describe_kernel,
        out_shape=(
            pltpu.VMEM((32, OBS), jnp.bfloat16),
            pltpu.VMEM((3, 48, OBS), jnp.bfloat16),
            pltpu.VMEM((1, OBS), jnp.float32),
            pltpu.VMEM((RHS, OBS), jnp.float32),
            pltpu.VMEM((RHS, OBS), jnp.float32),
        ),
        in_specs=[whole()] * 5,
        out_specs=[whole()] * 5,
        scratch_shapes=[pltpu.VMEM((16, OBS), jnp.float32)],
        name="describe",
    )(start, error_var, where_frac, spread, obs_type)


OWN = (1, 2, 3)
OUTER = (0, 1, 2)


def part_of(columns, steps, near_ref, own_ref, tile_ref):
    for slot, (column, step) in enumerate(zip(columns, steps)):
        far = near_ref[column, 16:32, :]
        far = jnp.concatenate([far, far, far], axis=0)
        power = lax.dot_general(far, own_ref[step], (((0,), (0,)), ((), ())), preferred_element_type=jnp.float32)
        tile_ref[slot] = jnp.exp2(power).astype(jnp.bfloat16)
    return products(lambda slot: near_ref[columns[slot], 0:16, :], tile_ref)


def build_same_kernel(near_ref, own_ref, added_ref, tile_ref, sum_ref, outer_own_ref, outer_sum_ref, rows_ref, scratch_ref):
    rows = near_ref[1, 16:32, :].astype(jnp.float32)
    row = [rows[at : at + 1] for at in range(16)]
    place = [row[3 * axis] + row[3 * axis + 1] + row[3 * axis + 2] for axis in range(3)]
    write_own(outer_own_ref, rows_ref, own_side(place, row[9], row[10:12], row[12] + row[13]))
    sum_ref[...] = added_ref[...] + part_of(OWN, SAME_BAND, near_ref, own_ref, tile_ref)
    outer_added = row[15] * near_ref[1, 0:16, :].astype(jnp.float32)
    outer_sum_ref[...] = outer_added + part_of(OUTER, SAME_BAND, near_ref, outer_own_ref, scratch_ref)


def build_other_kernel(
    near_ref, own_ref, added_ref, outer_own_ref, outer_added_ref, tile_ref, sum_ref, *more
):
    *outer_refs, scratch_ref = more
    total = added_ref[...] + part_of(OWN, OTHER_BAND, near_ref, own_ref, tile_ref)
    outer = outer_added_ref[...] + part_of(OUTER, OTHER_BAND, near_ref, outer_own_ref, scratch_ref)
    sum_ref[...] = total
    if len(outer_refs) == 1:
        outer_refs[0][...] = outer
    else:
        for ref, value in zip(outer_refs, (total, outer)):
            ref[...] = value.astype(jnp.bfloat16)


def products(field_of, tile_ref):
    return sum(jnp.dot(field_of(slot), tile_ref[slot], preferred_element_type=jnp.float32) for slot in range(3))


def apply_kernel(scaled, near_ref, tile_ref, *refs):
    total = refs[0][...]
    if scaled:
        total = total * refs[1][...]
    total = total + products(lambda slot: near_ref[slot], tile_ref)
    sum_ref, *sent = refs[1 + scaled :]
    sum_ref[...] = total
    for ref in sent:
        ref[...] = total.astype(jnp.bfloat16)


SAME_BAND = (1, 0, 1)
OTHER_BAND = (2, 1, 2)


def cost(built):
    entries = 3 * OBS * OBS
    return pl.CostEstimate(
        flops=2 * entries * (RHS + 256 * built),
        bytes_accessed=2 * entries,
        transcendentals=entries * built,
    )


def sums(last):
    shapes = [pltpu.VMEM((RHS, OBS), jnp.float32)]
    if last:
        shapes.append(pltpu.VMEM((RHS, OBS), jnp.bfloat16))
    return shapes


FIELD = pltpu.VMEM((RHS, OBS), jnp.float32)
SENT = pltpu.VMEM((RHS, OBS), jnp.bfloat16)
TILES = pltpu.VMEM((3, OBS, OBS), jnp.bfloat16)
OWN_SIDE = pltpu.VMEM((3, 48, OBS), jnp.bfloat16)


def build(kernel, shapes, operands, scratch):
    return pl.pallas_call(
        kernel,
        out_shape=shapes,
        in_specs=[whole()] * len(operands),
        out_specs=[whole()] * len(shapes),
        scratch_shapes=scratch,
        compiler_params=pltpu.CompilerParams(vmem_limit_bytes=16 << 20),
        cost_estimate=cost(2),
        name="build",
    )(*operands)


def apply(near, tiles, added, scale=None, last=False):
    shapes = sums(last)
    scales = [] if scale is None else [scale]
    return pl.pallas_call(
        functools.partial(apply_kernel, len(scales)),
        out_shape=shapes,
        in_specs=[whole()] * (3 + len(scales)),
        out_specs=[whole()] * len(shapes),
        compiler_params=pltpu.CompilerParams(vmem_limit_bytes=16 << 20),
        cost_estimate=cost(0),
        name="apply",
    )(near, tiles, added, *scales)


def coefficients(gram):
    def inner(left, right):
        total = 0.0
        for i in range(4):
            for j in range(4):
                if left[i] is not None and right[j] is not None:
                    total = total + left[i] * right[j] * gram[min(i, j), max(i, j)]
        return total

    def axpy(scale, added, start):
        out = []
        for a, s in zip(added, start):
            if a is None:
                out.append(s)
            else:
                out.append(scale * a if s is None else s + scale * a)
        return out

    one = jnp.ones_like(gram[0, 0])
    answer = [None] * 4
    residual = [one, None, None, None]
    direction = residual
    norm_now = gram[0, 0]
    for iteration in range(ITERS):
        image = [None] + direction[:3]
        step_len = norm_now / inner(direction, image)
        answer = axpy(step_len, direction, answer)
        residual = axpy(-step_len, image, residual)
        if iteration < ITERS - 1:
            norm_next = inner(residual, residual)
            direction = axpy(norm_next / norm_now, direction, residual)
            norm_now = norm_next
    return answer[:3], residual


def lane_sums(products):
    empty = jnp.zeros((128 - RHS * len(products), OBS), jnp.float32)
    stacked = jnp.concatenate([*products, empty], axis=0) if len(products) < 8 else jnp.concatenate(products, axis=0)
    ones = jnp.ones((8, OBS), jnp.bfloat16)
    total = 0.0
    for part in pieces(stacked):
        total = total + lax.dot_general(
            ones, part.astype(jnp.bfloat16), (((1,), (1,)), ((), ())), preferred_element_type=jnp.float32
        )
    return total[0:1]


MOMENTS = 6


def same_band_kernel(near_ref, tile_ref, second_ref, scale_ref, start_ref, first_ref, sum_ref, row_ref):
    start, first, second = start_ref[...], first_ref[...], second_ref[...]
    sum_ref[...] = second * scale_ref[...] + products(lambda slot: near_ref[slot], tile_ref)
    row_ref[...] = lane_sums(
        [start * start, start * first, first * first, start * second, first * second, second * second]
    )


def below_kernel(near_ref, tile_ref, part_ref, second_ref, row_ref, sum_ref, copies_ref):
    part = part_ref[...]
    total = part + products(lambda slot: near_ref[slot], tile_ref)
    sum_ref[...] = total
    product = second_ref[...] * (2.0 * total - part)
    before = [jnp.zeros_like(product)] * MOMENTS
    row = row_ref[...] + lane_sums([*before, product])
    copies_ref[...] = jnp.broadcast_to(row[None], copies_ref.shape)


def paired_kernel(swap_ref, both_ref, below_ref, above_ref, part_ref, sum_ref, sent_ref):
    band = lax.axis_index(LAT)
    inside = jnp.where((band == 0) | (band == BANDS - 1), 0.0, 1.0)

    def add(swap_tiles, both_tiles, position):
        total = part_ref[...] + products(lambda slot: swap_ref[slot], swap_tiles)
        total = total + inside * products(lambda slot: both_ref[position, slot], both_tiles)
        sum_ref[...] = total
        sent_ref[...] = total.astype(jnp.bfloat16)

    @pl.when(band % 2 == 1)
    def _():
        add(below_ref, above_ref, 1)

    @pl.when(band % 2 == 0)
    def _():
        add(above_ref, below_ref, 0)


def above_kernel(near_ref, total_ref, tile_ref, lower_ref, third_ref, copies_ref):
    third_ref[...] = lower_ref[...] + products(lambda slot: near_ref[slot], tile_ref)
    copies_ref[...] = jnp.broadcast_to(jnp.sum(total_ref[...], axis=0)[None], copies_ref.shape)


def finish_kernel(total_ref, start_ref, first_ref, second_ref, third_ref, answer_ref, residual_ref):
    totals = jnp.broadcast_to(jnp.sum(total_ref[...], axis=0), (RHS, 128))
    lane = lax.broadcasted_iota(jnp.int32, (RHS, 128), 1)
    row = lax.broadcasted_iota(jnp.int32, (RHS, 128), 0)
    moments = [
        jnp.sum(jnp.where(lane == row + RHS * at, totals, 0.0), axis=1, keepdims=True) for at in range(MOMENTS + 1)
    ]
    names = {(0, 0): 0, (0, 1): 1, (1, 1): 2, (0, 2): 3, (1, 2): 4, (2, 2): 5, (2, 3): 6, (0, 3): 4, (1, 3): 5}
    answer, residual = coefficients({pair: moments[at] for pair, at in names.items()})
    basis = (start_ref[...], first_ref[...], second_ref[...], third_ref[...])
    answer_ref[0, 0] = sum(c * v for c, v in zip(answer, basis))
    residual_ref[0, 0] = sum(c * v for c, v in zip(residual, basis))


def call(kernel, shapes, operands, name):
    return pl.pallas_call(
        kernel,
        out_shape=shapes,
        in_specs=[whole()] * len(operands),
        out_specs=[whole()] * len(shapes),
        compiler_params=pltpu.CompilerParams(vmem_limit_bytes=16 << 20),
        cost_estimate=cost(0),
        name=name,
    )(*operands)


def local(innovations, obs_error, where_frac, spread, obs_type):
    message, own, error_var, added, start = describe(
        innovations[0, 0], obs_error[0], where_frac[0, 0], spread[0], obs_type[0]
    )
    inner = partner(message, LON, 0)
    outer = partner(jnp.stack([message, inner]), LON, 1)
    wide = jnp.stack([outer[1], outer[0], message, inner])
    below, above = all_bands(wide)
    tiles, part, outer_own, outer = build(
        build_same_kernel,
        [TILES, FIELD, OWN_SIDE, FIELD],
        [wide, own, added],
        [pltpu.VMEM((16, OBS), jnp.float32), TILES],
    )
    tiles_below, part, outer = build(
        build_other_kernel, [TILES, FIELD, FIELD], [below, own, part, outer_own, outer], [TILES]
    )
    tiles_above, first, sent, outer_sent = build(
        build_other_kernel, [TILES, FIELD, SENT, SENT], [above, own, part, outer_own, outer], [TILES]
    )
    wide = jnp.stack([outer_sent, sent, partner(sent, LON, 0)])
    swap, both = all_bands_paired(wide)
    part, = apply(wide, tiles, first, error_var)
    field = pltpu.VMEM((RHS, OBS), jnp.float32)
    second, sent = call(
        paired_kernel,
        [field, pltpu.VMEM((RHS, OBS), jnp.bfloat16)],
        [swap, both, tiles_below, tiles_above, part],
        "paired",
    )
    wide = widened(sent)
    below, above = all_bands(wide)
    part, row = call(
        same_band_kernel,
        [field, pltpu.VMEM((1, 128), jnp.float32)],
        [wide, tiles, second, error_var, start, first],
        "same_band",
    )
    copies = [pltpu.VMEM((extent(axes), 1, 128), jnp.float32) for axes in GROUPS]
    lower, partial = call(below_kernel, [field, copies[0]], [below, tiles_below, part, second, row], "below")
    partial = lax.all_to_all(partial, GROUPS[0], 0, 0)
    third, partial = call(above_kernel, [field, copies[1]], [above, partial, tiles_above, lower], "above")
    totals = lax.all_to_all(partial, GROUPS[1], 0, 0)
    whole_field = jax.ShapeDtypeStruct((1, 1, RHS, OBS), jnp.float32)
    return call(finish_kernel, [whole_field] * 2, [totals, start, first, second, third], "finish")


def solution(mesh):
    fine = Mesh(mesh.devices.reshape(2, 4, 4, 8, 2), LAT + LON)
    in_specs = (
        P(LAT, LON, None, None),
        P(LAT, LON, None),
        P(LAT, LON, None, None),
        P(LAT, LON, None),
        P(LAT, LON, None),
    )
    out_specs = (P(LAT, LON, None, None), P(LAT, LON, None, None))
    return jax.shard_map(local, mesh=fine, in_specs=in_specs, out_specs=out_specs, check_vma=False)
```

```python
import functools
import math

import jax
import jax.numpy as jnp
from jax import lax
from jax.experimental import pallas as pl
from jax.experimental.pallas import tpu as pltpu
from jax.sharding import Mesh, PartitionSpec as P

ITERS = 3
BANDS = 8
SECTORS = 64
OBS = 512
RHS = 16

LAT_LIMIT = 80.0 * math.pi / 180.0
HORIZ_SQ = 0.05 * 0.05
VERT_SQ = 0.3 * 0.3
TAPER_STEP = 0.45
LOG2E = 1.0 / math.log(2.0)
HORIZ = LOG2E / HORIZ_SQ
VERT = LOG2E / (2.0 * VERT_SQ)
COUPLING = ((1.0, 0.45, 0.45), (0.45, 1.0, 0.25), (0.45, 0.25, 1.0))

LAT = ("z_lo", "x")
LON = ("z_hi", "y", "core")
GROUPS = (("z_lo", "z_hi", "x"), ("y", "core"))


def extent(axes):
    size = 1
    for axis in axes:
        size *= lax.axis_size(axis)
    return size


def pairs(count, first):
    return [[low, (low + 1) % count] for low in range(first, count, 2)]


def partner(block, axes, first):
    both = lax.all_gather(block, axes, axis_index_groups=pairs(extent(axes), first))
    leads = lax.axis_index(axes) % 2 == first
    return jnp.where(leads, both[1], both[0])


def widened(block):
    inner = partner(block, LON, 0)
    inner, block = lax.optimization_barrier((inner, block))
    outer = partner(block, LON, 1)
    return jnp.stack([outer, block, inner])


def all_bands(wide):
    count = extent(LAT)
    below = lax.ppermute(wide, LAT, [(i, i + 1) for i in range(count - 1)])
    above = lax.ppermute(wide, LAT, [(i + 1, i) for i in range(count - 1)])
    return below, above


def all_bands_paired(wide):
    count = extent(LAT)
    swap = lax.ppermute(wide, LAT, [p for a, b in pairs(count, 0) for p in ((a, b), (b, a))])
    return swap, lax.all_gather(wide, LAT, axis_index_groups=pairs(count, 1))


def rounded(value):
    return value.astype(jnp.bfloat16).astype(jnp.float32)


def pieces(value):
    high = rounded(value)
    mid = rounded(value - high)
    return high, mid, rounded(value - high - mid)


def own_side(place, level, kinds, offset):
    one = jnp.ones_like(level)

    def looked_up(column):
        logs = [math.log2(row[column]) for row in COUPLING]
        return logs[0] + kinds[0] * (logs[1] - logs[0]) + kinds[1] * (logs[2] - logs[0])

    at_height = looked_up(0)
    rows = [HORIZ * axis for axis in place for _ in range(3)]
    rows += [2.0 * VERT * level, looked_up(1) - at_height, looked_up(2) - at_height]
    return rows + [one, one, offset + at_height - HORIZ, jnp.zeros_like(level)]


def far_side(place, level, kinds, offset, error):
    rows = [piece for axis in place for piece in pieces(axis)]
    return rows + [level, *kinds, *pieces(offset)[:2], jnp.ones_like(level), error]


def write_own(own_ref, rows_ref, rows):
    for row in range(16):
        rows_ref[row : row + 1, :] = rows[row]
    for step in range(3):
        if step:
            rows_ref[14:15, :] = rows[14] + step * math.log2(TAPER_STEP)
        left = rows_ref[...]
        for piece in range(3):
            part = left.astype(jnp.bfloat16)
            own_ref[step, 16 * piece : 16 * piece + 16, :] = part
            left = left - part.astype(jnp.float32)


def describe_kernel(
    start_ref, error_ref, frac_ref, spread_ref, type_ref,
    message_ref, own_ref, error_out_ref, added_ref, kept_ref, rows_ref,
):
    frac = frac_ref[...].astype(jnp.float32)
    latitude = (lax.axis_index(LAT).astype(jnp.float32) + frac[0:1]) * (2.0 * LAT_LIMIT / BANDS) - LAT_LIMIT
    longitude = (lax.axis_index(LON).astype(jnp.float32) + frac[1:2]) * (2.0 * math.pi / SECTORS)
    angles = jnp.concatenate([latitude, longitude], axis=0)
    cosines, sines = jnp.cos(angles), jnp.sin(angles)
    place = (cosines[0:1] * cosines[1:2], cosines[0:1] * sines[1:2], sines[0:1])
    level = frac[2:3]
    offset = jnp.log(spread_ref[...].astype(jnp.float32)) * LOG2E - VERT * level * level
    kinds = [jnp.where(type_ref[...] == kind, jnp.ones_like(level), 0.0) for kind in (1, 2)]
    far = far_side(place, level, kinds, offset, error_ref[...])
    for row in range(16):
        rows_ref[row : row + 1, :] = far[row]
    message_ref[0:16, :] = start_ref[...].astype(jnp.bfloat16)
    message_ref[16:32, :] = rows_ref[...].astype(jnp.bfloat16)
    error_out_ref[...] = error_ref[...]
    kept_ref[...] = start_ref[...]
    added_ref[...] = error_ref[...] * start_ref[...]
    write_own(own_ref, rows_ref, own_side(place, level, kinds, offset))


def whole(space=pltpu.VMEM):
    return pl.BlockSpec(memory_space=space)


def describe(start, error_var, where_frac, spread, obs_type):
    return pl.pallas_call(
        describe_kernel,
        out_shape=(
            pltpu.VMEM((32, OBS), jnp.bfloat16),
            pltpu.VMEM((3, 48, OBS), jnp.bfloat16),
            pltpu.VMEM((1, OBS), jnp.float32),
            pltpu.VMEM((RHS, OBS), jnp.float32),
            pltpu.VMEM((RHS, OBS), jnp.float32),
        ),
        in_specs=[whole()] * 5,
        out_specs=[whole()] * 5,
        scratch_shapes=[pltpu.VMEM((16, OBS), jnp.float32)],
        name="describe",
    )(start, error_var, where_frac, spread, obs_type)


OWN = (1, 2, 3)
OUTER = (0, 1, 2)


def part_of(columns, steps, near_ref, own_ref, tile_ref):
    for slot, (column, step) in enumerate(zip(columns, steps)):
        far = near_ref[column, 16:32, :]
        far = jnp.concatenate([far, far, far], axis=0)
        power = lax.dot_general(far, own_ref[step], (((0,), (0,)), ((), ())), preferred_element_type=jnp.float32)
        tile_ref[slot] = jnp.exp2(power).astype(jnp.bfloat16)
    return products(lambda slot: near_ref[columns[slot], 0:16, :], tile_ref)


def build_same_kernel(near_ref, own_ref, added_ref, tile_ref, sum_ref, outer_own_ref, outer_sum_ref, rows_ref, scratch_ref):
    rows = near_ref[1, 16:32, :].astype(jnp.float32)
    row = [rows[at : at + 1] for at in range(16)]
    place = [row[3 * axis] + row[3 * axis + 1] + row[3 * axis + 2] for axis in range(3)]
    write_own(outer_own_ref, rows_ref, own_side(place, row[9], row[10:12], row[12] + row[13]))
    sum_ref[...] = added_ref[...] + part_of(OWN, SAME_BAND, near_ref, own_ref, tile_ref)
    outer_added = row[15] * near_ref[1, 0:16, :].astype(jnp.float32)
    outer_sum_ref[...] = outer_added + part_of(OUTER, SAME_BAND, near_ref, outer_own_ref, scratch_ref)


def build_other_kernel(
    near_ref, own_ref, added_ref, outer_own_ref, outer_added_ref, tile_ref, sum_ref, *more
):
    *outer_refs, scratch_ref = more
    total = added_ref[...] + part_of(OWN, OTHER_BAND, near_ref, own_ref, tile_ref)
    outer = outer_added_ref[...] + part_of(OUTER, OTHER_BAND, near_ref, outer_own_ref, scratch_ref)
    sum_ref[...] = total
    if len(outer_refs) == 1:
        outer_refs[0][...] = outer
    else:
        for ref, value in zip(outer_refs, (total, outer)):
            ref[...] = value.astype(jnp.bfloat16)


def products(field_of, tile_ref):
    return sum(jnp.dot(field_of(slot), tile_ref[slot], preferred_element_type=jnp.float32) for slot in range(3))


def apply_kernel(scaled, near_ref, tile_ref, *refs):
    total = refs[0][...]
    if scaled:
        total = total * refs[1][...]
    total = total + products(lambda slot: near_ref[slot], tile_ref)
    sum_ref, *sent = refs[1 + scaled :]
    sum_ref[...] = total
    for ref in sent:
        ref[...] = total.astype(jnp.bfloat16)


SAME_BAND = (1, 0, 1)
OTHER_BAND = (2, 1, 2)


def cost(built):
    entries = 3 * OBS * OBS
    return pl.CostEstimate(
        flops=2 * entries * (RHS + 256 * built),
        bytes_accessed=2 * entries,
        transcendentals=entries * built,
    )


def sums(last):
    shapes = [pltpu.VMEM((RHS, OBS), jnp.float32)]
    if last:
        shapes.append(pltpu.VMEM((RHS, OBS), jnp.bfloat16))
    return shapes


FIELD = pltpu.VMEM((RHS, OBS), jnp.float32)
SENT = pltpu.VMEM((RHS, OBS), jnp.bfloat16)
TILES = pltpu.VMEM((3, OBS, OBS), jnp.bfloat16)
OWN_SIDE = pltpu.VMEM((3, 48, OBS), jnp.bfloat16)


def build(kernel, shapes, operands, scratch):
    return pl.pallas_call(
        kernel,
        out_shape=shapes,
        in_specs=[whole()] * len(operands),
        out_specs=[whole()] * len(shapes),
        scratch_shapes=scratch,
        compiler_params=pltpu.CompilerParams(vmem_limit_bytes=16 << 20),
        cost_estimate=cost(2),
        name="build",
    )(*operands)


def apply(near, tiles, added, scale=None, last=False):
    shapes = sums(last)
    scales = [] if scale is None else [scale]
    return pl.pallas_call(
        functools.partial(apply_kernel, len(scales)),
        out_shape=shapes,
        in_specs=[whole()] * (3 + len(scales)),
        out_specs=[whole()] * len(shapes),
        compiler_params=pltpu.CompilerParams(vmem_limit_bytes=16 << 20),
        cost_estimate=cost(0),
        name="apply",
    )(near, tiles, added, *scales)


def coefficients(gram):
    def inner(left, right):
        total = 0.0
        for i in range(4):
            for j in range(4):
                if left[i] is not None and right[j] is not None:
                    total = total + left[i] * right[j] * gram[min(i, j), max(i, j)]
        return total

    def axpy(scale, added, start):
        out = []
        for a, s in zip(added, start):
            if a is None:
                out.append(s)
            else:
                out.append(scale * a if s is None else s + scale * a)
        return out

    one = jnp.ones_like(gram[0, 0])
    answer = [None] * 4
    residual = [one, None, None, None]
    direction = residual
    norm_now = gram[0, 0]
    for iteration in range(ITERS):
        image = [None] + direction[:3]
        step_len = norm_now / inner(direction, image)
        answer = axpy(step_len, direction, answer)
        residual = axpy(-step_len, image, residual)
        if iteration < ITERS - 1:
            norm_next = inner(residual, residual)
            direction = axpy(norm_next / norm_now, direction, residual)
            norm_now = norm_next
    return answer[:3], residual


def lane_sums(products):
    empty = jnp.zeros((128 - RHS * len(products), OBS), jnp.float32)
    stacked = jnp.concatenate([*products, empty], axis=0) if len(products) < 8 else jnp.concatenate(products, axis=0)
    ones = jnp.ones((8, OBS), jnp.bfloat16)
    total = 0.0
    for part in pieces(stacked):
        total = total + lax.dot_general(
            ones, part.astype(jnp.bfloat16), (((1,), (1,)), ((), ())), preferred_element_type=jnp.float32
        )
    return total[0:1]


MOMENTS = 6


def same_band_kernel(near_ref, tile_ref, second_ref, scale_ref, start_ref, first_ref, sum_ref, row_ref):
    start, first, second = start_ref[...], first_ref[...], second_ref[...]
    sum_ref[...] = second * scale_ref[...] + products(lambda slot: near_ref[slot], tile_ref)
    row_ref[...] = lane_sums(
        [start * start, start * first, first * first, start * second, first * second, second * second]
    )


def below_kernel(near_ref, tile_ref, part_ref, second_ref, row_ref, sum_ref, copies_ref):
    part = part_ref[...]
    total = part + products(lambda slot: near_ref[slot], tile_ref)
    sum_ref[...] = total
    product = second_ref[...] * (2.0 * total - part)
    before = [jnp.zeros_like(product)] * MOMENTS
    row = row_ref[...] + lane_sums([*before, product])
    copies_ref[...] = jnp.broadcast_to(row[None], copies_ref.shape)


def paired_kernel(swap_ref, both_ref, below_ref, above_ref, part_ref, sum_ref, sent_ref):
    band = lax.axis_index(LAT)
    inside = jnp.where((band == 0) | (band == BANDS - 1), 0.0, 1.0)

    def add(swap_tiles, both_tiles, position):
        total = part_ref[...] + products(lambda slot: swap_ref[slot], swap_tiles)
        total = total + inside * products(lambda slot: both_ref[position, slot], both_tiles)
        sum_ref[...] = total
        sent_ref[...] = total.astype(jnp.bfloat16)

    @pl.when(band % 2 == 1)
    def _():
        add(below_ref, above_ref, 1)

    @pl.when(band % 2 == 0)
    def _():
        add(above_ref, below_ref, 0)


def between_kernel(total_ref, copies_ref):
    copies_ref[...] = jnp.broadcast_to(jnp.sum(total_ref[...], axis=0)[None], copies_ref.shape)


def finish_kernel(total_ref, start_ref, first_ref, second_ref, third_ref, answer_ref, residual_ref):
    totals = jnp.broadcast_to(jnp.sum(total_ref[...], axis=0), (RHS, 128))
    lane = lax.broadcasted_iota(jnp.int32, (RHS, 128), 1)
    row = lax.broadcasted_iota(jnp.int32, (RHS, 128), 0)
    moments = [
        jnp.sum(jnp.where(lane == row + RHS * at, totals, 0.0), axis=1, keepdims=True) for at in range(MOMENTS + 1)
    ]
    names = {(0, 0): 0, (0, 1): 1, (1, 1): 2, (0, 2): 3, (1, 2): 4, (2, 2): 5, (2, 3): 6, (0, 3): 4, (1, 3): 5}
    answer, residual = coefficients({pair: moments[at] for pair, at in names.items()})
    basis = (start_ref[...], first_ref[...], second_ref[...], third_ref[...])
    answer_ref[0, 0] = sum(c * v for c, v in zip(answer, basis))
    residual_ref[0, 0] = sum(c * v for c, v in zip(residual, basis))


def call(kernel, shapes, operands, name):
    return pl.pallas_call(
        kernel,
        out_shape=shapes,
        in_specs=[whole()] * len(operands),
        out_specs=[whole()] * len(shapes),
        compiler_params=pltpu.CompilerParams(vmem_limit_bytes=16 << 20),
        cost_estimate=cost(0),
        name=name,
    )(*operands)


def local(innovations, obs_error, where_frac, spread, obs_type):
    message, own, error_var, added, start = describe(
        innovations[0, 0], obs_error[0], where_frac[0, 0], spread[0], obs_type[0]
    )
    inner = partner(message, LON, 0)
    outer = partner(jnp.stack([message, inner]), LON, 1)
    wide = jnp.stack([outer[1], outer[0], message, inner])
    below, above = all_bands(wide)
    tiles, part, outer_own, outer = build(
        build_same_kernel,
        [TILES, FIELD, OWN_SIDE, FIELD],
        [wide, own, added],
        [pltpu.VMEM((16, OBS), jnp.float32), TILES],
    )
    tiles_below, part, outer = build(
        build_other_kernel, [TILES, FIELD, FIELD], [below, own, part, outer_own, outer], [TILES]
    )
    tiles_above, first, sent, outer_sent = build(
        build_other_kernel, [TILES, FIELD, SENT, SENT], [above, own, part, outer_own, outer], [TILES]
    )
    wide = jnp.stack([outer_sent, sent, partner(sent, LON, 0)])
    swap, both = all_bands_paired(wide)
    part, = apply(wide, tiles, first, error_var)
    field = pltpu.VMEM((RHS, OBS), jnp.float32)
    second, sent = call(
        paired_kernel,
        [field, pltpu.VMEM((RHS, OBS), jnp.bfloat16)],
        [swap, both, tiles_below, tiles_above, part],
        "paired",
    )
    wide = widened(sent)
    below, above = all_bands(wide)
    part, row = call(
        same_band_kernel,
        [field, pltpu.VMEM((1, 128), jnp.float32)],
        [wide, tiles, second, error_var, start, first],
        "same_band",
    )
    copies = [pltpu.VMEM((extent(axes), 1, 128), jnp.float32) for axes in GROUPS]
    lower, partial = call(below_kernel, [field, copies[0]], [below, tiles_below, part, second, row], "below")
    partial = lax.all_to_all(partial, GROUPS[0], 0, 0)
    third, = apply(above, tiles_above, lower)
    partial, = call(between_kernel, [copies[1]], [partial], "between")
    totals = lax.all_to_all(partial, GROUPS[1], 0, 0)
    whole_field = jax.ShapeDtypeStruct((1, 1, RHS, OBS), jnp.float32)
    return call(finish_kernel, [whole_field] * 2, [totals, start, first, second, third], "finish")


def solution(mesh):
    fine = Mesh(mesh.devices.reshape(2, 4, 4, 8, 2), LAT + LON)
    in_specs = (
        P(LAT, LON, None, None),
        P(LAT, LON, None),
        P(LAT, LON, None, None),
        P(LAT, LON, None),
        P(LAT, LON, None),
    )
    out_specs = (P(LAT, LON, None, None), P(LAT, LON, None, None))
    return jax.shard_map(local, mesh=fine, in_specs=in_specs, out_specs=out_specs, check_vma=False)
```

```python
import functools
import math

import jax
import jax.numpy as jnp
from jax import lax
from jax.experimental import pallas as pl
from jax.experimental.pallas import tpu as pltpu
from jax.sharding import Mesh, PartitionSpec as P

ITERS = 3
BANDS = 8
SECTORS = 64
OBS = 512
RHS = 16

LAT_LIMIT = 80.0 * math.pi / 180.0
HORIZ_SQ = 0.05 * 0.05
VERT_SQ = 0.3 * 0.3
TAPER_STEP = 0.45
LOG2E = 1.0 / math.log(2.0)
HORIZ = LOG2E / HORIZ_SQ
VERT = LOG2E / (2.0 * VERT_SQ)
COUPLING = ((1.0, 0.45, 0.45), (0.45, 1.0, 0.25), (0.45, 0.25, 1.0))

LAT = ("z_lo", "x")
LON = ("z_hi", "y", "core")
GROUPS = (("z_lo", "z_hi", "x"), ("y", "core"))


def extent(axes):
    size = 1
    for axis in axes:
        size *= lax.axis_size(axis)
    return size


def pairs(count, first):
    return [[low, (low + 1) % count] for low in range(first, count, 2)]


def partner(block, axes, first):
    both = lax.all_gather(block, axes, axis_index_groups=pairs(extent(axes), first))
    leads = lax.axis_index(axes) % 2 == first
    return jnp.where(leads, both[1], both[0])


def widened(block):
    inner = partner(block, LON, 0)
    inner, block = lax.optimization_barrier((inner, block))
    outer = partner(block, LON, 1)
    return jnp.stack([outer, block, inner])


def all_bands(wide):
    count = extent(LAT)
    below = lax.ppermute(wide, LAT, [(i, i + 1) for i in range(count - 1)])
    above = lax.ppermute(wide, LAT, [(i + 1, i) for i in range(count - 1)])
    return below, above


def all_bands_paired(wide):
    count = extent(LAT)
    swap = lax.ppermute(wide, LAT, [p for a, b in pairs(count, 0) for p in ((a, b), (b, a))])
    return swap, lax.all_gather(wide, LAT, axis_index_groups=pairs(count, 1))


def rounded(value):
    return value.astype(jnp.bfloat16).astype(jnp.float32)


def pieces(value):
    high = rounded(value)
    mid = rounded(value - high)
    return high, mid, rounded(value - high - mid)


def own_side(place, level, kinds, offset):
    one = jnp.ones_like(level)

    def looked_up(column):
        logs = [math.log2(row[column]) for row in COUPLING]
        return logs[0] + kinds[0] * (logs[1] - logs[0]) + kinds[1] * (logs[2] - logs[0])

    at_height = looked_up(0)
    rows = [HORIZ * axis for axis in place for _ in range(3)]
    rows += [2.0 * VERT * level, looked_up(1) - at_height, looked_up(2) - at_height]
    return rows + [one, one, offset + at_height - HORIZ, jnp.zeros_like(level)]


def far_side(place, level, kinds, offset, error):
    rows = [piece for axis in place for piece in pieces(axis)]
    return rows + [level, *kinds, *pieces(offset)[:2], jnp.ones_like(level), error]


def write_own(own_ref, rows_ref, rows):
    for row in range(16):
        rows_ref[row : row + 1, :] = rows[row]
    for step in range(3):
        if step:
            rows_ref[14:15, :] = rows[14] + step * math.log2(TAPER_STEP)
        left = rows_ref[...]
        for piece in range(3):
            part = left.astype(jnp.bfloat16)
            own_ref[step, 16 * piece : 16 * piece + 16, :] = part
            left = left - part.astype(jnp.float32)


def describe_kernel(
    start_ref, error_ref, frac_ref, spread_ref, type_ref,
    message_ref, own_ref, error_out_ref, added_ref, kept_ref, rows_ref,
):
    frac = frac_ref[...].astype(jnp.float32)
    latitude = (lax.axis_index(LAT).astype(jnp.float32) + frac[0:1]) * (2.0 * LAT_LIMIT / BANDS) - LAT_LIMIT
    longitude = (lax.axis_index(LON).astype(jnp.float32) + frac[1:2]) * (2.0 * math.pi / SECTORS)
    angles = jnp.concatenate([latitude, longitude], axis=0)
    cosines, sines = jnp.cos(angles), jnp.sin(angles)
    place = (cosines[0:1] * cosines[1:2], cosines[0:1] * sines[1:2], sines[0:1])
    level = frac[2:3]
    offset = jnp.log(spread_ref[...].astype(jnp.float32)) * LOG2E - VERT * level * level
    kinds = [jnp.where(type_ref[...] == kind, jnp.ones_like(level), 0.0) for kind in (1, 2)]
    far = far_side(place, level, kinds, offset, error_ref[...])
    for row in range(16):
        rows_ref[row : row + 1, :] = far[row]
    message_ref[0:16, :] = start_ref[...].astype(jnp.bfloat16)
    message_ref[16:32, :] = rows_ref[...].astype(jnp.bfloat16)
    error_out_ref[...] = error_ref[...]
    kept_ref[...] = start_ref[...]
    added_ref[...] = error_ref[...] * start_ref[...]
    write_own(own_ref, rows_ref, own_side(place, level, kinds, offset))


def whole(space=pltpu.VMEM):
    return pl.BlockSpec(memory_space=space)


def describe(start, error_var, where_frac, spread, obs_type):
    return pl.pallas_call(
        describe_kernel,
        out_shape=(
            pltpu.VMEM((32, OBS), jnp.bfloat16),
            pltpu.VMEM((3, 48, OBS), jnp.bfloat16),
            pltpu.VMEM((1, OBS), jnp.float32),
            pltpu.VMEM((RHS, OBS), jnp.float32),
            pltpu.VMEM((RHS, OBS), jnp.float32),
        ),
        in_specs=[whole()] * 5,
        out_specs=[whole()] * 5,
        scratch_shapes=[pltpu.VMEM((16, OBS), jnp.float32)],
        name="describe",
    )(start, error_var, where_frac, spread, obs_type)


OWN = (1, 2, 3)
OUTER = (0, 1, 2)


def part_of(columns, steps, near_ref, own_ref, tile_ref):
    for slot, (column, step) in enumerate(zip(columns, steps)):
        far = near_ref[column, 16:32, :]
        far = jnp.concatenate([far, far, far], axis=0)
        power = lax.dot_general(far, own_ref[step], (((0,), (0,)), ((), ())), preferred_element_type=jnp.float32)
        tile_ref[slot] = jnp.exp2(power).astype(jnp.bfloat16)
    return products(lambda slot: near_ref[columns[slot], 0:16, :], tile_ref)


def build_same_kernel(near_ref, own_ref, added_ref, tile_ref, sum_ref, outer_own_ref, outer_sum_ref, rows_ref, scratch_ref):
    rows = near_ref[1, 16:32, :].astype(jnp.float32)
    row = [rows[at : at + 1] for at in range(16)]
    place = [row[3 * axis] + row[3 * axis + 1] + row[3 * axis + 2] for axis in range(3)]
    write_own(outer_own_ref, rows_ref, own_side(place, row[9], row[10:12], row[12] + row[13]))
    sum_ref[...] = added_ref[...] + part_of(OWN, SAME_BAND, near_ref, own_ref, tile_ref)
    outer_added = row[15] * near_ref[1, 0:16, :].astype(jnp.float32)
    outer_sum_ref[...] = outer_added + part_of(OUTER, SAME_BAND, near_ref, outer_own_ref, scratch_ref)


def build_other_kernel(
    near_ref, own_ref, added_ref, outer_own_ref, outer_added_ref, tile_ref, sum_ref, *more
):
    *outer_refs, scratch_ref = more
    total = added_ref[...] + part_of(OWN, OTHER_BAND, near_ref, own_ref, tile_ref)
    outer = outer_added_ref[...] + part_of(OUTER, OTHER_BAND, near_ref, outer_own_ref, scratch_ref)
    sum_ref[...] = total
    if len(outer_refs) == 1:
        outer_refs[0][...] = outer
    else:
        for ref, value in zip(outer_refs, (total, outer)):
            send(ref, value)


def products(field_of, tile_ref):
    total = sum(jnp.dot(field_of(slot), tile_ref[slot], preferred_element_type=jnp.float32) for slot in range(3))
    return total if total.shape[0] == RHS else total[:RHS] + total[RHS:]


def send(ref, value):
    high = value.astype(jnp.bfloat16)
    ref[0:RHS, :] = high
    ref[RHS : 2 * RHS, :] = (value - high.astype(jnp.float32)).astype(jnp.bfloat16)


def apply_kernel(near_ref, tile_ref, added_ref, scale_ref, sum_ref):
    sum_ref[...] = added_ref[...] * scale_ref[...] + products(lambda slot: near_ref[slot], tile_ref)


SAME_BAND = (1, 0, 1)
OTHER_BAND = (2, 1, 2)


def cost(built):
    entries = 3 * OBS * OBS
    return pl.CostEstimate(
        flops=2 * entries * (RHS + 256 * built),
        bytes_accessed=2 * entries,
        transcendentals=entries * built,
    )


FIELD = pltpu.VMEM((RHS, OBS), jnp.float32)
SENT = pltpu.VMEM((2 * RHS, OBS), jnp.bfloat16)
TILES = pltpu.VMEM((3, OBS, OBS), jnp.bfloat16)
OWN_SIDE = pltpu.VMEM((3, 48, OBS), jnp.bfloat16)


def build(kernel, shapes, operands, scratch):
    return pl.pallas_call(
        kernel,
        out_shape=shapes,
        in_specs=[whole()] * len(operands),
        out_specs=[whole()] * len(shapes),
        scratch_shapes=scratch,
        compiler_params=pltpu.CompilerParams(vmem_limit_bytes=16 << 20),
        cost_estimate=cost(2),
        name="build",
    )(*operands)


def coefficients(gram):
    def inner(left, right):
        total = 0.0
        for i in range(4):
            for j in range(4):
                if left[i] is not None and right[j] is not None:
                    total = total + left[i] * right[j] * gram[min(i, j), max(i, j)]
        return total

    def axpy(scale, added, start):
        out = []
        for a, s in zip(added, start):
            if a is None:
                out.append(s)
            else:
                out.append(scale * a if s is None else s + scale * a)
        return out

    one = jnp.ones_like(gram[0, 0])
    answer = [None] * 4
    residual = [one, None, None, None]
    direction = residual
    norm_now = gram[0, 0]
    for iteration in range(ITERS):
        image = [None] + direction[:3]
        step_len = norm_now / inner(direction, image)
        answer = axpy(step_len, direction, answer)
        residual = axpy(-step_len, image, residual)
        if iteration < ITERS - 1:
            norm_next = inner(residual, residual)
            direction = axpy(norm_next / norm_now, direction, residual)
            norm_now = norm_next
    return answer[:3], residual


def lane_sums(products):
    empty = jnp.zeros((128 - RHS * len(products), OBS), jnp.float32)
    stacked = jnp.concatenate([*products, empty], axis=0) if len(products) < 8 else jnp.concatenate(products, axis=0)
    ones = jnp.ones((8, OBS), jnp.bfloat16)
    total = 0.0
    for part in pieces(stacked):
        total = total + lax.dot_general(
            ones, part.astype(jnp.bfloat16), (((1,), (1,)), ((), ())), preferred_element_type=jnp.float32
        )
    return total[0:1]


MOMENTS = 6


def same_band_kernel(near_ref, tile_ref, second_ref, scale_ref, start_ref, first_ref, sum_ref, row_ref):
    start, first, second = start_ref[...], first_ref[...], second_ref[...]
    sum_ref[...] = second * scale_ref[...] + products(lambda slot: near_ref[slot], tile_ref)
    row_ref[...] = lane_sums(
        [start * start, start * first, first * first, start * second, first * second, second * second]
    )


def below_kernel(near_ref, tile_ref, part_ref, second_ref, row_ref, sum_ref, copies_ref):
    part = part_ref[...]
    total = part + products(lambda slot: near_ref[slot], tile_ref)
    sum_ref[...] = total
    product = second_ref[...] * (2.0 * total - part)
    before = [jnp.zeros_like(product)] * MOMENTS
    row = row_ref[...] + lane_sums([*before, product])
    copies_ref[...] = jnp.broadcast_to(row[None], copies_ref.shape)


def paired_kernel(swap_ref, both_ref, below_ref, above_ref, part_ref, sum_ref, sent_ref):
    band = lax.axis_index(LAT)
    inside = jnp.where((band == 0) | (band == BANDS - 1), 0.0, 1.0)

    def add(swap_tiles, both_tiles, position):
        total = part_ref[...] + products(lambda slot: swap_ref[slot], swap_tiles)
        total = total + inside * products(lambda slot: both_ref[position, slot], both_tiles)
        sum_ref[...] = total
        send(sent_ref, total)

    @pl.when(band % 2 == 1)
    def _():
        add(below_ref, above_ref, 1)

    @pl.when(band % 2 == 0)
    def _():
        add(above_ref, below_ref, 0)


def above_kernel(near_ref, total_ref, tile_ref, lower_ref, third_ref, copies_ref):
    third_ref[...] = lower_ref[...] + products(lambda slot: near_ref[slot], tile_ref)
    copies_ref[...] = jnp.broadcast_to(jnp.sum(total_ref[...], axis=0)[None], copies_ref.shape)


def finish_kernel(total_ref, start_ref, first_ref, second_ref, third_ref, answer_ref, residual_ref):
    totals = jnp.broadcast_to(jnp.sum(total_ref[...], axis=0), (RHS, 128))
    lane = lax.broadcasted_iota(jnp.int32, (RHS, 128), 1)
    row = lax.broadcasted_iota(jnp.int32, (RHS, 128), 0)
    moments = [
        jnp.sum(jnp.where(lane == row + RHS * at, totals, 0.0), axis=1, keepdims=True) for at in range(MOMENTS + 1)
    ]
    names = {(0, 0): 0, (0, 1): 1, (1, 1): 2, (0, 2): 3, (1, 2): 4, (2, 2): 5, (2, 3): 6, (0, 3): 4, (1, 3): 5}
    answer, residual = coefficients({pair: moments[at] for pair, at in names.items()})
    basis = (start_ref[...], first_ref[...], second_ref[...], third_ref[...])
    answer_ref[0, 0] = sum(c * v for c, v in zip(answer, basis))
    residual_ref[0, 0] = sum(c * v for c, v in zip(residual, basis))


def call(kernel, shapes, operands, name):
    return pl.pallas_call(
        kernel,
        out_shape=shapes,
        in_specs=[whole()] * len(operands),
        out_specs=[whole()] * len(shapes),
        compiler_params=pltpu.CompilerParams(vmem_limit_bytes=16 << 20),
        cost_estimate=cost(0),
        name=name,
    )(*operands)


def local(innovations, obs_error, where_frac, spread, obs_type):
    message, own, error_var, added, start = describe(
        innovations[0, 0], obs_error[0], where_frac[0, 0], spread[0], obs_type[0]
    )
    inner = partner(message, LON, 0)
    outer = partner(jnp.stack([message, inner]), LON, 1)
    wide = jnp.stack([outer[1], outer[0], message, inner])
    below, above = all_bands(wide)
    tiles, part, outer_own, outer = build(
        build_same_kernel,
        [TILES, FIELD, OWN_SIDE, FIELD],
        [wide, own, added],
        [pltpu.VMEM((16, OBS), jnp.float32), TILES],
    )
    tiles_below, part, outer = build(
        build_other_kernel, [TILES, FIELD, FIELD], [below, own, part, outer_own, outer], [TILES]
    )
    tiles_above, first, sent, outer_sent = build(
        build_other_kernel, [TILES, FIELD, SENT, SENT], [above, own, part, outer_own, outer], [TILES]
    )
    wide = jnp.stack([outer_sent, sent, partner(sent, LON, 0)])
    swap, both = all_bands_paired(wide)
    part, = call(apply_kernel, [FIELD], [wide, tiles, first, error_var], "apply")
    field = FIELD
    second, sent = call(
        paired_kernel,
        [field, SENT],
        [swap, both, tiles_below, tiles_above, part],
        "paired",
    )
    wide = widened(sent)
    below, above = all_bands(wide)
    part, row = call(
        same_band_kernel,
        [field, pltpu.VMEM((1, 128), jnp.float32)],
        [wide, tiles, second, error_var, start, first],
        "same_band",
    )
    copies = [pltpu.VMEM((extent(axes), 1, 128), jnp.float32) for axes in GROUPS]
    lower, partial = call(below_kernel, [field, copies[0]], [below, tiles_below, part, second, row], "below")
    partial = lax.all_to_all(partial, GROUPS[0], 0, 0)
    third, partial = call(above_kernel, [field, copies[1]], [above, partial, tiles_above, lower], "above")
    totals = lax.all_to_all(partial, GROUPS[1], 0, 0)
    whole_field = jax.ShapeDtypeStruct((1, 1, RHS, OBS), jnp.float32)
    return call(finish_kernel, [whole_field] * 2, [totals, start, first, second, third], "finish")


def solution(mesh):
    fine = Mesh(mesh.devices.reshape(2, 4, 4, 8, 2), LAT + LON)
    in_specs = (
        P(LAT, LON, None, None),
        P(LAT, LON, None),
        P(LAT, LON, None, None),
        P(LAT, LON, None),
        P(LAT, LON, None),
    )
    out_specs = (P(LAT, LON, None, None), P(LAT, LON, None, None))
    return jax.shard_map(local, mesh=fine, in_specs=in_specs, out_specs=out_specs, check_vma=False)
```

```python
import functools
import math

import jax
import jax.numpy as jnp
from jax import lax
from jax.experimental import pallas as pl
from jax.experimental.pallas import tpu as pltpu
from jax.sharding import Mesh, PartitionSpec as P

ITERS = 3
BANDS = 8
SECTORS = 64
OBS = 512
RHS = 16

LAT_LIMIT = 80.0 * math.pi / 180.0
HORIZ_SQ = 0.05 * 0.05
VERT_SQ = 0.3 * 0.3
TAPER_STEP = 0.45
LOG2E = 1.0 / math.log(2.0)
HORIZ = LOG2E / HORIZ_SQ
VERT = LOG2E / (2.0 * VERT_SQ)
COUPLING = ((1.0, 0.45, 0.45), (0.45, 1.0, 0.25), (0.45, 0.25, 1.0))

LAT = ("z_lo", "x")
LON = ("z_hi", "y", "core")
GROUPS = (("z_lo", "z_hi", "x"), ("y", "core"))


def extent(axes):
    size = 1
    for axis in axes:
        size *= lax.axis_size(axis)
    return size


def pairs(count, first):
    return [[low, (low + 1) % count] for low in range(first, count, 2)]


def partner(block, axes, first):
    both = lax.all_gather(block, axes, axis_index_groups=pairs(extent(axes), first))
    leads = lax.axis_index(axes) % 2 == first
    return jnp.where(leads, both[1], both[0])


def widened(block):
    inner = partner(block, LON, 0)
    inner, block = lax.optimization_barrier((inner, block))
    outer = partner(block, LON, 1)
    return jnp.stack([outer, block, inner])


def all_bands(wide):
    count = extent(LAT)
    below = lax.ppermute(wide, LAT, [(i, i + 1) for i in range(count - 1)])
    above = lax.ppermute(wide, LAT, [(i + 1, i) for i in range(count - 1)])
    return below, above


def rounded(value):
    return value.astype(jnp.bfloat16).astype(jnp.float32)


def pieces(value):
    high = rounded(value)
    mid = rounded(value - high)
    return high, mid, rounded(value - high - mid)


def own_side(place, level, kinds, offset):
    one = jnp.ones_like(level)

    def looked_up(column):
        logs = [math.log2(row[column]) for row in COUPLING]
        return logs[0] + kinds[0] * (logs[1] - logs[0]) + kinds[1] * (logs[2] - logs[0])

    at_height = looked_up(0)
    rows = [HORIZ * axis for axis in place for _ in range(3)]
    rows += [2.0 * VERT * level, looked_up(1) - at_height, looked_up(2) - at_height]
    return rows + [one, one, offset + at_height - HORIZ, jnp.zeros_like(level)]


def far_side(place, level, kinds, offset, error):
    rows = [piece for axis in place for piece in pieces(axis)]
    return rows + [level, *kinds, *pieces(offset)[:2], jnp.ones_like(level), error]


def write_own(own_ref, rows_ref, rows):
    for row in range(16):
        rows_ref[row : row + 1, :] = rows[row]
    for step in range(3):
        if step:
            rows_ref[14:15, :] = rows[14] + step * math.log2(TAPER_STEP)
        left = rows_ref[...]
        for piece in range(3):
            part = left.astype(jnp.bfloat16)
            own_ref[step, 16 * piece : 16 * piece + 16, :] = part
            left = left - part.astype(jnp.float32)


def describe_kernel(
    start_ref, error_ref, frac_ref, spread_ref, type_ref,
    message_ref, own_ref, error_out_ref, added_ref, kept_ref, rows_ref,
):
    frac = frac_ref[...].astype(jnp.float32)
    latitude = (lax.axis_index(LAT).astype(jnp.float32) + frac[0:1]) * (2.0 * LAT_LIMIT / BANDS) - LAT_LIMIT
    longitude = (lax.axis_index(LON).astype(jnp.float32) + frac[1:2]) * (2.0 * math.pi / SECTORS)
    angles = jnp.concatenate([latitude, longitude], axis=0)
    cosines, sines = jnp.cos(angles), jnp.sin(angles)
    place = (cosines[0:1] * cosines[1:2], cosines[0:1] * sines[1:2], sines[0:1])
    level = frac[2:3]
    offset = jnp.log(spread_ref[...].astype(jnp.float32)) * LOG2E - VERT * level * level
    kinds = [jnp.where(type_ref[...] == kind, jnp.ones_like(level), 0.0) for kind in (1, 2)]
    far = far_side(place, level, kinds, offset, error_ref[...])
    for row in range(16):
        rows_ref[row : row + 1, :] = far[row]
    message_ref[0:16, :] = start_ref[...].astype(jnp.bfloat16)
    message_ref[16:32, :] = rows_ref[...].astype(jnp.bfloat16)
    error_out_ref[...] = error_ref[...]
    kept_ref[...] = start_ref[...]
    added_ref[...] = error_ref[...] * start_ref[...]
    write_own(own_ref, rows_ref, own_side(place, level, kinds, offset))


def whole(space=pltpu.VMEM):
    return pl.BlockSpec(memory_space=space)


def describe(start, error_var, where_frac, spread, obs_type):
    return pl.pallas_call(
        describe_kernel,
        out_shape=(
            pltpu.VMEM((32, OBS), jnp.bfloat16),
            pltpu.VMEM((3, 48, OBS), jnp.bfloat16),
            pltpu.VMEM((1, OBS), jnp.float32),
            pltpu.VMEM((RHS, OBS), jnp.float32),
            pltpu.VMEM((RHS, OBS), jnp.float32),
        ),
        in_specs=[whole()] * 5,
        out_specs=[whole()] * 5,
        scratch_shapes=[pltpu.VMEM((16, OBS), jnp.float32)],
        name="describe",
    )(start, error_var, where_frac, spread, obs_type)


OWN = (1, 2, 3)
OUTER = (0, 1, 2)


def part_of(columns, steps, near_ref, own_ref, tile_ref):
    for slot, (column, step) in enumerate(zip(columns, steps)):
        far = near_ref[column, 16:32, :]
        far = jnp.concatenate([far, far, far], axis=0)
        power = lax.dot_general(far, own_ref[step], (((0,), (0,)), ((), ())), preferred_element_type=jnp.float32)
        tile_ref[slot] = jnp.exp2(power).astype(jnp.bfloat16)
    return products(lambda slot: near_ref[columns[slot], 0:16, :], tile_ref)


def build_same_kernel(near_ref, own_ref, added_ref, tile_ref, sum_ref, outer_own_ref, outer_sum_ref, rows_ref, scratch_ref):
    rows = near_ref[1, 16:32, :].astype(jnp.float32)
    row = [rows[at : at + 1] for at in range(16)]
    place = [row[3 * axis] + row[3 * axis + 1] + row[3 * axis + 2] for axis in range(3)]
    write_own(outer_own_ref, rows_ref, own_side(place, row[9], row[10:12], row[12] + row[13]))
    sum_ref[...] = added_ref[...] + part_of(OWN, SAME_BAND, near_ref, own_ref, tile_ref)
    outer_added = row[15] * near_ref[1, 0:16, :].astype(jnp.float32)
    outer_sum_ref[...] = outer_added + part_of(OUTER, SAME_BAND, near_ref, outer_own_ref, scratch_ref)


def build_other_kernel(
    near_ref, own_ref, added_ref, outer_own_ref, outer_added_ref, tile_ref, sum_ref, *more
):
    *outer_refs, scratch_ref = more
    total = added_ref[...] + part_of(OWN, OTHER_BAND, near_ref, own_ref, tile_ref)
    outer = outer_added_ref[...] + part_of(OUTER, OTHER_BAND, near_ref, outer_own_ref, scratch_ref)
    sum_ref[...] = total
    if len(outer_refs) == 1:
        outer_refs[0][...] = outer
    else:
        for ref, value in zip(outer_refs, (total, outer)):
            send(ref, value)


def products(field_of, tile_ref):
    total = sum(jnp.dot(field_of(slot), tile_ref[slot], preferred_element_type=jnp.float32) for slot in range(3))
    return total if total.shape[0] == RHS else total[:RHS] + total[RHS:]


def send(ref, value):
    high = value.astype(jnp.bfloat16)
    ref[0:RHS, :] = high
    ref[RHS : 2 * RHS, :] = (value - high.astype(jnp.float32)).astype(jnp.bfloat16)


def apply_kernel(near_ref, tile_ref, added_ref, *refs):
    *scale, sum_ref = refs
    added = added_ref[...] * scale[0][...] if scale else added_ref[...]
    sum_ref[...] = added + products(lambda slot: near_ref[slot], tile_ref)


SAME_BAND = (1, 0, 1)
OTHER_BAND = (2, 1, 2)


def cost(built):
    entries = 3 * OBS * OBS
    return pl.CostEstimate(
        flops=2 * entries * (RHS + 256 * built),
        bytes_accessed=2 * entries,
        transcendentals=entries * built,
    )


FIELD = pltpu.VMEM((RHS, OBS), jnp.float32)
SENT = pltpu.VMEM((2 * RHS, OBS), jnp.bfloat16)
TILES = pltpu.VMEM((3, OBS, OBS), jnp.bfloat16)
OWN_SIDE = pltpu.VMEM((3, 48, OBS), jnp.bfloat16)


def build(kernel, shapes, operands, scratch):
    return pl.pallas_call(
        kernel,
        out_shape=shapes,
        in_specs=[whole()] * len(operands),
        out_specs=[whole()] * len(shapes),
        scratch_shapes=scratch,
        compiler_params=pltpu.CompilerParams(vmem_limit_bytes=16 << 20),
        cost_estimate=cost(2),
        name="build",
    )(*operands)


def coefficients(gram):
    def inner(left, right):
        total = 0.0
        for i in range(4):
            for j in range(4):
                if left[i] is not None and right[j] is not None:
                    total = total + left[i] * right[j] * gram[min(i, j), max(i, j)]
        return total

    def axpy(scale, added, start):
        out = []
        for a, s in zip(added, start):
            if a is None:
                out.append(s)
            else:
                out.append(scale * a if s is None else s + scale * a)
        return out

    one = jnp.ones_like(gram[0, 0])
    answer = [None] * 4
    residual = [one, None, None, None]
    direction = residual
    norm_now = gram[0, 0]
    for iteration in range(ITERS):
        image = [None] + direction[:3]
        step_len = norm_now / inner(direction, image)
        answer = axpy(step_len, direction, answer)
        residual = axpy(-step_len, image, residual)
        if iteration < ITERS - 1:
            norm_next = inner(residual, residual)
            direction = axpy(norm_next / norm_now, direction, residual)
            norm_now = norm_next
    return answer[:3], residual


def lane_sums(products):
    empty = jnp.zeros((128 - RHS * len(products), OBS), jnp.float32)
    stacked = jnp.concatenate([*products, empty], axis=0) if len(products) < 8 else jnp.concatenate(products, axis=0)
    ones = jnp.ones((8, OBS), jnp.bfloat16)
    total = 0.0
    for part in pieces(stacked):
        total = total + lax.dot_general(
            ones, part.astype(jnp.bfloat16), (((1,), (1,)), ((), ())), preferred_element_type=jnp.float32
        )
    return total[0:1]


MOMENTS = 6


def same_band_kernel(near_ref, tile_ref, second_ref, scale_ref, start_ref, first_ref, sum_ref, row_ref):
    start, first, second = start_ref[...], first_ref[...], second_ref[...]
    sum_ref[...] = second * scale_ref[...] + products(lambda slot: near_ref[slot], tile_ref)
    row_ref[...] = lane_sums(
        [start * start, start * first, first * first, start * second, first * second, second * second]
    )


def below_kernel(near_ref, tile_ref, part_ref, second_ref, row_ref, sum_ref, copies_ref):
    part = part_ref[...]
    total = part + products(lambda slot: near_ref[slot], tile_ref)
    sum_ref[...] = total
    product = second_ref[...] * (2.0 * total - part)
    before = [jnp.zeros_like(product)] * MOMENTS
    row = row_ref[...] + lane_sums([*before, product])
    copies_ref[...] = jnp.broadcast_to(row[None], copies_ref.shape)


def second_kernel(near_ref, tile_ref, part_ref, sum_ref, sent_ref):
    total = part_ref[...] + products(lambda slot: near_ref[slot], tile_ref)
    sum_ref[...] = total
    send(sent_ref, total)


def above_kernel(near_ref, total_ref, tile_ref, lower_ref, third_ref, copies_ref):
    third_ref[...] = lower_ref[...] + products(lambda slot: near_ref[slot], tile_ref)
    copies_ref[...] = jnp.broadcast_to(jnp.sum(total_ref[...], axis=0)[None], copies_ref.shape)


def finish_kernel(total_ref, start_ref, first_ref, second_ref, third_ref, answer_ref, residual_ref):
    totals = jnp.broadcast_to(jnp.sum(total_ref[...], axis=0), (RHS, 128))
    lane = lax.broadcasted_iota(jnp.int32, (RHS, 128), 1)
    row = lax.broadcasted_iota(jnp.int32, (RHS, 128), 0)
    moments = [
        jnp.sum(jnp.where(lane == row + RHS * at, totals, 0.0), axis=1, keepdims=True) for at in range(MOMENTS + 1)
    ]
    names = {(0, 0): 0, (0, 1): 1, (1, 1): 2, (0, 2): 3, (1, 2): 4, (2, 2): 5, (2, 3): 6, (0, 3): 4, (1, 3): 5}
    answer, residual = coefficients({pair: moments[at] for pair, at in names.items()})
    basis = (start_ref[...], first_ref[...], second_ref[...], third_ref[...])
    answer_ref[0, 0] = sum(c * v for c, v in zip(answer, basis))
    residual_ref[0, 0] = sum(c * v for c, v in zip(residual, basis))


def call(kernel, shapes, operands, name):
    return pl.pallas_call(
        kernel,
        out_shape=shapes,
        in_specs=[whole()] * len(operands),
        out_specs=[whole()] * len(shapes),
        compiler_params=pltpu.CompilerParams(vmem_limit_bytes=16 << 20),
        cost_estimate=cost(0),
        name=name,
    )(*operands)


def local(innovations, obs_error, where_frac, spread, obs_type):
    message, own, error_var, added, start = describe(
        innovations[0, 0], obs_error[0], where_frac[0, 0], spread[0], obs_type[0]
    )
    inner = partner(message, LON, 0)
    outer = partner(jnp.stack([message, inner]), LON, 1)
    wide = jnp.stack([outer[1], outer[0], message, inner])
    below, above = all_bands(wide)
    tiles, part, outer_own, outer = build(
        build_same_kernel,
        [TILES, FIELD, OWN_SIDE, FIELD],
        [wide, own, added],
        [pltpu.VMEM((16, OBS), jnp.float32), TILES],
    )
    tiles_below, part, outer = build(
        build_other_kernel, [TILES, FIELD, FIELD], [below, own, part, outer_own, outer], [TILES]
    )
    tiles_above, first, sent, outer_sent = build(
        build_other_kernel, [TILES, FIELD, SENT, SENT], [above, own, part, outer_own, outer], [TILES]
    )
    wide = jnp.stack([outer_sent, sent, partner(sent, LON, 0)])
    below, above = all_bands(wide)
    field = FIELD
    part, = call(apply_kernel, [field], [wide, tiles, first, error_var], "apply")
    part, = call(apply_kernel, [field], [below, tiles_below, part], "apply")
    second, sent = call(second_kernel, [field, SENT], [above, tiles_above, part], "second")
    wide = widened(sent)
    below, above = all_bands(wide)
    part, row = call(
        same_band_kernel,
        [field, pltpu.VMEM((1, 128), jnp.float32)],
        [wide, tiles, second, error_var, start, first],
        "same_band",
    )
    copies = [pltpu.VMEM((extent(axes), 1, 128), jnp.float32) for axes in GROUPS]
    lower, partial = call(below_kernel, [field, copies[0]], [below, tiles_below, part, second, row], "below")
    partial = lax.all_to_all(partial, GROUPS[0], 0, 0)
    third, partial = call(above_kernel, [field, copies[1]], [above, partial, tiles_above, lower], "above")
    totals = lax.all_to_all(partial, GROUPS[1], 0, 0)
    whole_field = jax.ShapeDtypeStruct((1, 1, RHS, OBS), jnp.float32)
    return call(finish_kernel, [whole_field] * 2, [totals, start, first, second, third], "finish")


def solution(mesh):
    fine = Mesh(mesh.devices.reshape(2, 4, 4, 8, 2), LAT + LON)
    in_specs = (
        P(LAT, LON, None, None),
        P(LAT, LON, None),
        P(LAT, LON, None, None),
        P(LAT, LON, None),
        P(LAT, LON, None),
    )
    out_specs = (P(LAT, LON, None, None), P(LAT, LON, None, None))
    return jax.shard_map(local, mesh=fine, in_specs=in_specs, out_specs=out_specs, check_vma=False)
```

```python
import functools
import math

import jax
import jax.numpy as jnp
from jax import lax
from jax.experimental import pallas as pl
from jax.experimental.pallas import tpu as pltpu
from jax.sharding import Mesh, PartitionSpec as P

ITERS = 3
BANDS = 8
SECTORS = 64
OBS = 512
RHS = 16

LAT_LIMIT = 80.0 * math.pi / 180.0
HORIZ_SQ = 0.05 * 0.05
VERT_SQ = 0.3 * 0.3
TAPER_STEP = 0.45
LOG2E = 1.0 / math.log(2.0)
HORIZ = LOG2E / HORIZ_SQ
VERT = LOG2E / (2.0 * VERT_SQ)
COUPLING = ((1.0, 0.45, 0.45), (0.45, 1.0, 0.25), (0.45, 0.25, 1.0))

LAT = ("z_lo", "x")
LON = ("z_hi", "y", "core")
GROUPS = (("z_lo", "z_hi", "x"), ("y", "core"))


def extent(axes):
    size = 1
    for axis in axes:
        size *= lax.axis_size(axis)
    return size


def pairs(count, first):
    return [[low, (low + 1) % count] for low in range(first, count, 2)]


def partner(block, axes, first):
    both = lax.all_gather(block, axes, axis_index_groups=pairs(extent(axes), first))
    leads = lax.axis_index(axes) % 2 == first
    return jnp.where(leads, both[1], both[0])


def widened(block):
    inner = partner(block, LON, 0)
    inner, block = lax.optimization_barrier((inner, block))
    outer = partner(block, LON, 1)
    return jnp.stack([outer, block, inner])


def all_bands(wide):
    count = extent(LAT)
    below = lax.ppermute(wide, LAT, [(i, i + 1) for i in range(count - 1)])
    above = lax.ppermute(wide, LAT, [(i + 1, i) for i in range(count - 1)])
    return below, above


def all_bands_paired(wide):
    count = extent(LAT)
    swap = lax.ppermute(wide, LAT, [p for a, b in pairs(count - 1, 1) for p in ((a, b), (b, a))])
    return swap, lax.all_gather(wide, LAT, axis_index_groups=pairs(count, 0))


def rounded(value):
    return value.astype(jnp.bfloat16).astype(jnp.float32)


def pieces(value):
    high = rounded(value)
    mid = rounded(value - high)
    return high, mid, rounded(value - high - mid)


def own_side(place, level, kinds, offset):
    one = jnp.ones_like(level)

    def looked_up(column):
        logs = [math.log2(row[column]) for row in COUPLING]
        return logs[0] + kinds[0] * (logs[1] - logs[0]) + kinds[1] * (logs[2] - logs[0])

    at_height = looked_up(0)
    rows = [HORIZ * axis for axis in place for _ in range(3)]
    rows += [2.0 * VERT * level, looked_up(1) - at_height, looked_up(2) - at_height]
    return rows + [one, one, offset + at_height - HORIZ, jnp.zeros_like(level)]


def far_side(place, level, kinds, offset, error):
    rows = [piece for axis in place for piece in pieces(axis)]
    return rows + [level, *kinds, *pieces(offset)[:2], jnp.ones_like(level), error]


def write_own(own_ref, rows_ref, rows):
    for row in range(16):
        rows_ref[row : row + 1, :] = rows[row]
    for step in range(3):
        if step:
            rows_ref[14:15, :] = rows[14] + step * math.log2(TAPER_STEP)
        left = rows_ref[...]
        for piece in range(3):
            part = left.astype(jnp.bfloat16)
            own_ref[step, 16 * piece : 16 * piece + 16, :] = part
            left = left - part.astype(jnp.float32)


def describe_kernel(
    start_ref, error_ref, frac_ref, spread_ref, type_ref,
    message_ref, own_ref, error_out_ref, added_ref, kept_ref, rows_ref,
):
    frac = frac_ref[...].astype(jnp.float32)
    latitude = (lax.axis_index(LAT).astype(jnp.float32) + frac[0:1]) * (2.0 * LAT_LIMIT / BANDS) - LAT_LIMIT
    longitude = (lax.axis_index(LON).astype(jnp.float32) + frac[1:2]) * (2.0 * math.pi / SECTORS)
    angles = jnp.concatenate([latitude, longitude], axis=0)
    cosines, sines = jnp.cos(angles), jnp.sin(angles)
    place = (cosines[0:1] * cosines[1:2], cosines[0:1] * sines[1:2], sines[0:1])
    level = frac[2:3]
    offset = jnp.log(spread_ref[...].astype(jnp.float32)) * LOG2E - VERT * level * level
    kinds = [jnp.where(type_ref[...] == kind, jnp.ones_like(level), 0.0) for kind in (1, 2)]
    far = far_side(place, level, kinds, offset, error_ref[...])
    for row in range(16):
        rows_ref[row : row + 1, :] = far[row]
    message_ref[0:16, :] = start_ref[...].astype(jnp.bfloat16)
    message_ref[16:32, :] = rows_ref[...].astype(jnp.bfloat16)
    error_out_ref[...] = error_ref[...]
    kept_ref[...] = start_ref[...]
    added_ref[...] = error_ref[...] * start_ref[...]
    write_own(own_ref, rows_ref, own_side(place, level, kinds, offset))


def whole(space=pltpu.VMEM):
    return pl.BlockSpec(memory_space=space)


def describe(start, error_var, where_frac, spread, obs_type):
    return pl.pallas_call(
        describe_kernel,
        out_shape=(
            pltpu.VMEM((32, OBS), jnp.bfloat16),
            pltpu.VMEM((3, 48, OBS), jnp.bfloat16),
            pltpu.VMEM((1, OBS), jnp.float32),
            pltpu.VMEM((RHS, OBS), jnp.float32),
            pltpu.VMEM((RHS, OBS), jnp.float32),
        ),
        in_specs=[whole()] * 5,
        out_specs=[whole()] * 5,
        scratch_shapes=[pltpu.VMEM((16, OBS), jnp.float32)],
        name="describe",
    )(start, error_var, where_frac, spread, obs_type)


OWN = (1, 2, 3)
OUTER = (0, 1, 2)


def part_of(columns, steps, near_ref, own_ref, tile_ref):
    for slot, (column, step) in enumerate(zip(columns, steps)):
        far = near_ref[column, 16:32, :]
        far = jnp.concatenate([far, far, far], axis=0)
        power = lax.dot_general(far, own_ref[step], (((0,), (0,)), ((), ())), preferred_element_type=jnp.float32)
        tile_ref[slot] = jnp.exp2(power).astype(jnp.bfloat16)
    return products(lambda slot: near_ref[columns[slot], 0:16, :], tile_ref)


def build_same_kernel(near_ref, own_ref, added_ref, tile_ref, sum_ref, outer_own_ref, outer_sum_ref, rows_ref, scratch_ref):
    rows = near_ref[1, 16:32, :].astype(jnp.float32)
    row = [rows[at : at + 1] for at in range(16)]
    place = [row[3 * axis] + row[3 * axis + 1] + row[3 * axis + 2] for axis in range(3)]
    write_own(outer_own_ref, rows_ref, own_side(place, row[9], row[10:12], row[12] + row[13]))
    sum_ref[...] = added_ref[...] + part_of(OWN, SAME_BAND, near_ref, own_ref, tile_ref)
    outer_added = row[15] * near_ref[1, 0:16, :].astype(jnp.float32)
    outer_sum_ref[...] = outer_added + part_of(OUTER, SAME_BAND, near_ref, outer_own_ref, scratch_ref)


def build_other_kernel(
    near_ref, own_ref, added_ref, outer_own_ref, outer_added_ref, tile_ref, sum_ref, *more
):
    *outer_refs, scratch_ref = more
    total = added_ref[...] + part_of(OWN, OTHER_BAND, near_ref, own_ref, tile_ref)
    outer = outer_added_ref[...] + part_of(OUTER, OTHER_BAND, near_ref, outer_own_ref, scratch_ref)
    sum_ref[...] = total
    if len(outer_refs) == 1:
        outer_refs[0][...] = outer
    else:
        for ref, value in zip(outer_refs, (total, outer)):
            send(ref, value)


def products(field_of, tile_ref):
    total = sum(jnp.dot(field_of(slot), tile_ref[slot], preferred_element_type=jnp.float32) for slot in range(3))
    return total if total.shape[0] == RHS else total[:RHS] + total[RHS:]


def send(ref, value):
    high = value.astype(jnp.bfloat16)
    ref[0:RHS, :] = high
    ref[RHS : 2 * RHS, :] = (value - high.astype(jnp.float32)).astype(jnp.bfloat16)


def apply_kernel(near_ref, tile_ref, added_ref, scale_ref, sum_ref):
    sum_ref[...] = added_ref[...] * scale_ref[...] + products(lambda slot: near_ref[slot], tile_ref)


SAME_BAND = (1, 0, 1)
OTHER_BAND = (2, 1, 2)


def cost(built):
    entries = 3 * OBS * OBS
    return pl.CostEstimate(
        flops=2 * entries * (RHS + 256 * built),
        bytes_accessed=2 * entries,
        transcendentals=entries * built,
    )


FIELD = pltpu.VMEM((RHS, OBS), jnp.float32)
SENT = pltpu.VMEM((2 * RHS, OBS), jnp.bfloat16)
TILES = pltpu.VMEM((3, OBS, OBS), jnp.bfloat16)
OWN_SIDE = pltpu.VMEM((3, 48, OBS), jnp.bfloat16)


def build(kernel, shapes, operands, scratch):
    return pl.pallas_call(
        kernel,
        out_shape=shapes,
        in_specs=[whole()] * len(operands),
        out_specs=[whole()] * len(shapes),
        scratch_shapes=scratch,
        compiler_params=pltpu.CompilerParams(vmem_limit_bytes=16 << 20),
        cost_estimate=cost(2),
        name="build",
    )(*operands)


def coefficients(gram):
    def inner(left, right):
        total = 0.0
        for i in range(4):
            for j in range(4):
                if left[i] is not None and right[j] is not None:
                    total = total + left[i] * right[j] * gram[min(i, j), max(i, j)]
        return total

    def axpy(scale, added, start):
        out = []
        for a, s in zip(added, start):
            if a is None:
                out.append(s)
            else:
                out.append(scale * a if s is None else s + scale * a)
        return out

    one = jnp.ones_like(gram[0, 0])
    answer = [None] * 4
    residual = [one, None, None, None]
    direction = residual
    norm_now = gram[0, 0]
    for iteration in range(ITERS):
        image = [None] + direction[:3]
        step_len = norm_now / inner(direction, image)
        answer = axpy(step_len, direction, answer)
        residual = axpy(-step_len, image, residual)
        if iteration < ITERS - 1:
            norm_next = inner(residual, residual)
            direction = axpy(norm_next / norm_now, direction, residual)
            norm_now = norm_next
    return answer[:3], residual


def lane_sums(products):
    empty = jnp.zeros((128 - RHS * len(products), OBS), jnp.float32)
    stacked = jnp.concatenate([*products, empty], axis=0) if len(products) < 8 else jnp.concatenate(products, axis=0)
    ones = jnp.ones((8, OBS), jnp.bfloat16)
    total = 0.0
    for part in pieces(stacked):
        total = total + lax.dot_general(
            ones, part.astype(jnp.bfloat16), (((1,), (1,)), ((), ())), preferred_element_type=jnp.float32
        )
    return total[0:1]


MOMENTS = 6


def same_band_kernel(near_ref, tile_ref, second_ref, scale_ref, start_ref, first_ref, sum_ref, row_ref):
    start, first, second = start_ref[...], first_ref[...], second_ref[...]
    sum_ref[...] = second * scale_ref[...] + products(lambda slot: near_ref[slot], tile_ref)
    row_ref[...] = lane_sums(
        [start * start, start * first, first * first, start * second, first * second, second * second]
    )


def below_kernel(near_ref, tile_ref, part_ref, second_ref, row_ref, sum_ref, copies_ref):
    part = part_ref[...]
    total = part + products(lambda slot: near_ref[slot], tile_ref)
    sum_ref[...] = total
    product = second_ref[...] * (2.0 * total - part)
    before = [jnp.zeros_like(product)] * MOMENTS
    row = row_ref[...] + lane_sums([*before, product])
    copies_ref[...] = jnp.broadcast_to(row[None], copies_ref.shape)


def paired_kernel(swap_ref, both_ref, below_ref, above_ref, part_ref, sum_ref, sent_ref):
    odd = lax.axis_index(LAT) % 2

    def add(swap_tiles, both_tiles, position):
        total = part_ref[...] + products(lambda slot: swap_ref[slot], swap_tiles)
        total = total + products(lambda slot: both_ref[position, slot], both_tiles)
        sum_ref[...] = total
        send(sent_ref, total)

    @pl.when(odd == 1)
    def _():
        add(above_ref, below_ref, 0)

    @pl.when(odd == 0)
    def _():
        add(below_ref, above_ref, 1)


def above_kernel(near_ref, total_ref, tile_ref, lower_ref, third_ref, copies_ref):
    third_ref[...] = lower_ref[...] + products(lambda slot: near_ref[slot], tile_ref)
    copies_ref[...] = jnp.broadcast_to(jnp.sum(total_ref[...], axis=0)[None], copies_ref.shape)


def finish_kernel(total_ref, start_ref, first_ref, second_ref, third_ref, answer_ref, residual_ref):
    totals = jnp.broadcast_to(jnp.sum(total_ref[...], axis=0), (RHS, 128))
    lane = lax.broadcasted_iota(jnp.int32, (RHS, 128), 1)
    row = lax.broadcasted_iota(jnp.int32, (RHS, 128), 0)
    moments = [
        jnp.sum(jnp.where(lane == row + RHS * at, totals, 0.0), axis=1, keepdims=True) for at in range(MOMENTS + 1)
    ]
    names = {(0, 0): 0, (0, 1): 1, (1, 1): 2, (0, 2): 3, (1, 2): 4, (2, 2): 5, (2, 3): 6, (0, 3): 4, (1, 3): 5}
    answer, residual = coefficients({pair: moments[at] for pair, at in names.items()})
    basis = (start_ref[...], first_ref[...], second_ref[...], third_ref[...])
    answer_ref[0, 0] = sum(c * v for c, v in zip(answer, basis))
    residual_ref[0, 0] = sum(c * v for c, v in zip(residual, basis))


def call(kernel, shapes, operands, name):
    return pl.pallas_call(
        kernel,
        out_shape=shapes,
        in_specs=[whole()] * len(operands),
        out_specs=[whole()] * len(shapes),
        compiler_params=pltpu.CompilerParams(vmem_limit_bytes=16 << 20),
        cost_estimate=cost(0),
        name=name,
    )(*operands)


def local(innovations, obs_error, where_frac, spread, obs_type):
    message, own, error_var, added, start = describe(
        innovations[0, 0], obs_error[0], where_frac[0, 0], spread[0], obs_type[0]
    )
    inner = partner(message, LON, 0)
    outer = partner(jnp.stack([message, inner]), LON, 1)
    wide = jnp.stack([outer[1], outer[0], message, inner])
    below, above = all_bands(wide)
    tiles, part, outer_own, outer = build(
        build_same_kernel,
        [TILES, FIELD, OWN_SIDE, FIELD],
        [wide, own, added],
        [pltpu.VMEM((16, OBS), jnp.float32), TILES],
    )
    tiles_below, part, outer = build(
        build_other_kernel, [TILES, FIELD, FIELD], [below, own, part, outer_own, outer], [TILES]
    )
    tiles_above, first, sent, outer_sent = build(
        build_other_kernel, [TILES, FIELD, SENT, SENT], [above, own, part, outer_own, outer], [TILES]
    )
    wide = jnp.stack([outer_sent, sent, partner(sent, LON, 0)])
    swap, both = all_bands_paired(wide)
    part, = call(apply_kernel, [FIELD], [wide, tiles, first, error_var], "apply")
    field = FIELD
    second, sent = call(
        paired_kernel,
        [field, SENT],
        [swap, both, tiles_below, tiles_above, part],
        "paired",
    )
    wide = widened(sent)
    below, above = all_bands(wide)
    part, row = call(
        same_band_kernel,
        [field, pltpu.VMEM((1, 128), jnp.float32)],
        [wide, tiles, second, error_var, start, first],
        "same_band",
    )
    copies = [pltpu.VMEM((extent(axes), 1, 128), jnp.float32) for axes in GROUPS]
    lower, partial = call(below_kernel, [field, copies[0]], [below, tiles_below, part, second, row], "below")
    partial = lax.all_to_all(partial, GROUPS[0], 0, 0)
    third, partial = call(above_kernel, [field, copies[1]], [above, partial, tiles_above, lower], "above")
    totals = lax.all_to_all(partial, GROUPS[1], 0, 0)
    whole_field = jax.ShapeDtypeStruct((1, 1, RHS, OBS), jnp.float32)
    return call(finish_kernel, [whole_field] * 2, [totals, start, first, second, third], "finish")


def solution(mesh):
    fine = Mesh(mesh.devices.reshape(2, 4, 4, 8, 2), LAT + LON)
    in_specs = (
        P(LAT, LON, None, None),
        P(LAT, LON, None),
        P(LAT, LON, None, None),
        P(LAT, LON, None),
        P(LAT, LON, None),
    )
    out_specs = (P(LAT, LON, None, None), P(LAT, LON, None, None))
    return jax.shard_map(local, mesh=fine, in_specs=in_specs, out_specs=out_specs, check_vma=False)
```

```python
import functools
import math

import jax
import jax.numpy as jnp
from jax import lax
from jax.experimental import pallas as pl
from jax.experimental.pallas import tpu as pltpu
from jax.sharding import Mesh, PartitionSpec as P

ITERS = 3
BANDS = 8
SECTORS = 64
OBS = 512
RHS = 16

LAT_LIMIT = 80.0 * math.pi / 180.0
HORIZ_SQ = 0.05 * 0.05
VERT_SQ = 0.3 * 0.3
TAPER_STEP = 0.45
LOG2E = 1.0 / math.log(2.0)
HORIZ = LOG2E / HORIZ_SQ
VERT = LOG2E / (2.0 * VERT_SQ)
COUPLING = ((1.0, 0.45, 0.45), (0.45, 1.0, 0.25), (0.45, 0.25, 1.0))

LAT = ("z_lo", "x")
LON = ("z_hi", "y", "core")
GROUPS = (("z_lo", "z_hi", "x"), ("y", "core"))


def extent(axes):
    size = 1
    for axis in axes:
        size *= lax.axis_size(axis)
    return size


def pairs(count, first):
    return [[low, (low + 1) % count] for low in range(first, count, 2)]


def partner(block, axes, first):
    both = lax.all_gather(block, axes, axis_index_groups=pairs(extent(axes), first))
    leads = lax.axis_index(axes) % 2 == first
    return jnp.where(leads, both[1], both[0])


def widened(block):
    inner = partner(block, LON, 0)
    inner, block = lax.optimization_barrier((inner, block))
    outer = partner(block, LON, 1)
    return jnp.stack([outer, block, inner])


def all_bands(wide):
    count = extent(LAT)
    below = lax.ppermute(wide, LAT, [(i, i + 1) for i in range(count - 1)])
    above = lax.ppermute(wide, LAT, [(i + 1, i) for i in range(count - 1)])
    return below, above


def all_bands_paired(wide):
    count = extent(LAT)
    swap = lax.ppermute(wide, LAT, [p for a, b in pairs(count, 0) for p in ((a, b), (b, a))])
    return swap, lax.all_gather(wide, LAT, axis_index_groups=pairs(count, 1))


def rounded(value):
    return value.astype(jnp.bfloat16).astype(jnp.float32)


def pieces(value):
    high = rounded(value)
    mid = rounded(value - high)
    return high, mid, rounded(value - high - mid)


def own_side(place, level, kinds, offset):
    one = jnp.ones_like(level)

    def looked_up(column):
        logs = [math.log2(row[column]) for row in COUPLING]
        return logs[0] + kinds[0] * (logs[1] - logs[0]) + kinds[1] * (logs[2] - logs[0])

    at_height = looked_up(0)
    rows = [HORIZ * axis for axis in place for _ in range(3)]
    rows += [2.0 * VERT * level, looked_up(1) - at_height, looked_up(2) - at_height]
    return rows + [one, one, offset + at_height - HORIZ, jnp.zeros_like(level)]


def far_side(place, level, kinds, offset, error):
    rows = [piece for axis in place for piece in pieces(axis)]
    return rows + [level, *kinds, *pieces(offset)[:2], jnp.ones_like(level), error]


def write_own(own_ref, rows_ref, rows):
    for row in range(16):
        rows_ref[row : row + 1, :] = rows[row]
    for step in range(3):
        if step:
            rows_ref[14:15, :] = rows[14] + step * math.log2(TAPER_STEP)
        left = rows_ref[...]
        for piece in range(3):
            part = left.astype(jnp.bfloat16)
            own_ref[step, 16 * piece : 16 * piece + 16, :] = part
            left = left - part.astype(jnp.float32)


def describe_kernel(
    start_ref, error_ref, frac_ref, spread_ref, type_ref,
    message_ref, own_ref, error_out_ref, added_ref, kept_ref, rows_ref,
):
    frac = frac_ref[...].astype(jnp.float32)
    latitude = (lax.axis_index(LAT).astype(jnp.float32) + frac[0:1]) * (2.0 * LAT_LIMIT / BANDS) - LAT_LIMIT
    longitude = (lax.axis_index(LON).astype(jnp.float32) + frac[1:2]) * (2.0 * math.pi / SECTORS)
    angles = jnp.concatenate([latitude, longitude], axis=0)
    cosines, sines = jnp.cos(angles), jnp.sin(angles)
    place = (cosines[0:1] * cosines[1:2], cosines[0:1] * sines[1:2], sines[0:1])
    level = frac[2:3]
    offset = jnp.log(spread_ref[...].astype(jnp.float32)) * LOG2E - VERT * level * level
    kinds = [jnp.where(type_ref[...] == kind, jnp.ones_like(level), 0.0) for kind in (1, 2)]
    far = far_side(place, level, kinds, offset, error_ref[...])
    for row in range(16):
        rows_ref[row : row + 1, :] = far[row]
    message_ref[0:16, :] = start_ref[...].astype(jnp.bfloat16)
    message_ref[16:32, :] = rows_ref[...].astype(jnp.bfloat16)
    error_out_ref[...] = error_ref[...]
    kept_ref[...] = start_ref[...]
    added_ref[...] = error_ref[...] * start_ref[...]
    write_own(own_ref, rows_ref, own_side(place, level, kinds, offset))


def whole(space=pltpu.VMEM):
    return pl.BlockSpec(memory_space=space)


def describe(start, error_var, where_frac, spread, obs_type):
    return pl.pallas_call(
        describe_kernel,
        out_shape=(
            pltpu.VMEM((32, OBS), jnp.bfloat16),
            pltpu.VMEM((3, 48, OBS), jnp.bfloat16),
            pltpu.VMEM((1, OBS), jnp.float32),
            pltpu.VMEM((RHS, OBS), jnp.float32),
            pltpu.VMEM((RHS, OBS), jnp.float32),
        ),
        in_specs=[whole()] * 5,
        out_specs=[whole()] * 5,
        scratch_shapes=[pltpu.VMEM((16, OBS), jnp.float32)],
        name="describe",
    )(start, error_var, where_frac, spread, obs_type)


OWN = (1, 2, 3)
OUTER = (0, 1, 2)


def part_of(columns, steps, near_ref, own_ref, tile_ref):
    for slot, (column, step) in enumerate(zip(columns, steps)):
        far = near_ref[column, 16:32, :]
        far = jnp.concatenate([far, far, far], axis=0)
        power = lax.dot_general(far, own_ref[step], (((0,), (0,)), ((), ())), preferred_element_type=jnp.float32)
        tile_ref[slot] = jnp.exp2(power).astype(jnp.bfloat16)
    return products(lambda slot: near_ref[columns[slot], 0:16, :], tile_ref)


def build_same_kernel(near_ref, own_ref, added_ref, tile_ref, sum_ref, outer_own_ref, outer_sum_ref, rows_ref, scratch_ref):
    rows = near_ref[1, 16:32, :].astype(jnp.float32)
    row = [rows[at : at + 1] for at in range(16)]
    place = [row[3 * axis] + row[3 * axis + 1] + row[3 * axis + 2] for axis in range(3)]
    write_own(outer_own_ref, rows_ref, own_side(place, row[9], row[10:12], row[12] + row[13]))
    sum_ref[...] = added_ref[...] + part_of(OWN, SAME_BAND, near_ref, own_ref, tile_ref)
    outer_added = row[15] * near_ref[1, 0:16, :].astype(jnp.float32)
    outer_sum_ref[...] = outer_added + part_of(OUTER, SAME_BAND, near_ref, outer_own_ref, scratch_ref)


def build_other_kernel(
    near_ref, own_ref, added_ref, outer_own_ref, outer_added_ref, tile_ref, sum_ref, *more
):
    *outer_refs, scratch_ref = more
    total = added_ref[...] + part_of(OWN, OTHER_BAND, near_ref, own_ref, tile_ref)
    outer = outer_added_ref[...] + part_of(OUTER, OTHER_BAND, near_ref, outer_own_ref, scratch_ref)
    sum_ref[...] = total
    if len(outer_refs) == 1:
        outer_refs[0][...] = outer
    else:
        for ref, value in zip(outer_refs, (total, outer)):
            send(ref, value)


def products(field_of, tile_ref):
    total = sum(jnp.dot(field_of(slot), tile_ref[slot], preferred_element_type=jnp.float32) for slot in range(3))
    return total if total.shape[0] == RHS else total[:RHS] + total[RHS:]


def send(ref, value):
    high = value.astype(jnp.bfloat16)
    ref[0:RHS, :] = high
    ref[RHS : 2 * RHS, :] = (value - high.astype(jnp.float32)).astype(jnp.bfloat16)


def apply_kernel(near_ref, tile_ref, added_ref, scale_ref, sum_ref):
    sum_ref[...] = added_ref[...] * scale_ref[...] + products(lambda slot: near_ref[slot], tile_ref)


SAME_BAND = (1, 0, 1)
OTHER_BAND = (2, 1, 2)


def cost(built):
    entries = 3 * OBS * OBS
    return pl.CostEstimate(
        flops=2 * entries * (RHS + 256 * built),
        bytes_accessed=2 * entries,
        transcendentals=entries * built,
    )


FIELD = pltpu.VMEM((RHS, OBS), jnp.float32)
SENT = pltpu.VMEM((2 * RHS, OBS), jnp.bfloat16)
TILES = pltpu.VMEM((3, OBS, OBS), jnp.bfloat16)
OWN_SIDE = pltpu.VMEM((3, 48, OBS), jnp.bfloat16)


def build(kernel, shapes, operands, scratch):
    return pl.pallas_call(
        kernel,
        out_shape=shapes,
        in_specs=[whole()] * len(operands),
        out_specs=[whole()] * len(shapes),
        scratch_shapes=scratch,
        compiler_params=pltpu.CompilerParams(vmem_limit_bytes=16 << 20),
        cost_estimate=cost(2),
        name="build",
    )(*operands)


def coefficients(gram):
    def inner(left, right):
        total = 0.0
        for i in range(4):
            for j in range(4):
                if left[i] is not None and right[j] is not None:
                    total = total + left[i] * right[j] * gram[min(i, j), max(i, j)]
        return total

    def axpy(scale, added, start):
        out = []
        for a, s in zip(added, start):
            if a is None:
                out.append(s)
            else:
                out.append(scale * a if s is None else s + scale * a)
        return out

    one = jnp.ones_like(gram[0, 0])
    answer = [None] * 4
    residual = [one, None, None, None]
    direction = residual
    norm_now = gram[0, 0]
    for iteration in range(ITERS):
        image = [None] + direction[:3]
        step_len = norm_now / inner(direction, image)
        answer = axpy(step_len, direction, answer)
        residual = axpy(-step_len, image, residual)
        if iteration < ITERS - 1:
            norm_next = inner(residual, residual)
            direction = axpy(norm_next / norm_now, direction, residual)
            norm_now = norm_next
    return answer[:3], residual


def lane_sums(products):
    empty = jnp.zeros((128 - RHS * len(products), OBS), jnp.float32)
    stacked = jnp.concatenate([*products, empty], axis=0) if len(products) < 8 else jnp.concatenate(products, axis=0)
    ones = jnp.ones((8, OBS), jnp.bfloat16)
    total = 0.0
    for part in pieces(stacked):
        total = total + lax.dot_general(
            ones, part.astype(jnp.bfloat16), (((1,), (1,)), ((), ())), preferred_element_type=jnp.float32
        )
    return total[0:1]


MOMENTS = 6


def same_band_kernel(near_ref, tile_ref, second_ref, scale_ref, start_ref, first_ref, sum_ref, row_ref):
    start, first, second = start_ref[...], first_ref[...], second_ref[...]
    sum_ref[...] = second * scale_ref[...] + products(lambda slot: near_ref[slot], tile_ref)
    row_ref[...] = lane_sums(
        [start * start, start * first, first * first, start * second, first * second, second * second]
    )


def below_kernel(near_ref, tile_ref, part_ref, second_ref, row_ref, sum_ref, copies_ref):
    part = part_ref[...]
    total = part + products(lambda slot: near_ref[slot], tile_ref)
    sum_ref[...] = total
    product = second_ref[...] * (2.0 * total - part)
    before = [jnp.zeros_like(product)] * MOMENTS
    row = row_ref[...] + lane_sums([*before, product])
    copies_ref[...] = jnp.broadcast_to(row[None], copies_ref.shape)


def paired_kernel(swap_ref, both_ref, below_ref, above_ref, part_ref, sum_ref, sent_ref):
    band = lax.axis_index(LAT)
    inside = jnp.where((band == 0) | (band == BANDS - 1), 0.0, 1.0)

    def add(swap_tiles, both_tiles, position):
        total = part_ref[...] + products(lambda slot: swap_ref[slot], swap_tiles)
        total = total + inside * products(lambda slot: both_ref[position, slot], both_tiles)
        sum_ref[...] = total
        send(sent_ref, total)

    @pl.when(band % 2 == 1)
    def _():
        add(below_ref, above_ref, 1)

    @pl.when(band % 2 == 0)
    def _():
        add(above_ref, below_ref, 0)


def above_kernel(near_ref, total_ref, tile_ref, lower_ref, third_ref, copies_ref):
    third_ref[...] = lower_ref[...] + products(lambda slot: near_ref[slot], tile_ref)
    copies_ref[...] = jnp.broadcast_to(jnp.sum(total_ref[...], axis=0)[None], copies_ref.shape)


def finish_kernel(total_ref, start_ref, first_ref, second_ref, third_ref, answer_ref, residual_ref):
    totals = jnp.broadcast_to(jnp.sum(total_ref[...], axis=0), (RHS, 128))
    lane = lax.broadcasted_iota(jnp.int32, (RHS, 128), 1)
    row = lax.broadcasted_iota(jnp.int32, (RHS, 128), 0)
    moments = [
        jnp.sum(jnp.where(lane == row + RHS * at, totals, 0.0), axis=1, keepdims=True) for at in range(MOMENTS + 1)
    ]
    names = {(0, 0): 0, (0, 1): 1, (1, 1): 2, (0, 2): 3, (1, 2): 4, (2, 2): 5, (2, 3): 6, (0, 3): 4, (1, 3): 5}
    answer, residual = coefficients({pair: moments[at] for pair, at in names.items()})
    basis = (start_ref[...], first_ref[...], second_ref[...], third_ref[...])
    answer_ref[0, 0] = sum(c * v for c, v in zip(answer, basis))
    residual_ref[0, 0] = sum(c * v for c, v in zip(residual, basis))


def call(kernel, shapes, operands, name):
    return pl.pallas_call(
        kernel,
        out_shape=shapes,
        in_specs=[whole()] * len(operands),
        out_specs=[whole()] * len(shapes),
        compiler_params=pltpu.CompilerParams(vmem_limit_bytes=16 << 20),
        cost_estimate=cost(0),
        name=name,
    )(*operands)


def local(innovations, obs_error, where_frac, spread, obs_type):
    message, own, error_var, added, start = describe(
        innovations[0, 0], obs_error[0], where_frac[0, 0], spread[0], obs_type[0]
    )
    inner = partner(message, LON, 0)
    outer = partner(jnp.stack([message, inner]), LON, 1)
    wide = jnp.stack([outer[1], outer[0], message, inner])
    below, above = all_bands(wide)
    tiles, part, outer_own, outer = build(
        build_same_kernel,
        [TILES, FIELD, OWN_SIDE, FIELD],
        [wide, own, added],
        [pltpu.VMEM((16, OBS), jnp.float32), TILES],
    )
    tiles_below, part, outer = build(
        build_other_kernel, [TILES, FIELD, FIELD], [below, own, part, outer_own, outer], [TILES]
    )
    tiles_above, first, sent, outer_sent = build(
        build_other_kernel, [TILES, FIELD, SENT, SENT], [above, own, part, outer_own, outer], [TILES]
    )
    wide = jnp.stack([outer_sent, sent, partner(sent, LON, 0)])
    swap, both = all_bands_paired(wide[:, :RHS])
    part, = call(apply_kernel, [FIELD], [wide, tiles, first, error_var], "apply")
    field = FIELD
    second, sent = call(
        paired_kernel,
        [field, SENT],
        [swap, both, tiles_below, tiles_above, part],
        "paired",
    )
    wide = widened(sent)
    below, above = all_bands(wide)
    part, row = call(
        same_band_kernel,
        [field, pltpu.VMEM((1, 128), jnp.float32)],
        [wide, tiles, second, error_var, start, first],
        "same_band",
    )
    copies = [pltpu.VMEM((extent(axes), 1, 128), jnp.float32) for axes in GROUPS]
    lower, partial = call(below_kernel, [field, copies[0]], [below, tiles_below, part, second, row], "below")
    partial = lax.all_to_all(partial, GROUPS[0], 0, 0)
    third, partial = call(above_kernel, [field, copies[1]], [above, partial, tiles_above, lower], "above")
    totals = lax.all_to_all(partial, GROUPS[1], 0, 0)
    whole_field = jax.ShapeDtypeStruct((1, 1, RHS, OBS), jnp.float32)
    return call(finish_kernel, [whole_field] * 2, [totals, start, first, second, third], "finish")


def solution(mesh):
    fine = Mesh(mesh.devices.reshape(2, 4, 4, 8, 2), LAT + LON)
    in_specs = (
        P(LAT, LON, None, None),
        P(LAT, LON, None),
        P(LAT, LON, None, None),
        P(LAT, LON, None),
        P(LAT, LON, None),
    )
    out_specs = (P(LAT, LON, None, None), P(LAT, LON, None, None))
    return jax.shard_map(local, mesh=fine, in_specs=in_specs, out_specs=out_specs, check_vma=False)
```

```python
import functools
import math

import jax
import jax.numpy as jnp
from jax import lax
from jax.experimental import pallas as pl
from jax.experimental.pallas import tpu as pltpu
from jax.sharding import Mesh, PartitionSpec as P

ITERS = 3
BANDS = 8
SECTORS = 64
OBS = 512
RHS = 16

LAT_LIMIT = 80.0 * math.pi / 180.0
HORIZ_SQ = 0.05 * 0.05
VERT_SQ = 0.3 * 0.3
TAPER_STEP = 0.45
LOG2E = 1.0 / math.log(2.0)
HORIZ = LOG2E / HORIZ_SQ
VERT = LOG2E / (2.0 * VERT_SQ)
COUPLING = ((1.0, 0.45, 0.45), (0.45, 1.0, 0.25), (0.45, 0.25, 1.0))

LAT = ("z_lo", "x")
LON = ("z_hi", "y", "core")
GROUPS = (("z_lo", "z_hi", "x"), ("y", "core"))


def extent(axes):
    size = 1
    for axis in axes:
        size *= lax.axis_size(axis)
    return size


def pairs(count, first):
    return [[low, (low + 1) % count] for low in range(first, count, 2)]


def partner(block, axes, first):
    both = lax.all_gather(block, axes, axis_index_groups=pairs(extent(axes), first))
    leads = lax.axis_index(axes) % 2 == first
    return jnp.where(leads, both[1], both[0])


def widened(block):
    inner = partner(block, LON, 0)
    inner, block = lax.optimization_barrier((inner, block))
    outer = partner(block, LON, 1)
    return jnp.stack([outer, block, inner])


def all_bands(wide):
    count = extent(LAT)
    below = lax.ppermute(wide, LAT, [(i, i + 1) for i in range(count - 1)])
    above = lax.ppermute(wide, LAT, [(i + 1, i) for i in range(count - 1)])
    return below, above


def all_bands_paired(wide):
    count = extent(LAT)
    swap = lax.ppermute(wide, LAT, [p for a, b in pairs(count, 0) for p in ((a, b), (b, a))])
    return swap, lax.all_gather(wide, LAT, axis_index_groups=pairs(count, 1))


def rounded(value):
    return value.astype(jnp.bfloat16).astype(jnp.float32)


def pieces(value):
    high = rounded(value)
    mid = rounded(value - high)
    return high, mid, rounded(value - high - mid)


def own_side(place, level, kinds, offset):
    one = jnp.ones_like(level)

    def looked_up(column):
        logs = [math.log2(row[column]) for row in COUPLING]
        return logs[0] + kinds[0] * (logs[1] - logs[0]) + kinds[1] * (logs[2] - logs[0])

    at_height = looked_up(0)
    rows = [HORIZ * axis for axis in place for _ in range(3)]
    rows += [2.0 * VERT * level, looked_up(1) - at_height, looked_up(2) - at_height]
    return rows + [one, one, offset + at_height - HORIZ, jnp.zeros_like(level)]


def far_side(place, level, kinds, offset, error):
    rows = [piece for axis in place for piece in pieces(axis)]
    return rows + [level, *kinds, *pieces(offset)[:2], jnp.ones_like(level), error]


def write_own(own_ref, rows_ref, rows):
    for row in range(16):
        rows_ref[row : row + 1, :] = rows[row]
    for step in range(3):
        if step:
            rows_ref[14:15, :] = rows[14] + step * math.log2(TAPER_STEP)
        left = rows_ref[...]
        for piece in range(3):
            part = left.astype(jnp.bfloat16)
            own_ref[step, 16 * piece : 16 * piece + 16, :] = part
            left = left - part.astype(jnp.float32)


def describe_kernel(
    start_ref, error_ref, frac_ref, spread_ref, type_ref,
    message_ref, own_ref, error_out_ref, added_ref, kept_ref, rows_ref,
):
    frac = frac_ref[...].astype(jnp.float32)
    latitude = (lax.axis_index(LAT).astype(jnp.float32) + frac[0:1]) * (2.0 * LAT_LIMIT / BANDS) - LAT_LIMIT
    longitude = (lax.axis_index(LON).astype(jnp.float32) + frac[1:2]) * (2.0 * math.pi / SECTORS)
    angles = jnp.concatenate([latitude, longitude], axis=0)
    cosines, sines = jnp.cos(angles), jnp.sin(angles)
    place = (cosines[0:1] * cosines[1:2], cosines[0:1] * sines[1:2], sines[0:1])
    level = frac[2:3]
    offset = jnp.log(spread_ref[...].astype(jnp.float32)) * LOG2E - VERT * level * level
    kinds = [jnp.where(type_ref[...] == kind, jnp.ones_like(level), 0.0) for kind in (1, 2)]
    far = far_side(place, level, kinds, offset, error_ref[...])
    for row in range(16):
        rows_ref[row : row + 1, :] = far[row]
    message_ref[0:16, :] = start_ref[...].astype(jnp.bfloat16)
    message_ref[16:32, :] = rows_ref[...].astype(jnp.bfloat16)
    error_out_ref[...] = error_ref[...]
    kept_ref[...] = start_ref[...]
    added_ref[...] = error_ref[...] * start_ref[...]
    write_own(own_ref, rows_ref, own_side(place, level, kinds, offset))


def whole(space=pltpu.VMEM):
    return pl.BlockSpec(memory_space=space)


def describe(start, error_var, where_frac, spread, obs_type):
    return pl.pallas_call(
        describe_kernel,
        out_shape=(
            pltpu.VMEM((32, OBS), jnp.bfloat16),
            pltpu.VMEM((3, 48, OBS), jnp.bfloat16),
            pltpu.VMEM((1, OBS), jnp.float32),
            pltpu.VMEM((RHS, OBS), jnp.float32),
            pltpu.VMEM((RHS, OBS), jnp.float32),
        ),
        in_specs=[whole()] * 5,
        out_specs=[whole()] * 5,
        scratch_shapes=[pltpu.VMEM((16, OBS), jnp.float32)],
        name="describe",
    )(start, error_var, where_frac, spread, obs_type)


OWN = (1, 2, 3)
OUTER = (0, 1, 2)


def part_of(columns, steps, near_ref, own_ref, tile_ref):
    for slot, (column, step) in enumerate(zip(columns, steps)):
        far = near_ref[column, 16:32, :]
        far = jnp.concatenate([far, far, far], axis=0)
        power = lax.dot_general(far, own_ref[step], (((0,), (0,)), ((), ())), preferred_element_type=jnp.float32)
        tile_ref[slot] = jnp.exp2(power).astype(jnp.bfloat16)
    return products(lambda slot: near_ref[columns[slot], 0:16, :], tile_ref)


def build_same_kernel(near_ref, own_ref, added_ref, tile_ref, sum_ref, outer_own_ref, outer_sum_ref, rows_ref, scratch_ref):
    rows = near_ref[1, 16:32, :].astype(jnp.float32)
    row = [rows[at : at + 1] for at in range(16)]
    place = [row[3 * axis] + row[3 * axis + 1] + row[3 * axis + 2] for axis in range(3)]
    write_own(outer_own_ref, rows_ref, own_side(place, row[9], row[10:12], row[12] + row[13]))
    sum_ref[...] = added_ref[...] + part_of(OWN, SAME_BAND, near_ref, own_ref, tile_ref)
    outer_added = row[15] * near_ref[1, 0:16, :].astype(jnp.float32)
    outer_sum_ref[...] = outer_added + part_of(OUTER, SAME_BAND, near_ref, outer_own_ref, scratch_ref)


def build_other_kernel(
    near_ref, own_ref, added_ref, outer_own_ref, outer_added_ref, tile_ref, sum_ref, *more
):
    *outer_refs, scratch_ref = more
    total = added_ref[...] + part_of(OWN, OTHER_BAND, near_ref, own_ref, tile_ref)
    outer = outer_added_ref[...] + part_of(OUTER, OTHER_BAND, near_ref, outer_own_ref, scratch_ref)
    sum_ref[...] = total
    if len(outer_refs) == 1:
        outer_refs[0][...] = outer
    else:
        for ref, value in zip(outer_refs, (total, outer)):
            send(ref, value)


def products(field_of, tile_ref):
    total = sum(jnp.dot(field_of(slot), tile_ref[slot], preferred_element_type=jnp.float32) for slot in range(3))
    return total if total.shape[0] == RHS else total[:RHS] + total[RHS:]


def send(ref, value):
    high = value.astype(jnp.bfloat16)
    ref[0:RHS, :] = high
    ref[RHS : 2 * RHS, :] = (value - high.astype(jnp.float32)).astype(jnp.bfloat16)


def apply_kernel(near_ref, tile_ref, added_ref, scale_ref, sum_ref):
    sum_ref[...] = added_ref[...] * scale_ref[...] + products(lambda slot: near_ref[slot], tile_ref)


SAME_BAND = (1, 0, 1)
OTHER_BAND = (2, 1, 2)


def cost(built):
    entries = 3 * OBS * OBS
    return pl.CostEstimate(
        flops=2 * entries * (RHS + 256 * built),
        bytes_accessed=2 * entries,
        transcendentals=entries * built,
    )


FIELD = pltpu.VMEM((RHS, OBS), jnp.float32)
SENT = pltpu.VMEM((2 * RHS, OBS), jnp.bfloat16)
TILES = pltpu.VMEM((3, OBS, OBS), jnp.bfloat16)
OWN_SIDE = pltpu.VMEM((3, 48, OBS), jnp.bfloat16)


def build(kernel, shapes, operands, scratch):
    return pl.pallas_call(
        kernel,
        out_shape=shapes,
        in_specs=[whole()] * len(operands),
        out_specs=[whole()] * len(shapes),
        scratch_shapes=scratch,
        compiler_params=pltpu.CompilerParams(vmem_limit_bytes=16 << 20),
        cost_estimate=cost(2),
        name="build",
    )(*operands)


def coefficients(gram):
    def inner(left, right):
        total = 0.0
        for i in range(4):
            for j in range(4):
                if left[i] is not None and right[j] is not None:
                    total = total + left[i] * right[j] * gram[min(i, j), max(i, j)]
        return total

    def axpy(scale, added, start):
        out = []
        for a, s in zip(added, start):
            if a is None:
                out.append(s)
            else:
                out.append(scale * a if s is None else s + scale * a)
        return out

    one = jnp.ones_like(gram[0, 0])
    answer = [None] * 4
    residual = [one, None, None, None]
    direction = residual
    norm_now = gram[0, 0]
    for iteration in range(ITERS):
        image = [None] + direction[:3]
        step_len = norm_now / inner(direction, image)
        answer = axpy(step_len, direction, answer)
        residual = axpy(-step_len, image, residual)
        if iteration < ITERS - 1:
            norm_next = inner(residual, residual)
            direction = axpy(norm_next / norm_now, direction, residual)
            norm_now = norm_next
    return answer[:3], residual


def lane_sums(products):
    empty = jnp.zeros((128 - RHS * len(products), OBS), jnp.float32)
    stacked = jnp.concatenate([*products, empty], axis=0) if len(products) < 8 else jnp.concatenate(products, axis=0)
    ones = jnp.ones((8, OBS), jnp.bfloat16)
    total = 0.0
    for part in pieces(stacked):
        total = total + lax.dot_general(
            ones, part.astype(jnp.bfloat16), (((1,), (1,)), ((), ())), preferred_element_type=jnp.float32
        )
    return total[0:1]


MOMENTS = 6


def same_band_kernel(near_ref, tile_ref, second_ref, scale_ref, start_ref, first_ref, sum_ref, row_ref):
    start, first, second = start_ref[...], first_ref[...], second_ref[...]
    sum_ref[...] = second * scale_ref[...] + products(lambda slot: near_ref[slot], tile_ref)
    row_ref[...] = lane_sums(
        [start * start, start * first, first * first, start * second, first * second, second * second]
    )


def below_kernel(near_ref, tile_ref, part_ref, second_ref, row_ref, sum_ref, copies_ref):
    part = part_ref[...]
    total = part + products(lambda slot: near_ref[slot], tile_ref)
    sum_ref[...] = total
    product = second_ref[...] * (2.0 * total - part)
    before = [jnp.zeros_like(product)] * MOMENTS
    row = row_ref[...] + lane_sums([*before, product])
    copies_ref[...] = jnp.broadcast_to(row[None], copies_ref.shape)


def paired_kernel(swap_ref, both_ref, below_ref, above_ref, part_ref, sum_ref, sent_ref):
    band = lax.axis_index(LAT)
    inside = jnp.where((band == 0) | (band == BANDS - 1), 0.0, 1.0)

    def add(swap_tiles, both_tiles, position):
        total = part_ref[...] + products(lambda slot: swap_ref[slot], swap_tiles)
        total = total + inside * products(lambda slot: both_ref[position, slot], both_tiles)
        sum_ref[...] = total
        send(sent_ref, total)

    @pl.when(band % 2 == 1)
    def _():
        add(below_ref, above_ref, 1)

    @pl.when(band % 2 == 0)
    def _():
        add(above_ref, below_ref, 0)


def above_kernel(near_ref, total_ref, tile_ref, lower_ref, third_ref, copies_ref):
    third_ref[...] = lower_ref[...] + products(lambda slot: near_ref[slot], tile_ref)
    copies_ref[...] = jnp.broadcast_to(jnp.sum(total_ref[...], axis=0)[None], copies_ref.shape)


def finish_kernel(total_ref, start_ref, first_ref, second_ref, third_ref, answer_ref, residual_ref):
    totals = jnp.broadcast_to(jnp.sum(total_ref[...], axis=0), (RHS, 128))
    lane = lax.broadcasted_iota(jnp.int32, (RHS, 128), 1)
    row = lax.broadcasted_iota(jnp.int32, (RHS, 128), 0)
    moments = [
        jnp.sum(jnp.where(lane == row + RHS * at, totals, 0.0), axis=1, keepdims=True) for at in range(MOMENTS + 1)
    ]
    names = {(0, 0): 0, (0, 1): 1, (1, 1): 2, (0, 2): 3, (1, 2): 4, (2, 2): 5, (2, 3): 6, (0, 3): 4, (1, 3): 5}
    answer, residual = coefficients({pair: moments[at] for pair, at in names.items()})
    basis = (start_ref[...], first_ref[...], second_ref[...], third_ref[...])
    answer_ref[0, 0] = sum(c * v for c, v in zip(answer, basis))
    residual_ref[0, 0] = sum(c * v for c, v in zip(residual, basis))


def call(kernel, shapes, operands, name):
    return pl.pallas_call(
        kernel,
        out_shape=shapes,
        in_specs=[whole()] * len(operands),
        out_specs=[whole()] * len(shapes),
        compiler_params=pltpu.CompilerParams(vmem_limit_bytes=16 << 20),
        cost_estimate=cost(0),
        name=name,
    )(*operands)


def local(innovations, obs_error, where_frac, spread, obs_type):
    message, own, error_var, added, start = describe(
        innovations[0, 0], obs_error[0], where_frac[0, 0], spread[0], obs_type[0]
    )
    inner = partner(message, LON, 0)
    outer = partner(jnp.stack([message, inner]), LON, 1)
    wide = jnp.stack([outer[1], outer[0], message, inner])
    below, above = all_bands(wide)
    tiles, part, outer_own, outer = build(
        build_same_kernel,
        [TILES, FIELD, OWN_SIDE, FIELD],
        [wide, own, added],
        [pltpu.VMEM((16, OBS), jnp.float32), TILES],
    )
    tiles_below, part, outer = build(
        build_other_kernel, [TILES, FIELD, FIELD], [below, own, part, outer_own, outer], [TILES]
    )
    tiles_above, first, sent, outer_sent = build(
        build_other_kernel, [TILES, FIELD, SENT, SENT], [above, own, part, outer_own, outer], [TILES]
    )
    wide = jnp.stack([outer_sent, sent, partner(sent, LON, 0)])
    swap, both = all_bands_paired(wide[:, :RHS])
    part, = call(apply_kernel, [FIELD], [wide, tiles, first, error_var], "apply")
    field = FIELD
    second, sent = call(
        paired_kernel,
        [field, SENT],
        [swap, both, tiles_below, tiles_above, part],
        "paired",
    )
    wide = widened(sent)
    below, above = all_bands(wide[:, :RHS])
    part, row = call(
        same_band_kernel,
        [field, pltpu.VMEM((1, 128), jnp.float32)],
        [wide, tiles, second, error_var, start, first],
        "same_band",
    )
    copies = [pltpu.VMEM((extent(axes), 1, 128), jnp.float32) for axes in GROUPS]
    lower, partial = call(below_kernel, [field, copies[0]], [below, tiles_below, part, second, row], "below")
    partial = lax.all_to_all(partial, GROUPS[0], 0, 0)
    third, partial = call(above_kernel, [field, copies[1]], [above, partial, tiles_above, lower], "above")
    totals = lax.all_to_all(partial, GROUPS[1], 0, 0)
    whole_field = jax.ShapeDtypeStruct((1, 1, RHS, OBS), jnp.float32)
    return call(finish_kernel, [whole_field] * 2, [totals, start, first, second, third], "finish")


def solution(mesh):
    fine = Mesh(mesh.devices.reshape(2, 4, 4, 8, 2), LAT + LON)
    in_specs = (
        P(LAT, LON, None, None),
        P(LAT, LON, None),
        P(LAT, LON, None, None),
        P(LAT, LON, None),
        P(LAT, LON, None),
    )
    out_specs = (P(LAT, LON, None, None), P(LAT, LON, None, None))
    return jax.shard_map(local, mesh=fine, in_specs=in_specs, out_specs=out_specs, check_vma=False)
```

```python
import functools
import math

import jax
import jax.numpy as jnp
from jax import lax
from jax.experimental import pallas as pl
from jax.experimental.pallas import tpu as pltpu
from jax.sharding import Mesh, PartitionSpec as P

ITERS = 3
BANDS = 8
SECTORS = 64
OBS = 512
RHS = 16

LAT_LIMIT = 80.0 * math.pi / 180.0
HORIZ_SQ = 0.05 * 0.05
VERT_SQ = 0.3 * 0.3
TAPER_STEP = 0.45
LOG2E = 1.0 / math.log(2.0)
HORIZ = LOG2E / HORIZ_SQ
VERT = LOG2E / (2.0 * VERT_SQ)
COUPLING = ((1.0, 0.45, 0.45), (0.45, 1.0, 0.25), (0.45, 0.25, 1.0))

LAT = ("z_lo", "x")
LON = ("z_hi", "y", "core")
GROUPS = (("y", "core"), ("z_lo", "z_hi", "x"))


def extent(axes):
    size = 1
    for axis in axes:
        size *= lax.axis_size(axis)
    return size


def pairs(count, first):
    return [[low, (low + 1) % count] for low in range(first, count, 2)]


def partner(block, axes, first):
    both = lax.all_gather(block, axes, axis_index_groups=pairs(extent(axes), first))
    leads = lax.axis_index(axes) % 2 == first
    return jnp.where(leads, both[1], both[0])


def widened(block):
    inner = partner(block, LON, 0)
    inner, block = lax.optimization_barrier((inner, block))
    outer = partner(block, LON, 1)
    return jnp.stack([outer, block, inner])


def all_bands(wide):
    count = extent(LAT)
    below = lax.ppermute(wide, LAT, [(i, i + 1) for i in range(count - 1)])
    above = lax.ppermute(wide, LAT, [(i + 1, i) for i in range(count - 1)])
    return below, above


def all_bands_paired(wide):
    count = extent(LAT)
    swap = lax.ppermute(wide, LAT, [p for a, b in pairs(count, 0) for p in ((a, b), (b, a))])
    return swap, lax.all_gather(wide, LAT, axis_index_groups=pairs(count, 1))


def rounded(value):
    return value.astype(jnp.bfloat16).astype(jnp.float32)


def pieces(value):
    high = rounded(value)
    mid = rounded(value - high)
    return high, mid, rounded(value - high - mid)


def own_side(place, level, kinds, offset):
    one = jnp.ones_like(level)

    def looked_up(column):
        logs = [math.log2(row[column]) for row in COUPLING]
        return logs[0] + kinds[0] * (logs[1] - logs[0]) + kinds[1] * (logs[2] - logs[0])

    at_height = looked_up(0)
    rows = [HORIZ * axis for axis in place for _ in range(3)]
    rows += [2.0 * VERT * level, looked_up(1) - at_height, looked_up(2) - at_height]
    return rows + [one, one, offset + at_height - HORIZ, jnp.zeros_like(level)]


def far_side(place, level, kinds, offset, error):
    rows = [piece for axis in place for piece in pieces(axis)]
    return rows + [level, *kinds, *pieces(offset)[:2], jnp.ones_like(level), error]


def write_own(own_ref, rows_ref, rows):
    for row in range(16):
        rows_ref[row : row + 1, :] = rows[row]
    for step in range(3):
        if step:
            rows_ref[14:15, :] = rows[14] + step * math.log2(TAPER_STEP)
        left = rows_ref[...]
        for piece in range(3):
            part = left.astype(jnp.bfloat16)
            own_ref[step, 16 * piece : 16 * piece + 16, :] = part
            left = left - part.astype(jnp.float32)


def describe_kernel(
    start_ref, error_ref, frac_ref, spread_ref, type_ref,
    message_ref, own_ref, error_out_ref, added_ref, kept_ref, rows_ref,
):
    frac = frac_ref[...].astype(jnp.float32)
    latitude = (lax.axis_index(LAT).astype(jnp.float32) + frac[0:1]) * (2.0 * LAT_LIMIT / BANDS) - LAT_LIMIT
    longitude = (lax.axis_index(LON).astype(jnp.float32) + frac[1:2]) * (2.0 * math.pi / SECTORS)
    angles = jnp.concatenate([latitude, longitude], axis=0)
    cosines, sines = jnp.cos(angles), jnp.sin(angles)
    place = (cosines[0:1] * cosines[1:2], cosines[0:1] * sines[1:2], sines[0:1])
    level = frac[2:3]
    offset = jnp.log(spread_ref[...].astype(jnp.float32)) * LOG2E - VERT * level * level
    kinds = [jnp.where(type_ref[...] == kind, jnp.ones_like(level), 0.0) for kind in (1, 2)]
    far = far_side(place, level, kinds, offset, error_ref[...])
    for row in range(16):
        rows_ref[row : row + 1, :] = far[row]
    message_ref[0:16, :] = start_ref[...].astype(jnp.bfloat16)
    message_ref[16:32, :] = rows_ref[...].astype(jnp.bfloat16)
    error_out_ref[...] = error_ref[...]
    kept_ref[...] = start_ref[...]
    added_ref[...] = error_ref[...] * start_ref[...]
    write_own(own_ref, rows_ref, own_side(place, level, kinds, offset))


def whole(space=pltpu.VMEM):
    return pl.BlockSpec(memory_space=space)


def describe(start, error_var, where_frac, spread, obs_type):
    return pl.pallas_call(
        describe_kernel,
        out_shape=(
            pltpu.VMEM((32, OBS), jnp.bfloat16),
            pltpu.VMEM((3, 48, OBS), jnp.bfloat16),
            pltpu.VMEM((1, OBS), jnp.float32),
            pltpu.VMEM((RHS, OBS), jnp.float32),
            pltpu.VMEM((RHS, OBS), jnp.float32),
        ),
        in_specs=[whole()] * 5,
        out_specs=[whole()] * 5,
        scratch_shapes=[pltpu.VMEM((16, OBS), jnp.float32)],
        name="describe",
    )(start, error_var, where_frac, spread, obs_type)


OWN = (1, 2, 3)
OUTER = (0, 1, 2)


def part_of(columns, steps, near_ref, own_ref, tile_ref):
    for slot, (column, step) in enumerate(zip(columns, steps)):
        far = near_ref[column, 16:32, :]
        far = jnp.concatenate([far, far, far], axis=0)
        power = lax.dot_general(far, own_ref[step], (((0,), (0,)), ((), ())), preferred_element_type=jnp.float32)
        tile_ref[slot] = jnp.exp2(power).astype(jnp.bfloat16)
    return products(lambda slot: near_ref[columns[slot], 0:16, :], tile_ref)


def build_same_kernel(near_ref, own_ref, added_ref, tile_ref, sum_ref, outer_own_ref, outer_sum_ref, rows_ref, scratch_ref):
    rows = near_ref[1, 16:32, :].astype(jnp.float32)
    row = [rows[at : at + 1] for at in range(16)]
    place = [row[3 * axis] + row[3 * axis + 1] + row[3 * axis + 2] for axis in range(3)]
    write_own(outer_own_ref, rows_ref, own_side(place, row[9], row[10:12], row[12] + row[13]))
    sum_ref[...] = added_ref[...] + part_of(OWN, SAME_BAND, near_ref, own_ref, tile_ref)
    outer_added = row[15] * near_ref[1, 0:16, :].astype(jnp.float32)
    outer_sum_ref[...] = outer_added + part_of(OUTER, SAME_BAND, near_ref, outer_own_ref, scratch_ref)


def build_other_kernel(
    near_ref, own_ref, added_ref, outer_own_ref, outer_added_ref, tile_ref, sum_ref, *more
):
    *outer_refs, scratch_ref = more
    total = added_ref[...] + part_of(OWN, OTHER_BAND, near_ref, own_ref, tile_ref)
    outer = outer_added_ref[...] + part_of(OUTER, OTHER_BAND, near_ref, outer_own_ref, scratch_ref)
    sum_ref[...] = total
    if len(outer_refs) == 1:
        outer_refs[0][...] = outer
    else:
        for ref, value in zip(outer_refs, (total, outer)):
            send(ref, value)


def products(field_of, tile_ref):
    total = sum(jnp.dot(field_of(slot), tile_ref[slot], preferred_element_type=jnp.float32) for slot in range(3))
    return total if total.shape[0] == RHS else total[:RHS] + total[RHS:]


def send(ref, value):
    high = value.astype(jnp.bfloat16)
    ref[0:RHS, :] = high
    ref[RHS : 2 * RHS, :] = (value - high.astype(jnp.float32)).astype(jnp.bfloat16)


def apply_kernel(near_ref, tile_ref, added_ref, scale_ref, sum_ref):
    sum_ref[...] = added_ref[...] * scale_ref[...] + products(lambda slot: near_ref[slot], tile_ref)


SAME_BAND = (1, 0, 1)
OTHER_BAND = (2, 1, 2)


def cost(built):
    entries = 3 * OBS * OBS
    return pl.CostEstimate(
        flops=2 * entries * (RHS + 256 * built),
        bytes_accessed=2 * entries,
        transcendentals=entries * built,
    )


FIELD = pltpu.VMEM((RHS, OBS), jnp.float32)
SENT = pltpu.VMEM((2 * RHS, OBS), jnp.bfloat16)
TILES = pltpu.VMEM((3, OBS, OBS), jnp.bfloat16)
OWN_SIDE = pltpu.VMEM((3, 48, OBS), jnp.bfloat16)


def build(kernel, shapes, operands, scratch):
    return pl.pallas_call(
        kernel,
        out_shape=shapes,
        in_specs=[whole()] * len(operands),
        out_specs=[whole()] * len(shapes),
        scratch_shapes=scratch,
        compiler_params=pltpu.CompilerParams(vmem_limit_bytes=16 << 20),
        cost_estimate=cost(2),
        name="build",
    )(*operands)


def coefficients(gram):
    def inner(left, right):
        total = 0.0
        for i in range(4):
            for j in range(4):
                if left[i] is not None and right[j] is not None:
                    total = total + left[i] * right[j] * gram[min(i, j), max(i, j)]
        return total

    def axpy(scale, added, start):
        out = []
        for a, s in zip(added, start):
            if a is None:
                out.append(s)
            else:
                out.append(scale * a if s is None else s + scale * a)
        return out

    one = jnp.ones_like(gram[0, 0])
    answer = [None] * 4
    residual = [one, None, None, None]
    direction = residual
    norm_now = gram[0, 0]
    for iteration in range(ITERS):
        image = [None] + direction[:3]
        step_len = norm_now / inner(direction, image)
        answer = axpy(step_len, direction, answer)
        residual = axpy(-step_len, image, residual)
        if iteration < ITERS - 1:
            norm_next = inner(residual, residual)
            direction = axpy(norm_next / norm_now, direction, residual)
            norm_now = norm_next
    return answer[:3], residual


def lane_sums(products):
    empty = jnp.zeros((128 - RHS * len(products), OBS), jnp.float32)
    stacked = jnp.concatenate([*products, empty], axis=0) if len(products) < 8 else jnp.concatenate(products, axis=0)
    ones = jnp.ones((8, OBS), jnp.bfloat16)
    total = 0.0
    for part in pieces(stacked):
        total = total + lax.dot_general(
            ones, part.astype(jnp.bfloat16), (((1,), (1,)), ((), ())), preferred_element_type=jnp.float32
        )
    return total[0:1]


MOMENTS = 6


def same_band_kernel(near_ref, tile_ref, second_ref, scale_ref, start_ref, first_ref, sum_ref, row_ref):
    start, first, second = start_ref[...], first_ref[...], second_ref[...]
    sum_ref[...] = second * scale_ref[...] + products(lambda slot: near_ref[slot], tile_ref)
    row_ref[...] = lane_sums(
        [start * start, start * first, first * first, start * second, first * second, second * second]
    )


def below_kernel(near_ref, tile_ref, part_ref, second_ref, row_ref, sum_ref, copies_ref):
    part = part_ref[...]
    total = part + products(lambda slot: near_ref[slot], tile_ref)
    sum_ref[...] = total
    product = second_ref[...] * (2.0 * total - part)
    before = [jnp.zeros_like(product)] * MOMENTS
    row = row_ref[...] + lane_sums([*before, product])
    copies_ref[...] = jnp.broadcast_to(row[None], copies_ref.shape)


def paired_kernel(swap_ref, both_ref, below_ref, above_ref, part_ref, sum_ref, sent_ref):
    band = lax.axis_index(LAT)
    inside = jnp.where((band == 0) | (band == BANDS - 1), 0.0, 1.0)

    def add(swap_tiles, both_tiles, position):
        total = part_ref[...] + products(lambda slot: swap_ref[slot], swap_tiles)
        total = total + inside * products(lambda slot: both_ref[position, slot], both_tiles)
        sum_ref[...] = total
        send(sent_ref, total)

    @pl.when(band % 2 == 1)
    def _():
        add(below_ref, above_ref, 1)

    @pl.when(band % 2 == 0)
    def _():
        add(above_ref, below_ref, 0)


def above_kernel(near_ref, total_ref, tile_ref, lower_ref, third_ref, copies_ref):
    third_ref[...] = lower_ref[...] + products(lambda slot: near_ref[slot], tile_ref)
    copies_ref[...] = jnp.broadcast_to(jnp.sum(total_ref[...], axis=0)[None], copies_ref.shape)


def finish_kernel(total_ref, start_ref, first_ref, second_ref, third_ref, answer_ref, residual_ref):
    totals = jnp.broadcast_to(jnp.sum(total_ref[...], axis=0), (RHS, 128))
    lane = lax.broadcasted_iota(jnp.int32, (RHS, 128), 1)
    row = lax.broadcasted_iota(jnp.int32, (RHS, 128), 0)
    moments = [
        jnp.sum(jnp.where(lane == row + RHS * at, totals, 0.0), axis=1, keepdims=True) for at in range(MOMENTS + 1)
    ]
    names = {(0, 0): 0, (0, 1): 1, (1, 1): 2, (0, 2): 3, (1, 2): 4, (2, 2): 5, (2, 3): 6, (0, 3): 4, (1, 3): 5}
    answer, residual = coefficients({pair: moments[at] for pair, at in names.items()})
    basis = (start_ref[...], first_ref[...], second_ref[...], third_ref[...])
    answer_ref[0, 0] = sum(c * v for c, v in zip(answer, basis))
    residual_ref[0, 0] = sum(c * v for c, v in zip(residual, basis))


def call(kernel, shapes, operands, name):
    return pl.pallas_call(
        kernel,
        out_shape=shapes,
        in_specs=[whole()] * len(operands),
        out_specs=[whole()] * len(shapes),
        compiler_params=pltpu.CompilerParams(vmem_limit_bytes=16 << 20),
        cost_estimate=cost(0),
        name=name,
    )(*operands)


def local(innovations, obs_error, where_frac, spread, obs_type):
    message, own, error_var, added, start = describe(
        innovations[0, 0], obs_error[0], where_frac[0, 0], spread[0], obs_type[0]
    )
    inner = partner(message, LON, 0)
    outer = partner(jnp.stack([message, inner]), LON, 1)
    wide = jnp.stack([outer[1], outer[0], message, inner])
    below, above = all_bands(wide)
    tiles, part, outer_own, outer = build(
        build_same_kernel,
        [TILES, FIELD, OWN_SIDE, FIELD],
        [wide, own, added],
        [pltpu.VMEM((16, OBS), jnp.float32), TILES],
    )
    tiles_below, part, outer = build(
        build_other_kernel, [TILES, FIELD, FIELD], [below, own, part, outer_own, outer], [TILES]
    )
    tiles_above, first, sent, outer_sent = build(
        build_other_kernel, [TILES, FIELD, SENT, SENT], [above, own, part, outer_own, outer], [TILES]
    )
    wide = jnp.stack([outer_sent, sent, partner(sent, LON, 0)])
    swap, both = all_bands_paired(wide[:, :RHS])
    part, = call(apply_kernel, [FIELD], [wide, tiles, first, error_var], "apply")
    field = FIELD
    second, sent = call(
        paired_kernel,
        [field, SENT],
        [swap, both, tiles_below, tiles_above, part],
        "paired",
    )
    wide = widened(sent)
    below, above = all_bands(wide[:, :RHS])
    part, row = call(
        same_band_kernel,
        [field, pltpu.VMEM((1, 128), jnp.float32)],
        [wide, tiles, second, error_var, start, first],
        "same_band",
    )
    copies = [pltpu.VMEM((extent(axes), 1, 128), jnp.float32) for axes in GROUPS]
    lower, partial = call(below_kernel, [field, copies[0]], [below, tiles_below, part, second, row], "below")
    partial = lax.all_to_all(partial, GROUPS[0], 0, 0)
    third, partial = call(above_kernel, [field, copies[1]], [above, partial, tiles_above, lower], "above")
    totals = lax.all_to_all(partial, GROUPS[1], 0, 0)
    whole_field = jax.ShapeDtypeStruct((1, 1, RHS, OBS), jnp.float32)
    return call(finish_kernel, [whole_field] * 2, [totals, start, first, second, third], "finish")


def solution(mesh):
    fine = Mesh(mesh.devices.reshape(2, 4, 4, 8, 2), LAT + LON)
    in_specs = (
        P(LAT, LON, None, None),
        P(LAT, LON, None),
        P(LAT, LON, None, None),
        P(LAT, LON, None),
        P(LAT, LON, None),
    )
    out_specs = (P(LAT, LON, None, None), P(LAT, LON, None, None))
    return jax.shard_map(local, mesh=fine, in_specs=in_specs, out_specs=out_specs, check_vma=False)
```

```python
import functools
import math

import jax
import jax.numpy as jnp
from jax import lax
from jax.experimental import pallas as pl
from jax.experimental.pallas import tpu as pltpu
from jax.sharding import Mesh, PartitionSpec as P

ITERS = 3
BANDS = 8
SECTORS = 64
OBS = 512
RHS = 16

LAT_LIMIT = 80.0 * math.pi / 180.0
HORIZ_SQ = 0.05 * 0.05
VERT_SQ = 0.3 * 0.3
TAPER_STEP = 0.45
LOG2E = 1.0 / math.log(2.0)
HORIZ = LOG2E / HORIZ_SQ
VERT = LOG2E / (2.0 * VERT_SQ)
COUPLING = ((1.0, 0.45, 0.45), (0.45, 1.0, 0.25), (0.45, 0.25, 1.0))

LAT = ("z_lo", "x")
LON = ("z_hi", "y", "core")
GROUPS = (("y", "core"), ("z_lo", "z_hi", "x"))


def extent(axes):
    size = 1
    for axis in axes:
        size *= lax.axis_size(axis)
    return size


def pairs(count, first):
    return [[low, (low + 1) % count] for low in range(first, count, 2)]


def partner(block, axes, first):
    both = lax.all_gather(block, axes, axis_index_groups=pairs(extent(axes), first))
    leads = lax.axis_index(axes) % 2 == first
    return jnp.where(leads, both[1], both[0])


def widened(block):
    inner = partner(block, LON, 0)
    inner, block = lax.optimization_barrier((inner, block))
    outer = partner(block, LON, 1)
    return jnp.stack([outer, block, inner])


def all_bands(wide):
    count = extent(LAT)
    below = lax.ppermute(wide, LAT, [(i, i + 1) for i in range(count - 1)])
    above = lax.ppermute(wide, LAT, [(i + 1, i) for i in range(count - 1)])
    return below, above


def all_bands_paired(wide):
    count = extent(LAT)
    swap = lax.ppermute(wide, LAT, [p for a, b in pairs(count, 0) for p in ((a, b), (b, a))])
    return swap, lax.all_gather(wide, LAT, axis_index_groups=pairs(count, 1))


def rounded(value):
    return value.astype(jnp.bfloat16).astype(jnp.float32)


def pieces(value):
    high = rounded(value)
    mid = rounded(value - high)
    return high, mid, rounded(value - high - mid)


def own_side(place, level, kinds, offset):
    one = jnp.ones_like(level)

    def looked_up(column):
        logs = [math.log2(row[column]) for row in COUPLING]
        return logs[0] + kinds[0] * (logs[1] - logs[0]) + kinds[1] * (logs[2] - logs[0])

    at_height = looked_up(0)
    rows = [HORIZ * axis for axis in place for _ in range(3)]
    rows += [2.0 * VERT * level, looked_up(1) - at_height, looked_up(2) - at_height]
    return rows + [one, one, offset + at_height - HORIZ, jnp.zeros_like(level)]


def far_side(place, level, kinds, offset, error):
    rows = [piece for axis in place for piece in pieces(axis)]
    return rows + [level, *kinds, *pieces(offset)[:2], jnp.ones_like(level), error]


def write_own(own_ref, rows_ref, rows):
    for row in range(16):
        rows_ref[row : row + 1, :] = rows[row]
    for step in range(3):
        if step:
            rows_ref[14:15, :] = rows[14] + step * math.log2(TAPER_STEP)
        left = rows_ref[...]
        for piece in range(3):
            part = left.astype(jnp.bfloat16)
            own_ref[step, 16 * piece : 16 * piece + 16, :] = part
            left = left - part.astype(jnp.float32)


def describe_kernel(
    start_ref, error_ref, frac_ref, spread_ref, type_ref,
    message_ref, error_out_ref, added_ref, kept_ref, rows_ref,
):
    frac = frac_ref[...].astype(jnp.float32)
    latitude = (lax.axis_index(LAT).astype(jnp.float32) + frac[0:1]) * (2.0 * LAT_LIMIT / BANDS) - LAT_LIMIT
    longitude = (lax.axis_index(LON).astype(jnp.float32) + frac[1:2]) * (2.0 * math.pi / SECTORS)
    angles = jnp.concatenate([latitude, longitude], axis=0)
    cosines, sines = jnp.cos(angles), jnp.sin(angles)
    place = (cosines[0:1] * cosines[1:2], cosines[0:1] * sines[1:2], sines[0:1])
    level = frac[2:3]
    offset = jnp.log(spread_ref[...].astype(jnp.float32)) * LOG2E - VERT * level * level
    kinds = [jnp.where(type_ref[...] == kind, jnp.ones_like(level), 0.0) for kind in (1, 2)]
    far = far_side(place, level, kinds, offset, error_ref[...])
    for row in range(16):
        rows_ref[row : row + 1, :] = far[row]
    message_ref[0:16, :] = start_ref[...].astype(jnp.bfloat16)
    message_ref[16:32, :] = rows_ref[...].astype(jnp.bfloat16)
    error_out_ref[...] = error_ref[...]
    kept_ref[...] = start_ref[...]
    added_ref[...] = error_ref[...] * start_ref[...]


def whole(space=pltpu.VMEM):
    return pl.BlockSpec(memory_space=space)


def describe(start, error_var, where_frac, spread, obs_type):
    return pl.pallas_call(
        describe_kernel,
        out_shape=(
            pltpu.VMEM((32, OBS), jnp.bfloat16),
            pltpu.VMEM((1, OBS), jnp.float32),
            pltpu.VMEM((RHS, OBS), jnp.float32),
            pltpu.VMEM((RHS, OBS), jnp.float32),
        ),
        in_specs=[whole()] * 5,
        out_specs=[whole()] * 4,
        scratch_shapes=[pltpu.VMEM((16, OBS), jnp.float32)],
        name="describe",
    )(start, error_var, where_frac, spread, obs_type)


OWN = (1, 2, 3)
OUTER = (0, 1, 2)


def part_of(columns, steps, near_ref, own_ref, tile_ref):
    for slot, (column, step) in enumerate(zip(columns, steps)):
        far = near_ref[column, 16:32, :]
        far = jnp.concatenate([far, far, far], axis=0)
        power = lax.dot_general(far, own_ref[step], (((0,), (0,)), ((), ())), preferred_element_type=jnp.float32)
        tile_ref[slot] = jnp.exp2(power).astype(jnp.bfloat16)
    return products(lambda slot: near_ref[columns[slot], 0:16, :], tile_ref)


def build_same_kernel(
    near_ref, added_ref, tile_ref, sum_ref, own_ref, outer_own_ref, outer_sum_ref, rows_ref, scratch_ref
):
    for column, side_ref in ((2, own_ref), (1, outer_own_ref)):
        rows = near_ref[column, 16:32, :].astype(jnp.float32)
        row = [rows[at : at + 1] for at in range(16)]
        place = [row[3 * axis] + row[3 * axis + 1] + row[3 * axis + 2] for axis in range(3)]
        write_own(side_ref, rows_ref, own_side(place, row[9], row[10:12], row[12] + row[13]))
    sum_ref[...] = added_ref[...] + part_of(OWN, SAME_BAND, near_ref, own_ref, tile_ref)
    outer_added = row[15] * near_ref[1, 0:16, :].astype(jnp.float32)
    outer_sum_ref[...] = outer_added + part_of(OUTER, SAME_BAND, near_ref, outer_own_ref, scratch_ref)


def build_other_kernel(
    near_ref, own_ref, added_ref, outer_own_ref, outer_added_ref, tile_ref, sum_ref, *more
):
    *outer_refs, scratch_ref = more
    total = added_ref[...] + part_of(OWN, OTHER_BAND, near_ref, own_ref, tile_ref)
    outer = outer_added_ref[...] + part_of(OUTER, OTHER_BAND, near_ref, outer_own_ref, scratch_ref)
    sum_ref[...] = total
    if len(outer_refs) == 1:
        outer_refs[0][...] = outer
    else:
        for ref, value in zip(outer_refs, (total, outer)):
            send(ref, value)


def products(field_of, tile_ref):
    total = sum(jnp.dot(field_of(slot), tile_ref[slot], preferred_element_type=jnp.float32) for slot in range(3))
    return total if total.shape[0] == RHS else total[:RHS] + total[RHS:]


def send(ref, value):
    high = value.astype(jnp.bfloat16)
    ref[0:RHS, :] = high
    ref[RHS : 2 * RHS, :] = (value - high.astype(jnp.float32)).astype(jnp.bfloat16)


def apply_kernel(near_ref, tile_ref, added_ref, scale_ref, sum_ref):
    sum_ref[...] = added_ref[...] * scale_ref[...] + products(lambda slot: near_ref[slot], tile_ref)


SAME_BAND = (1, 0, 1)
OTHER_BAND = (2, 1, 2)


def cost(built):
    entries = 3 * OBS * OBS
    return pl.CostEstimate(
        flops=2 * entries * (RHS + 256 * built),
        bytes_accessed=2 * entries,
        transcendentals=entries * built,
    )


FIELD = pltpu.VMEM((RHS, OBS), jnp.float32)
SENT = pltpu.VMEM((2 * RHS, OBS), jnp.bfloat16)
TILES = pltpu.VMEM((3, OBS, OBS), jnp.bfloat16)
OWN_SIDE = pltpu.VMEM((3, 48, OBS), jnp.bfloat16)


def build(kernel, shapes, operands, scratch):
    return pl.pallas_call(
        kernel,
        out_shape=shapes,
        in_specs=[whole()] * len(operands),
        out_specs=[whole()] * len(shapes),
        scratch_shapes=scratch,
        compiler_params=pltpu.CompilerParams(vmem_limit_bytes=16 << 20),
        cost_estimate=cost(2),
        name="build",
    )(*operands)


def coefficients(gram):
    def inner(left, right):
        total = 0.0
        for i in range(4):
            for j in range(4):
                if left[i] is not None and right[j] is not None:
                    total = total + left[i] * right[j] * gram[min(i, j), max(i, j)]
        return total

    def axpy(scale, added, start):
        out = []
        for a, s in zip(added, start):
            if a is None:
                out.append(s)
            else:
                out.append(scale * a if s is None else s + scale * a)
        return out

    one = jnp.ones_like(gram[0, 0])
    answer = [None] * 4
    residual = [one, None, None, None]
    direction = residual
    norm_now = gram[0, 0]
    for iteration in range(ITERS):
        image = [None] + direction[:3]
        step_len = norm_now / inner(direction, image)
        answer = axpy(step_len, direction, answer)
        residual = axpy(-step_len, image, residual)
        if iteration < ITERS - 1:
            norm_next = inner(residual, residual)
            direction = axpy(norm_next / norm_now, direction, residual)
            norm_now = norm_next
    return answer[:3], residual


def lane_sums(products):
    empty = jnp.zeros((128 - RHS * len(products), OBS), jnp.float32)
    stacked = jnp.concatenate([*products, empty], axis=0) if len(products) < 8 else jnp.concatenate(products, axis=0)
    ones = jnp.ones((8, OBS), jnp.bfloat16)
    total = 0.0
    for part in pieces(stacked):
        total = total + lax.dot_general(
            ones, part.astype(jnp.bfloat16), (((1,), (1,)), ((), ())), preferred_element_type=jnp.float32
        )
    return total[0:1]


MOMENTS = 6


def same_band_kernel(near_ref, tile_ref, second_ref, scale_ref, start_ref, first_ref, sum_ref, row_ref):
    start, first, second = start_ref[...], first_ref[...], second_ref[...]
    sum_ref[...] = second * scale_ref[...] + products(lambda slot: near_ref[slot], tile_ref)
    row_ref[...] = lane_sums(
        [start * start, start * first, first * first, start * second, first * second, second * second]
    )


def below_kernel(near_ref, tile_ref, part_ref, second_ref, row_ref, sum_ref, copies_ref):
    part = part_ref[...]
    total = part + products(lambda slot: near_ref[slot], tile_ref)
    sum_ref[...] = total
    product = second_ref[...] * (2.0 * total - part)
    before = [jnp.zeros_like(product)] * MOMENTS
    row = row_ref[...] + lane_sums([*before, product])
    copies_ref[...] = jnp.broadcast_to(row[None], copies_ref.shape)


def paired_kernel(swap_ref, both_ref, below_ref, above_ref, part_ref, sum_ref, sent_ref):
    band = lax.axis_index(LAT)
    inside = jnp.where((band == 0) | (band == BANDS - 1), 0.0, 1.0)

    def add(swap_tiles, both_tiles, position):
        total = part_ref[...] + products(lambda slot: swap_ref[slot], swap_tiles)
        total = total + inside * products(lambda slot: both_ref[position, slot], both_tiles)
        sum_ref[...] = total
        send(sent_ref, total)

    @pl.when(band % 2 == 1)
    def _():
        add(below_ref, above_ref, 1)

    @pl.when(band % 2 == 0)
    def _():
        add(above_ref, below_ref, 0)


def above_kernel(near_ref, total_ref, tile_ref, lower_ref, third_ref, copies_ref):
    third_ref[...] = lower_ref[...] + products(lambda slot: near_ref[slot], tile_ref)
    copies_ref[...] = jnp.broadcast_to(jnp.sum(total_ref[...], axis=0)[None], copies_ref.shape)


def finish_kernel(total_ref, start_ref, first_ref, second_ref, third_ref, answer_ref, residual_ref):
    totals = jnp.broadcast_to(jnp.sum(total_ref[...], axis=0), (RHS, 128))
    lane = lax.broadcasted_iota(jnp.int32, (RHS, 128), 1)
    row = lax.broadcasted_iota(jnp.int32, (RHS, 128), 0)
    moments = [
        jnp.sum(jnp.where(lane == row + RHS * at, totals, 0.0), axis=1, keepdims=True) for at in range(MOMENTS + 1)
    ]
    names = {(0, 0): 0, (0, 1): 1, (1, 1): 2, (0, 2): 3, (1, 2): 4, (2, 2): 5, (2, 3): 6, (0, 3): 4, (1, 3): 5}
    answer, residual = coefficients({pair: moments[at] for pair, at in names.items()})
    basis = (start_ref[...], first_ref[...], second_ref[...], third_ref[...])
    answer_ref[0, 0] = sum(c * v for c, v in zip(answer, basis))
    residual_ref[0, 0] = sum(c * v for c, v in zip(residual, basis))


def call(kernel, shapes, operands, name):
    return pl.pallas_call(
        kernel,
        out_shape=shapes,
        in_specs=[whole()] * len(operands),
        out_specs=[whole()] * len(shapes),
        compiler_params=pltpu.CompilerParams(vmem_limit_bytes=16 << 20),
        cost_estimate=cost(0),
        name=name,
    )(*operands)


def local(innovations, obs_error, where_frac, spread, obs_type):
    message, error_var, added, start = describe(
        innovations[0, 0], obs_error[0], where_frac[0, 0], spread[0], obs_type[0]
    )
    inner = partner(message, LON, 0)
    outer = partner(jnp.stack([message, inner]), LON, 1)
    wide = jnp.stack([outer[1], outer[0], message, inner])
    below, above = all_bands(wide)
    tiles, part, own, outer_own, outer = build(
        build_same_kernel,
        [TILES, FIELD, OWN_SIDE, OWN_SIDE, FIELD],
        [wide, added],
        [pltpu.VMEM((16, OBS), jnp.float32), TILES],
    )
    tiles_below, part, outer = build(
        build_other_kernel, [TILES, FIELD, FIELD], [below, own, part, outer_own, outer], [TILES]
    )
    tiles_above, first, sent, outer_sent = build(
        build_other_kernel, [TILES, FIELD, SENT, SENT], [above, own, part, outer_own, outer], [TILES]
    )
    wide = jnp.stack([outer_sent, sent, partner(sent, LON, 0)])
    swap, both = all_bands_paired(wide[:, :RHS])
    part, = call(apply_kernel, [FIELD], [wide, tiles, first, error_var], "apply")
    field = FIELD
    second, sent = call(
        paired_kernel,
        [field, SENT],
        [swap, both, tiles_below, tiles_above, part],
        "paired",
    )
    wide = widened(sent)
    below, above = all_bands(wide[:, :RHS])
    part, row = call(
        same_band_kernel,
        [field, pltpu.VMEM((1, 128), jnp.float32)],
        [wide, tiles, second, error_var, start, first],
        "same_band",
    )
    copies = [pltpu.VMEM((extent(axes), 1, 128), jnp.float32) for axes in GROUPS]
    lower, partial = call(below_kernel, [field, copies[0]], [below, tiles_below, part, second, row], "below")
    partial = lax.all_to_all(partial, GROUPS[0], 0, 0)
    third, partial = call(above_kernel, [field, copies[1]], [above, partial, tiles_above, lower], "above")
    totals = lax.all_to_all(partial, GROUPS[1], 0, 0)
    whole_field = jax.ShapeDtypeStruct((1, 1, RHS, OBS), jnp.float32)
    return call(finish_kernel, [whole_field] * 2, [totals, start, first, second, third], "finish")


def solution(mesh):
    fine = Mesh(mesh.devices.reshape(2, 4, 4, 8, 2), LAT + LON)
    in_specs = (
        P(LAT, LON, None, None),
        P(LAT, LON, None),
        P(LAT, LON, None, None),
        P(LAT, LON, None),
        P(LAT, LON, None),
    )
    out_specs = (P(LAT, LON, None, None), P(LAT, LON, None, None))
    return jax.shard_map(local, mesh=fine, in_specs=in_specs, out_specs=out_specs, check_vma=False)
```
